32 devices in a mesh: tm: 8 (over z, y), head: 4 (over x, core).
Axes of the slice: x: 2, y: 2, z: 4, core: 2. Of those that a mesh axis runs over, the one named last changes fastest.
Arguments:
- tokens: bfloat16 [2048, 1024], P('tm'), may hold values from -24 to 24
- q_weight: bfloat16 [1024, 1024], P(None, 'head'), may hold values from -2 to 2
- k_weight: bfloat16 [1024, 1024], P(None, 'head'), may hold values from -2 to 2
- v_weight: bfloat16 [1024, 1024], P(None, 'head'), may hold values from -0.1875 to 0.1875
- o_weight: bfloat16 [1024, 1024], P('head'), may hold values from -0.1875 to 0.1875
- rand_blocks: int32 [16, 3], P('tm'), may hold values from 0 to 15, as said below
- global_pos: int32 [256], replicated, may hold values from 0 to 2047, as said below
Outputs:
- mixed_out: bfloat16 [2048, 1024], P(('tm', 'head'))
The draws below stay inside these ranges and needn't reach their ends.
Inputs may be any that keep to these rules, and one draw needn't show every extreme that they name: rand_blocks[b, r] names a block whose shard index (block // 2) differs from that of b by at most 2; in every draw some entry differs by exactly 2. `global_pos`: 256 distinct positions in ascending order.
All inputs are finite; a program needn't handle non-finite values.
Results may differ from the reference program's by a relative error of at most 0.011.
Values may be sent and summed in bfloat16 or wider, within the bound.
No kernel may reach another device: no remote copies, remote signals or barrier semaphores. Data moves between devices by JAX's collectives and lax.ppermute only.
A program may use at most 64 MiB of HBM per device.

```python
import math
import jax
import jax.numpy as jnp
from jax import lax

D = 1024
HEADS = 16
HEAD_DIM = 64
BLOCK = 128
GLOBALS = 256
RAND = 3
SPREAD = 2
TOK_DEV = 256
TOKENS = 2048
BLOCKS = 16


def weight_matrix(key):
    return jnp.clip(jax.random.normal(key, (D, D), jnp.float32), -6.0, 6.0) * math.sqrt(3.0 / D)


def draw_q_weight(key, part):
    return weight_matrix(jax.random.fold_in(key, 11)).astype(jnp.bfloat16)


def draw_k_weight(key, part):
    own_matrix = weight_matrix(jax.random.fold_in(key, 12))
    return own_matrix.astype(jnp.bfloat16)


def draw_tokens(key, part):
    drawn_rows = jnp.clip(jax.random.normal(key, (TOKENS, D), jnp.float32), -6.0, 6.0)
    return drawn_rows.astype(jnp.bfloat16)


def draw_rand_blocks(key, part):
    per_shard = TOK_DEV // BLOCK
    shard_total = BLOCKS // per_shard
    home_shard = jnp.arange(BLOCKS, dtype=jnp.int32)[:, None] // per_shard
    lowest = jnp.maximum(home_shard - SPREAD, 0)
    highest = jnp.minimum(home_shard + SPREAD, shard_total - 1)
    first_key, second_key = jax.random.split(key)
    picked_shard = lowest + jax.random.randint(first_key, (BLOCKS, RAND), 0, highest - lowest + 1)
    picked_shard = picked_shard.at[0, 0].set(SPREAD)
    inner_block = jax.random.randint(second_key, (BLOCKS, RAND), 0, per_shard)
    return (picked_shard * per_shard + inner_block).astype(jnp.int32)


def draw_global_pos(key, part):
    shuffled = jax.random.permutation(key, jnp.arange(TOKENS, dtype=jnp.int32))
    return jnp.sort(shuffled[:GLOBALS]).astype(jnp.int32)


def steps_of(stream_key, dims, pieces, least, high):
    factor_of = 1.0
    for axis_at, shards_of in pieces:
        steps = jax.random.uniform(jax.random.fold_in(jax.random.fold_in(stream_key, 6), axis_at), (shards_of,), jnp.float32, least / len(pieces), high / len(pieces))
        factor_of = factor_of * jnp.repeat(jnp.exp(steps), dims[axis_at] // shards_of).reshape((-1,) + (1,) * (len(dims) - 1 - axis_at))
    return factor_of


def centred(own_key, extent, scale, most, pieces=(), held_as=jnp.bfloat16):
    values = scale * jax.random.normal(own_key, extent, jnp.float32)
    if pieces:
        values = values * steps_of(own_key, extent, pieces, -0.22, 0.18)
    return jnp.clip(values, -most, most).astype(held_as)


def setup_inputs(seed: int = 0) -> dict:
    key_of = jax.random.split(jax.random.key(seed), 8)
    tokens = draw_tokens(jax.random.fold_in(key_of[7], 71), 0)
    q_weight = draw_q_weight(jax.random.fold_in(key_of[7], 71), 0)
    k_weight = draw_k_weight(jax.random.fold_in(key_of[7], 71), 0)
    v_weight = centred(key_of[3], (D, D), D ** -0.5, 0.1875, ((1, 4),))
    o_weight = centred(key_of[4], (D, D), D ** -0.5, 0.1875, ((0, 4),))
    rand_blocks = draw_rand_blocks(jax.random.fold_in(key_of[7], 71), 0)
    global_pos = draw_global_pos(jax.random.fold_in(key_of[7], 71), 0)
    return dict(tokens=tokens, q_weight=q_weight, k_weight=k_weight, v_weight=v_weight, o_weight=o_weight, rand_blocks=rand_blocks, global_pos=global_pos)


def reference(tokens, q_weight, k_weight, v_weight, o_weight, rand_blocks, global_pos):
    score_scale = HEAD_DIM ** -0.5
    queries = jnp.dot(tokens, q_weight, preferred_element_type=jnp.float32).astype(jnp.bfloat16).reshape(TOKENS, HEADS, HEAD_DIM)
    keys_all = jnp.dot(tokens, k_weight, preferred_element_type=jnp.float32).astype(jnp.bfloat16).reshape(TOKENS, HEADS, HEAD_DIM)
    values_all = jnp.dot(tokens, v_weight, preferred_element_type=jnp.float32).astype(jnp.bfloat16).reshape(TOKENS, HEADS, HEAD_DIM)
    glob_q = queries[global_pos]
    glob_k = keys_all[global_pos]
    glob_v = values_all[global_pos]

    def global_head(operands):
        query_head, key_head, value_head = operands
        scores = jnp.dot(query_head, key_head.T, preferred_element_type=jnp.float32) * score_scale
        weights = jnp.exp(scores - jnp.max(scores, axis=1, keepdims=True))
        summed = jnp.dot(weights, value_head.astype(jnp.float32), precision=lax.Precision.HIGHEST)
        return (summed / jnp.sum(weights, axis=1, keepdims=True)).astype(jnp.bfloat16)

    global_out = lax.map(global_head, (jnp.transpose(glob_q, (1, 0, 2)), jnp.transpose(keys_all, (1, 0, 2)), jnp.transpose(values_all, (1, 0, 2))))
    key_blocks = keys_all.reshape(BLOCKS, BLOCK, HEADS, HEAD_DIM)
    value_blocks = values_all.reshape(BLOCKS, BLOCK, HEADS, HEAD_DIM)
    padded_k = jnp.pad(keys_all, ((2 * BLOCK, BLOCK), (0, 0), (0, 0)))
    padded_v = jnp.pad(values_all, ((2 * BLOCK, BLOCK), (0, 0), (0, 0)))

    def one_block(block_id):
        first_row = (block_id * BLOCK).astype(jnp.int32)
        query_block = lax.dynamic_slice_in_dim(queries, first_row, BLOCK, 0)
        window_k = lax.dynamic_slice_in_dim(padded_k, first_row, 4 * BLOCK, 0)
        window_v = lax.dynamic_slice_in_dim(padded_v, first_row, 4 * BLOCK, 0)
        random_k = key_blocks[rand_blocks[block_id]].reshape(RAND * BLOCK, HEADS, HEAD_DIM)
        random_v = value_blocks[rand_blocks[block_id]].reshape(RAND * BLOCK, HEADS, HEAD_DIM)
        keys_block = jnp.concatenate([window_k, random_k, glob_k], axis=0)
        values_block = jnp.concatenate([window_v, random_v, glob_v], axis=0)
        spots = first_row - 2 * BLOCK + jnp.arange(4 * BLOCK, dtype=jnp.int32)
        valid = jnp.concatenate([(spots >= 0) & (spots < TOKENS), jnp.ones((RAND * BLOCK + GLOBALS,), dtype=bool)])
        scores = jnp.einsum("qhd,khd->hqk", query_block.astype(jnp.float32), keys_block.astype(jnp.float32)) * score_scale
        scores = jnp.where(valid[None, None, :], scores, -jnp.inf)
        peak = jnp.max(scores, axis=2, keepdims=True)
        expo = jnp.exp(scores - peak)
        denominator = jnp.sum(expo, axis=2)
        rounded = lax.optimization_barrier(expo.astype(jnp.bfloat16)).astype(jnp.float32)
        numerator = jnp.einsum("hqk,khd->qhd", rounded, values_block.astype(jnp.float32))
        return (numerator / jnp.transpose(denominator)[:, :, None]).astype(jnp.bfloat16)

    blocks_out = lax.map(one_block, jnp.arange(BLOCKS, dtype=jnp.int32))
    attended = blocks_out.reshape(TOKENS, D)
    attended = attended.at[global_pos].set(jnp.transpose(global_out, (1, 0, 2)).reshape(GLOBALS, D))
    return jnp.dot(attended, o_weight, preferred_element_type=jnp.float32).astype(jnp.bfloat16)
```

```python
import functools
import math

import jax
import jax.numpy as jnp
from jax import lax
from jax.experimental import pallas as pl
from jax.experimental.pallas import tpu as pltpu
from jax.sharding import PartitionSpec as P

HEAD_DIM = 64
BLOCK = 128
LANES = 128
NEVER = -1e30
RING_MOST = 16
VMEM_BYTES = 40 * 1024 * 1024


def project_kernel(t_ref, k_ref, v_ref, kv_ref, acc_ref):
    step = pl.program_id(0)
    feats = k_ref.shape[1]

    @pl.when(step == 0)
    def _():
        acc_ref[...] = jnp.zeros_like(acc_ref)

    rows = t_ref[...]
    acc_ref[:, :feats] += jnp.dot(rows, k_ref[...], preferred_element_type=jnp.float32)
    acc_ref[:, feats:] += jnp.dot(rows, v_ref[...], preferred_element_type=jnp.float32)

    @pl.when(step == pl.num_programs(0) - 1)
    def _():
        kv_ref[...] = acc_ref[...].astype(kv_ref.dtype)


def project(tokens, k_weight, v_weight):
    rows, depth = tokens.shape
    feats = k_weight.shape[1]
    part = depth // 4
    return pl.pallas_call(
        project_kernel,
        grid=(4,),
        out_shape=jax.ShapeDtypeStruct((rows, 2 * feats), jnp.bfloat16),
        in_specs=[
            pl.BlockSpec((rows, part), lambda i: (0, i)),
            pl.BlockSpec((part, feats), lambda i: (i, 0)),
            pl.BlockSpec((part, feats), lambda i: (i, 0)),
        ],
        out_specs=pl.BlockSpec((rows, 2 * feats), lambda i: (0, 0)),
        scratch_shapes=[pltpu.VMEM((rows, 2 * feats), jnp.float32)],
        compiler_params=pltpu.CompilerParams(vmem_limit_bytes=VMEM_BYTES),
    )(tokens, k_weight, v_weight)


def attend_kernel(slots, parts, here_ref, q_ref, bias_ref, glob_ref, *refs):
    kv_refs = refs[:slots]
    out_refs = refs[slots : slots + parts]
    table, peaks, sums, mixed = refs[slots + parts :]
    step = pl.program_id(0)
    rows, feats = q_ref.shape
    span = kv_refs[0].shape[0]
    per_shard = rows // BLOCK
    pairs = feats // LANES
    scale = HEAD_DIM ** (-0.5) * math.log2(math.e)

    @pl.when(step == 0)
    def _():
        peaks[...] = jnp.full_like(peaks, NEVER)
        sums[...] = jnp.zeros_like(sums)

    for j in range(per_shard):
        at = slice(j * BLOCK, (j + 1) * BLOCK)
        table[at, :] = jnp.where(glob_ref[at, :] > 0, 0.0, bias_ref[j : j + 1, :])

    lane = lax.broadcasted_iota(jnp.int32, (1, LANES), 1)

    def one_pair(pair, carry):
        lanes = pl.ds(pl.multiple_of(pair * LANES, LANES), LANES)
        v_lanes = pl.ds(pl.multiple_of(feats + pair * LANES, LANES), LANES)
        for odd in range(LANES // HEAD_DIM):
            head = pair * (LANES // HEAD_DIM) + odd
            mine = (lane // HEAD_DIM) == odd
            q = jnp.where(mine, q_ref[:, lanes], jnp.zeros((), q_ref.dtype))
            scores = []
            peak = peaks[head]
            for i in range(slots):
                s = lax.dot_general(
                    q,
                    kv_refs[i][:, lanes],
                    (((1,), (1,)), ((), ())),
                    preferred_element_type=jnp.float32,
                )
                s = s * scale + table[:, i * span : (i + 1) * span]
                scores.append(s)
            best = functools.reduce(jnp.maximum, [jnp.max(s, axis=1, keepdims=True) for s in scores])
            new = jnp.maximum(peak, best)
            total = sums[head] * jnp.exp2(peak - new)
            for i in range(slots):
                e = jnp.exp2(scores[i] - new[:, :1]).astype(jnp.bfloat16)
                v = jnp.where(mine, kv_refs[i][:, v_lanes], jnp.ones((), jnp.bfloat16))
                total = total + jnp.dot(e, v, preferred_element_type=jnp.float32)
            peaks[head] = new
            sums[head] = total
        return carry

    lax.fori_loop(0, pairs, one_pair, 0)

    @pl.when(step == pl.num_programs(0) - 1)
    def _():
        for pair in range(pairs):
            done = []
            for odd in range(LANES // HEAD_DIM):
                total = sums[pair * (LANES // HEAD_DIM) + odd]
                done.append(total / pltpu.roll(total, HEAD_DIM, 1))
            mixed[:, pair * LANES : (pair + 1) * LANES] = jnp.where(lane < HEAD_DIM, done[0], done[1])
        piece = rows // parts
        for d in range(parts):
            first = pl.multiple_of((here_ref[0] ^ d) * piece, piece)
            out_refs[d][...] = mixed[pl.ds(first, piece), :].astype(out_refs[d].dtype)


def attend(queries, bias, is_global, here, kvs, parts):
    rows, feats = queries.shape
    span = rows
    if isinstance(kvs, list):
        slots, steps = len(kvs), 1
        operands = kvs
    else:
        slots = 4
        steps = kvs.shape[0] // (slots * span)
        operands = [kvs] * slots

    def spot(i):
        return pl.BlockSpec((span, 2 * feats), lambda s: (s * slots + i if steps > 1 else 0, 0))

    heads = feats // HEAD_DIM
    return pl.pallas_call(
        functools.partial(attend_kernel, slots, parts),
        grid=(steps,),
        out_shape=[jax.ShapeDtypeStruct((rows // parts, feats), jnp.bfloat16)] * parts,
        in_specs=[
            pl.BlockSpec(memory_space=pltpu.SMEM),
            pl.BlockSpec((rows, feats), lambda s: (0, 0)),
            pl.BlockSpec((bias.shape[0], slots * span), lambda s: (0, s)),
            pl.BlockSpec((rows, 1), lambda s: (0, 0)),
        ]
        + [spot(i) for i in range(slots)],
        out_specs=[pl.BlockSpec((rows // parts, feats), lambda s: (0, 0))] * parts,
        scratch_shapes=[
            pltpu.VMEM((rows, slots * span), jnp.float32),
            pltpu.VMEM((heads, rows, LANES), jnp.float32),
            pltpu.VMEM((heads, rows, LANES), jnp.float32),
            pltpu.VMEM((rows, feats), jnp.float32),
        ],
        compiler_params=pltpu.CompilerParams(vmem_limit_bytes=VMEM_BYTES),
    )(here, queries, bias, is_global, *operands)


def mix_kernel(parts, *refs):
    total = None
    for i in range(parts):
        term = jnp.dot(refs[i][...], refs[parts + i][...], preferred_element_type=jnp.float32)
        total = term if total is None else total + term
    refs[2 * parts][...] = total.astype(refs[2 * parts].dtype)


def mix(pieces, o_blocks):
    parts = len(pieces)
    rows, columns = pieces[0].shape[0], o_blocks[0].shape[1]
    return pl.pallas_call(
        functools.partial(mix_kernel, parts),
        out_shape=jax.ShapeDtypeStruct((rows, columns), jnp.bfloat16),
        in_specs=[pl.BlockSpec(memory_space=pltpu.VMEM)] * (2 * parts),
        out_specs=pl.BlockSpec(memory_space=pltpu.VMEM),
        compiler_params=pltpu.CompilerParams(vmem_limit_bytes=VMEM_BYTES),
    )(*pieces, *o_blocks)


def swapped(block, axis, distance):
    return lax.ppermute(block, axis, [(i, i ^ distance) for i in range(lax.axis_size(axis))])


def turned(block, axis, distance):
    n = lax.axis_size(axis)
    return lax.ppermute(block, axis, [(i, (i + distance) % n) for i in range(n)])


def shards(tokens, q_weight, k_weight, v_weight, o_weight, rand_blocks, global_pos):
    tok_rows = tokens.shape[0]
    per_shard = tok_rows // BLOCK
    n = lax.axis_size("tm")
    me = lax.axis_index("tm")
    parts = lax.axis_size("head")
    here = lax.axis_index("head")

    kv = project(tokens, k_weight, v_weight)
    if n <= RING_MOST:
        column = [kv] + [turned(kv, "tm", 2 * k) for k in range(1, n // 2)]
        other = [swapped(block, "tm", 1) for block in column]
        kvs = column + other
        far = [(me - 2 * k) % n for k in range(n // 2)]
        held = jnp.stack(far + [shard ^ 1 for shard in far])
    else:
        kvs = lax.all_gather(kv, "tm", tiled=True)
        held = jnp.arange(n, dtype=jnp.int32)
    o_blocks = [o_weight] + [swapped(o_weight, "head", d) for d in range(1, parts)]

    queries = jnp.dot(tokens, q_weight, preferred_element_type=jnp.float32).astype(jnp.bfloat16)
    own = me * tok_rows + jnp.arange(tok_rows, dtype=jnp.int32)
    is_global = jnp.any(own[:, None] == global_pos[None, :], axis=1, keepdims=True)
    spots = (held[:, None] * tok_rows + jnp.arange(tok_rows, dtype=jnp.int32)[None, :]).reshape(-1)
    listed = jnp.any(spots[None, :] == global_pos[:, None], axis=0)
    key_block = spots // BLOCK
    block_ids = me * per_shard + jnp.arange(per_shard, dtype=jnp.int32)
    away = key_block[None, :] - block_ids[:, None]
    times = ((away >= -2) & (away <= 1)).astype(jnp.int32) + listed[None, :].astype(jnp.int32)
    for r in range(rand_blocks.shape[1]):
        times = times + (rand_blocks[:, r : r + 1] == key_block[None, :]).astype(jnp.int32)
    bias = jnp.where(times > 0, jnp.log2(jnp.maximum(times, 1).astype(jnp.float32)), NEVER)

    pieces = attend(
        queries, bias, is_global.astype(jnp.float32), here.reshape(1).astype(jnp.int32), kvs, parts
    )
    pieces = [pieces[0]] + [swapped(pieces[d], "head", d) for d in range(1, parts)]
    return mix(pieces, o_blocks)


def solution(mesh):
    placed = (
        P("tm", None),
        P(None, "head"),
        P(None, "head"),
        P(None, "head"),
        P("head", None),
        P("tm", None),
        P(),
    )
    return jax.shard_map(
        shards, mesh=mesh, in_specs=placed, out_specs=P(("tm", "head"), None), check_vma=False
    )
```

```python
import functools
import math

import jax
import jax.numpy as jnp
from jax import lax
from jax.experimental import pallas as pl
from jax.experimental.pallas import tpu as pltpu
from jax.sharding import Mesh
from jax.sharding import PartitionSpec as P

HEAD_DIM = 64
BLOCK = 128
LANES = 128
NEVER = -1e30
NEAR = 2
RING_MOST = 8
MIB = 1024 * 1024


def project_kernel(side_ref, t_ref, q_ref, k_ref, v_ref, q_out, kv_out, q_acc, kv_acc):
    step = pl.program_id(0)
    feats = k_ref.shape[1]
    rows = t_ref[...]
    q = jnp.dot(rows, q_ref[...], preferred_element_type=jnp.float32)
    k = jnp.dot(rows, k_ref[...], preferred_element_type=jnp.float32)
    v = jnp.dot(rows, v_ref[...], preferred_element_type=jnp.float32)

    @pl.when(step == 0)
    def _():
        q_acc[...] = q
        kv_acc[:, :feats] = k
        kv_acc[:, feats:] = v

    @pl.when(step > 0)
    def _():
        q_acc[...] += q
        kv_acc[:, :feats] += k
        kv_acc[:, feats:] += v

    @pl.when(step == pl.num_programs(0) - 1)
    def _():
        q_out[...] = q_acc[...].astype(q_out.dtype)
        kv_out[...] = kv_acc[...].astype(kv_out.dtype)


def project(side, tokens, q_weight, k_weight, v_weight):
    rows, depth = tokens.shape
    feats = k_weight.shape[1] // NEAR
    steps = 4
    part = depth // steps
    weight = pl.BlockSpec((part, feats), lambda i, side_ref: (i, side_ref[0]))
    return pl.pallas_call(
        project_kernel,
        grid_spec=pltpu.PrefetchScalarGridSpec(
            num_scalar_prefetch=1,
            grid=(steps,),
            in_specs=[pl.BlockSpec((rows, part), lambda i, side_ref: (0, i)), weight, weight, weight],
            out_specs=[
                pl.BlockSpec((rows, feats), lambda i, side_ref: (0, 0)),
                pl.BlockSpec((rows, 2 * feats), lambda i, side_ref: (0, 0)),
            ],
            scratch_shapes=[
                pltpu.VMEM((rows, feats), jnp.float32),
                pltpu.VMEM((rows, 2 * feats), jnp.float32),
            ],
        ),
        out_shape=[
            jax.ShapeDtypeStruct((rows, feats), jnp.bfloat16),
            jax.ShapeDtypeStruct((rows, 2 * feats), jnp.bfloat16),
        ],
        compiler_params=pltpu.CompilerParams(vmem_limit_bytes=56 * MIB),
        cost_estimate=pl.CostEstimate(
            flops=6 * rows * depth * feats,
            bytes_accessed=2 * depth * (rows + 3 * feats) + 6 * rows * feats,
            transcendentals=0,
        ),
    )(side, tokens, q_weight, k_weight, v_weight)


def attend_kernel(slots, fresh, parts, side_ref, qa_ref, qb_ref, bias_ref, glob_ref, *refs):
    state = 0 if fresh else 2
    old, refs = refs[:state], refs[state:]
    kv_refs, refs = refs[:slots], refs[slots:]
    if parts:
        out_ref, table, mixed, peaks, sums = refs
    else:
        peaks, sums, table = refs
    step = pl.program_id(0)
    half, feats = qa_ref.shape
    span = kv_refs[0].shape[0]
    pairs = feats // LANES
    per_pair = LANES // HEAD_DIM
    scale = HEAD_DIM ** (-0.5) * math.log2(math.e)
    lane = lax.broadcasted_iota(jnp.int32, (1, LANES), 1)

    @pl.when(step == 0)
    def _():
        if fresh:
            peaks[...] = jnp.full_like(peaks, NEVER)
            sums[...] = jnp.zeros_like(sums)
        else:
            peaks[...] = old[0][...]
            sums[...] = old[1][...]

    for j in range(bias_ref.shape[0]):
        at = slice(j * BLOCK, (j + 1) * BLOCK)
        table[at, :] = jnp.where(glob_ref[at, :] > 0, 0.0, bias_ref[j : j + 1, :])

    for top, q_ref in enumerate((qa_ref, qb_ref)):
        at = slice(top * half, (top + 1) * half)
        for pair in range(pairs):
            lanes = slice(pair * LANES, (pair + 1) * LANES)
            v_lanes = slice(feats + pair * LANES, feats + (pair + 1) * LANES)
            for odd in range(per_pair):
                head = pair * per_pair + odd
                mine = (lane // HEAD_DIM) == odd
                q = jnp.where(mine, q_ref[:, lanes], jnp.zeros((), q_ref.dtype))
                scores = []
                for i in range(slots):
                    s = lax.dot_general(
                        q,
                        kv_refs[i][:, lanes],
                        (((1,), (1,)), ((), ())),
                        preferred_element_type=jnp.float32,
                    )
                    scores.append(s * scale + table[at, i * span : (i + 1) * span])
                top_score = functools.reduce(jnp.maximum, scores)
                peak = peaks[head, at, :]
                new = jnp.maximum(peak, jnp.max(top_score, axis=1, keepdims=True))
                total = sums[head, at, :] * jnp.exp2(peak - new)
                for i in range(slots):
                    e = jnp.exp2(scores[i] - new[:, :1]).astype(jnp.bfloat16)
                    v = jnp.where(mine, kv_refs[i][:, v_lanes], jnp.ones((), jnp.bfloat16))
                    total = total + jnp.dot(e, v, preferred_element_type=jnp.float32)
                peaks[head, at, :] = new
                sums[head, at, :] = total

    if parts:

        @pl.when(step == pl.num_programs(0) - 1)
        def _():
            for pair in range(pairs):
                done = []
                for odd in range(per_pair):
                    total = sums[pair * per_pair + odd]
                    done.append(total / pltpu.roll(total, HEAD_DIM, 1))
                mixed[:, pair * LANES : (pair + 1) * LANES] = jnp.where(
                    lane < HEAD_DIM, done[0], done[1]
                )
            piece = half // parts
            for near in range(NEAR):
                for part in range(parts):
                    first = pl.multiple_of((side_ref[0] ^ near) * half, half) + part * piece
                    out_ref[near * parts + part] = mixed[pl.ds(first, piece), :].astype(out_ref.dtype)


def attend(side, q_a, q_b, bias, is_global, old, kvs, parts):
    half, feats = q_a.shape
    rows = NEAR * half
    span = half
    heads = feats // HEAD_DIM
    steps = 1
    slots = len(kvs)
    operands = kvs
    if slots == 1:
        slots = 4
        steps = kvs[0].shape[0] // (slots * span)
        operands = kvs * slots

    def spot(i):
        return pl.BlockSpec((span, 2 * feats), lambda s: (s * slots + i if steps > 1 else 0, 0))

    state = [jax.ShapeDtypeStruct((heads, rows, LANES), jnp.float32)] * 2
    state_spec = [pl.BlockSpec((heads, rows, LANES), lambda s: (0, 0, 0))] * 2
    table = pltpu.VMEM((rows, slots * span), jnp.float32)
    if parts:
        out_shape = jax.ShapeDtypeStruct((NEAR * parts, half // parts, feats), jnp.bfloat16)
        out_specs = pl.BlockSpec(out_shape.shape, lambda s: (0, 0, 0))
        scratch = [table, pltpu.VMEM((rows, feats), jnp.float32)]
        scratch += [pltpu.VMEM(each.shape, each.dtype) for each in state]
    else:
        out_shape, out_specs, scratch = state, state_spec, [table]
    area = rows * slots * span * steps
    return pl.pallas_call(
        functools.partial(attend_kernel, slots, not old, parts),
        grid=(steps,),
        out_shape=out_shape,
        in_specs=[
            pl.BlockSpec(memory_space=pltpu.SMEM),
            pl.BlockSpec((half, feats), lambda s: (0, 0)),
            pl.BlockSpec((half, feats), lambda s: (0, 0)),
            pl.BlockSpec((bias.shape[0], slots * span), lambda s: (0, s)),
            pl.BlockSpec((rows, 1), lambda s: (0, 0)),
        ]
        + (state_spec if old else [])
        + [spot(i) for i in range(slots)],
        out_specs=out_specs,
        scratch_shapes=scratch,
        compiler_params=pltpu.CompilerParams(vmem_limit_bytes=40 * MIB),
        cost_estimate=pl.CostEstimate(
            flops=8 * area * LANES, bytes_accessed=8 * area // rows * feats, transcendentals=heads * area
        ),
    )(side, q_a, q_b, bias, is_global, *old, *operands)


def mix_kernel(parts, here_ref, got_ref, *refs):
    total = None
    for d in range(parts):
        source = here_ref[0] ^ d
        rows = jnp.concatenate([got_ref[near * parts + source] for near in range(NEAR)], axis=1)
        term = jnp.dot(rows, refs[d][...], preferred_element_type=jnp.float32)
        total = term if total is None else total + term
    refs[parts][...] = total.astype(refs[parts].dtype)


def mix(here, got, o_blocks):
    parts = len(o_blocks)
    rows, columns = got.shape[1], o_blocks[0].shape[1]
    vmem = pl.BlockSpec(memory_space=pltpu.VMEM)
    return pl.pallas_call(
        functools.partial(mix_kernel, parts),
        out_shape=jax.ShapeDtypeStruct((rows, columns), jnp.bfloat16),
        in_specs=[pl.BlockSpec(memory_space=pltpu.SMEM)] + [vmem] * (1 + parts),
        out_specs=vmem,
        compiler_params=pltpu.CompilerParams(vmem_limit_bytes=40 * MIB),
    )(here, got, *o_blocks)


def swapped(block, axis, distance):
    return lax.ppermute(block, axis, [(i, i ^ distance) for i in range(lax.axis_size(axis))])


def turned(block, axis, distance):
    n = lax.axis_size(axis)
    return lax.ppermute(block, axis, [(i, (i + distance) % n) for i in range(n)])


def shards(tokens, q_weight, k_weight, v_weight, o_weight, rand_blocks, global_pos):
    tok_rows = tokens.shape[0]
    per_shard = tok_rows // BLOCK
    far_count = lax.axis_size("far")
    far = lax.axis_index("far")
    near = lax.axis_index("near")
    parts = lax.axis_size("head")
    here = lax.axis_index("head").reshape(1).astype(jnp.int32)
    side = near.reshape(1).astype(jnp.int32)

    tokens_b = swapped(tokens, "near", 1)
    rand_b = swapped(rand_blocks, "near", 1)
    q_a, kv_a = project(side, tokens, q_weight, k_weight, v_weight)
    q_b, kv_b = project(side, tokens_b, q_weight, k_weight, v_weight)
    ring = far_count <= RING_MOST
    if ring:
        first = [kv_a] + [turned(kv_a, "far", k) for k in range(1, far_count)] + [kv_b]
        second = [turned(kv_b, "far", k) for k in range(1, far_count)]
        fars = [(far - k) % far_count for k in range(far_count)]
        held = jnp.stack([NEAR * f + near for f in fars] + [NEAR * f + 1 - near for f in fars])
    else:
        first = [lax.all_gather(kv_a, "far", tiled=True)]
        second = [lax.all_gather(kv_b, "far", tiled=True)]
        fars = NEAR * jnp.arange(far_count, dtype=jnp.int32)
        held = jnp.concatenate([fars + near, fars + 1 - near])
    o_blocks = [o_weight] + [swapped(o_weight, "head", d) for d in range(1, parts)]

    inner = jnp.arange(tok_rows, dtype=jnp.int32)
    own_shards = jnp.stack([NEAR * far + near, NEAR * far + 1 - near])
    own = (own_shards[:, None] * tok_rows + inner[None, :]).reshape(-1)
    is_global = jnp.any(own[:, None] == global_pos[None, :], axis=1, keepdims=True)
    spots = (held[:, None] * tok_rows + inner[None, :]).reshape(-1)
    listed = jnp.any(spots[None, :] == global_pos[:, None], axis=0)
    key_block = spots // BLOCK
    block_ids = (
        own_shards[:, None] * per_shard + jnp.arange(per_shard, dtype=jnp.int32)[None, :]
    ).reshape(-1)
    away = key_block[None, :] - block_ids[:, None]
    times = ((away >= -2) & (away <= 1)).astype(jnp.int32) + listed[None, :].astype(jnp.int32)
    rand = jnp.concatenate([rand_blocks, rand_b], axis=0)
    for r in range(rand.shape[1]):
        times = times + (rand[:, r : r + 1] == key_block[None, :]).astype(jnp.int32)
    bias = jnp.where(times > 0, jnp.log2(jnp.maximum(times, 1).astype(jnp.float32)), NEVER)
    is_global = is_global.astype(jnp.float32)

    cut = (len(first) if ring else far_count) * tok_rows
    old = attend(side, q_a, q_b, bias[:, :cut], is_global, [], first, 0)
    sent = attend(side, q_a, q_b, bias[:, cut:], is_global, old, second, parts)
    got = lax.all_to_all(sent, ("near", "head"), 0, 0, tiled=True)
    return mix(here, got, o_blocks)


def solution(mesh):
    count, parts = mesh.devices.shape
    split = Mesh(mesh.devices.reshape(count // NEAR, NEAR, parts), ("far", "near", "head"))
    tm = ("far", "near")
    placed = (
        P(tm, None),
        P(None, "head"),
        P(None, "head"),
        P(None, "head"),
        P("head", None),
        P(tm, None),
        P(),
    )
    return jax.shard_map(
        shards, mesh=split, in_specs=placed, out_specs=P((*tm, "head"), None), check_vma=False
    )
```

```python
import functools
import math

import jax
import jax.numpy as jnp
from jax import lax
from jax.experimental import pallas as pl
from jax.experimental.pallas import tpu as pltpu
from jax.sharding import Mesh
from jax.sharding import PartitionSpec as P

HEAD_DIM = 64
BLOCK = 128
LANES = 128
DIGIT = 128
TILE_ROWS = 16
NEVER = -1e30
MIB = 1024 * 1024
VMEM = pl.BlockSpec(memory_space=pltpu.VMEM)
SMEM = pl.BlockSpec(memory_space=pltpu.SMEM)
ANY = pl.BlockSpec(memory_space=pl.ANY)


def low_half():
    return lax.broadcasted_iota(jnp.int32, (1, LANES), 1) < HEAD_DIM


def half_turn(block):
    return pltpu.roll(block, HEAD_DIM, 1)


def project_kernel(chunks, place_ref, rand_ref, t_hbm, q_hbm, k_hbm, v_hbm, own_ref, *refs):
    sent_refs, (t_ref, w_ref, all_ref, sems) = refs[:-4], refs[-4:]
    rows, depth = t_ref.shape
    feats = w_ref.shape[2]
    heads = feats // HEAD_DIM
    part = depth // chunks
    copies = []
    for c in range(chunks):
        at = slice(c * part, (c + 1) * part)
        group = [pltpu.make_async_copy(t_hbm.at[:, at], t_ref.at[:, at], sems.at[c, 0])]
        for i, w_hbm in enumerate((q_hbm, k_hbm, v_hbm)):
            group.append(pltpu.make_async_copy(w_hbm.at[at, :], w_ref.at[i, at, :], sems.at[c, 1 + i]))
        for copy in group:
            copy.start()
        copies.append(group)
    totals = [None] * 3
    for c in range(chunks):
        at = slice(c * part, (c + 1) * part)
        for copy in copies[c]:
            copy.wait()
        for i in range(3):
            term = jnp.dot(t_ref[:, at], w_ref[i, at, :], preferred_element_type=jnp.float32)
            totals[i] = term if c == 0 else totals[i] + term
    q, k, v = totals
    low = low_half()
    for pair in range(heads // 2):
        at = slice(pair * LANES, (pair + 1) * LANES)
        q2, k2, v2 = q[:, at], k[:, at], v[:, at]
        top, bottom = q2[: rows // 2], q2[rows // 2 :]
        kv = (jnp.where(low, k2, half_turn(v2)), jnp.where(low, half_turn(k2), v2))
        qs = (jnp.where(low, top, half_turn(bottom)), jnp.where(low, half_turn(top), bottom))
        for odd in range(2):
            all_ref[2 * pair + odd, :rows, :] = kv[odd].astype(jnp.bfloat16)
            all_ref[2 * pair + odd, rows : rows + rows // 2, :] = qs[odd].astype(jnp.bfloat16)
    near = place_ref[0]
    digit_rows = sent_refs[0].shape[0] - rows - rows // 2
    row = lax.broadcasted_iota(jnp.int32, (digit_rows, LANES), 0)
    digits = jnp.zeros((digit_rows, LANES), jnp.float32)
    picks = rand_ref.shape[1]
    for j in range(rand_ref.shape[0]):
        for r in range(picks):
            at = 2 * (j * picks + r)
            value = rand_ref[j, r]
            digits = jnp.where(row == at, (value // DIGIT).astype(jnp.float32), digits)
            digits = jnp.where(row == at + 1, (value % DIGIT).astype(jnp.float32), digits)
    own_ref[...] = all_ref[near, :rows, :]
    for d in range(heads):
        sent_refs[d][: rows + rows // 2, :] = all_ref[near ^ d]
        sent_refs[d][rows + rows // 2 :, :] = digits.astype(jnp.bfloat16)


def project(place, rand_blocks, tokens, q_weight, k_weight, v_weight):
    rows, depth = tokens.shape
    feats = k_weight.shape[1]
    heads = feats // HEAD_DIM
    chunks = 4
    message = rows + rows // 2
    digit_rows = -(-2 * rand_blocks.size // TILE_ROWS) * TILE_ROWS
    return pl.pallas_call(
        functools.partial(project_kernel, chunks),
        in_specs=[SMEM, SMEM, ANY, ANY, ANY, ANY],
        out_specs=[VMEM] * (1 + heads),
        out_shape=[jax.ShapeDtypeStruct((rows, LANES), jnp.bfloat16)]
        + [jax.ShapeDtypeStruct((message + digit_rows, LANES), jnp.bfloat16)] * heads,
        scratch_shapes=[
            pltpu.VMEM((rows, depth), jnp.bfloat16),
            pltpu.VMEM((3, depth, feats), jnp.bfloat16),
            pltpu.VMEM((heads, message, LANES), jnp.bfloat16),
            pltpu.SemaphoreType.DMA((chunks, 4)),
        ],
        compiler_params=pltpu.CompilerParams(vmem_limit_bytes=56 * MIB),
        cost_estimate=pl.CostEstimate(
            flops=6 * rows * depth * feats, bytes_accessed=2 * depth * (rows + 3 * feats), transcendentals=0
        ),
    )(place, rand_blocks, tokens, q_weight, k_weight, v_weight)


def pack_kernel(*refs):
    out_ref = refs[-1]
    rows = out_ref.shape[0] // (len(refs) - 1)
    for i, ref in enumerate(refs[:-1]):
        out_ref[i * rows : (i + 1) * rows, :] = ref[:rows, :]


def pack(rows, messages):
    return pl.pallas_call(
        pack_kernel,
        in_specs=[VMEM] * len(messages),
        out_specs=VMEM,
        out_shape=jax.ShapeDtypeStruct((rows * len(messages), LANES), jnp.bfloat16),
        compiler_params=pltpu.CompilerParams(vmem_limit_bytes=32 * MIB),
    )(*messages)


def attend_kernel(heads, picks, plan, steps, fresh, parts, place_ref, listed_ref, glob_ref, *refs):
    messages, refs = refs[:heads], refs[heads:]
    old, refs = ([], refs) if fresh else (refs[:2], refs[2:])
    count = 1 + max(entry[0] for entry in plan)
    kv_refs, refs = refs[:count], refs[count:]
    if parts:
        out_ref, peaks, sums, q_ref, bias_ref = refs
    else:
        peaks, sums, q_ref, bias_ref = refs
    span = glob_ref.shape[0] // heads
    per_shard = span // BLOCK
    near, far = place_ref[0], place_ref[1]
    step = pl.program_id(0) if steps > 1 else 0
    scale = HEAD_DIM ** (-0.5) * math.log2(math.e)
    low = low_half()

    def once(when, body):
        if steps > 1:
            pl.when(step == when)(body)
        else:
            body()

    def begin():
        if fresh:
            peaks[...] = jnp.full_like(peaks, NEVER)
            sums[...] = jnp.zeros_like(sums)
        else:
            peaks[...] = old[0][...]
            sums[...] = old[1][...]
        for d in range(heads):
            packed = messages[d][span : span + span // 2, :].astype(jnp.float32)
            top = jnp.where(low, packed, 0.0)
            bottom = jnp.where(low, half_turn(packed), 0.0)
            q_ref[d * span : d * span + span // 2, :] = top.astype(q_ref.dtype)
            q_ref[d * span + span // 2 : (d + 1) * span, :] = bottom.astype(q_ref.dtype)

    once(0, begin)

    for d in range(heads):
        rand = messages[d][span + span // 2 :, :].astype(jnp.float32)
        for j in range(per_shard):
            block = (far * heads + (near ^ d)) * per_shard + j
            chosen = []
            for r in range(picks):
                at = 2 * (j * picks + r)
                chosen.append(rand[at : at + 1, :] * DIGIT + rand[at + 1 : at + 2, :])
            for i, (_, _, group, slot) in enumerate(plan):
                there = far if group == "own" else (far ^ 1 if group == "other" else step)
                for b in range(per_shard):
                    key_block = (there * heads + (near ^ slot)) * per_shard + b
                    away = key_block - block
                    window = jnp.where((away >= -2) & (away <= 1), 1.0, 0.0)
                    times = listed_ref[pl.ds(key_block, 1), :] + window
                    for pick in chosen:
                        times = times + jnp.where(pick == key_block.astype(jnp.float32), 1.0, 0.0)
                    value = jnp.where(times > 0, jnp.log2(jnp.maximum(times, 1.0)), NEVER)
                    at = d * per_shard + j
                    lanes = slice(i * span + b * BLOCK, i * span + (b + 1) * BLOCK)
                    bias_ref[at : at + 1, lanes] = value

    def one_tile(tile, carry):
        rows = pl.ds(pl.multiple_of(tile * span, span), span)
        q = q_ref[rows, :]
        glob = glob_ref[rows, :] > 0
        scores = []
        for i, (ref, first, _, _) in enumerate(plan):
            s = lax.dot_general(
                q,
                kv_refs[ref][first : first + span, :],
                (((1,), (1,)), ((), ())),
                preferred_element_type=jnp.float32,
            )
            halves = []
            for j in range(per_shard):
                at = slice(j * BLOCK, (j + 1) * BLOCK)
                bias = bias_ref[pl.ds(tile * per_shard + j, 1), i * span : (i + 1) * span]
                halves.append(s[at, :] * scale + jnp.where(glob[at, :], 0.0, bias))
            scores.append(jnp.concatenate(halves, axis=0))
        best = functools.reduce(jnp.maximum, scores)
        peak = peaks[rows, :]
        new = jnp.maximum(peak, jnp.max(best, axis=1, keepdims=True))
        total = sums[rows, :] * jnp.exp2(peak - new)
        for i, (ref, first, _, _) in enumerate(plan):
            e = jnp.exp2(scores[i] - new[:, :1]).astype(jnp.bfloat16)
            v = jnp.where(low, jnp.ones((), jnp.bfloat16), kv_refs[ref][first : first + span, :])
            total = total + jnp.dot(e, v, preferred_element_type=jnp.float32)
        peaks[rows, :] = new
        sums[rows, :] = total
        return carry

    lax.fori_loop(0, heads, one_tile, 0)

    def finish():
        total = sums[...]
        sums[...] = total / half_turn(total)
        piece = span // parts
        for other in range(heads):
            for part in range(parts):
                first = pl.multiple_of((near ^ other) * span, span) + part * piece
                top = sums[pl.ds(first, piece // 2), :]
                bottom = sums[pl.ds(first + piece // 2, piece // 2), :]
                packed = jnp.where(low, half_turn(top), bottom)
                out_ref[other * parts + part] = packed.astype(out_ref.dtype)

    if parts:
        once(steps - 1, finish)


def attend(place, picks, listed, is_global, messages, old, kvs, plan, steps, parts):
    heads = len(messages)
    rows = is_global.shape[0]
    span = rows // heads
    state = [jax.ShapeDtypeStruct((rows, LANES), jnp.float32)] * 2
    scratch = [
        pltpu.VMEM((rows, LANES), jnp.bfloat16),
        pltpu.VMEM((rows // BLOCK, len(plan) * span), jnp.float32),
    ]
    if parts:
        out_shape = jax.ShapeDtypeStruct((heads * parts, span // parts // 2, LANES), jnp.bfloat16)
        scratch = [pltpu.VMEM(each.shape, each.dtype) for each in state] + scratch
    else:
        out_shape = state
    if steps > 1:
        kv_specs = [pl.BlockSpec((rows, LANES), lambda s: (s, 0))]
        placing = dict(grid=(steps,))
    else:
        kv_specs = [VMEM] * len(kvs)
        placing = {}
    area = rows * len(plan) * span * steps
    return pl.pallas_call(
        functools.partial(attend_kernel, heads, picks, plan, steps, not old, parts),
        out_shape=out_shape,
        in_specs=[SMEM, VMEM, VMEM] + [VMEM] * (heads + len(old)) + kv_specs,
        out_specs=VMEM if parts else [VMEM] * 2,
        scratch_shapes=scratch,
        compiler_params=pltpu.CompilerParams(vmem_limit_bytes=32 * MIB),
        cost_estimate=pl.CostEstimate(
            flops=4 * area * LANES, bytes_accessed=8 * rows * LANES, transcendentals=area
        ),
        **placing,
    )(place, listed, is_global, *messages, *old, *kvs)


def mix_kernel(near_count, order, here_ref, got_ref, *refs):
    parts = len(order)
    half = got_ref.shape[1]
    low = low_half()
    total = None
    for i, d in enumerate(order):
        source = here_ref[0] ^ d
        columns = []
        for near in range(0, near_count, 2):
            even = got_ref[near * parts + source].astype(jnp.float32)
            odd = got_ref[(near + 1) * parts + source].astype(jnp.float32)
            top = jnp.where(low, even, half_turn(odd))
            bottom = jnp.where(low, half_turn(even), odd)
            columns.append(jnp.concatenate([top, bottom], axis=0).astype(jnp.bfloat16))
        rows = jnp.concatenate(columns, axis=1)
        term = jnp.dot(rows, refs[i][...], preferred_element_type=jnp.float32)
        total = term if total is None else total + term
    refs[parts][...] = total.astype(refs[parts].dtype)


def mix(here, got, o_blocks, order):
    parts = len(o_blocks)
    return pl.pallas_call(
        functools.partial(mix_kernel, got.shape[0] // parts, order),
        out_shape=jax.ShapeDtypeStruct((2 * got.shape[1], o_blocks[0].shape[1]), jnp.bfloat16),
        in_specs=[SMEM] + [VMEM] * (1 + parts),
        out_specs=VMEM,
        compiler_params=pltpu.CompilerParams(vmem_limit_bytes=32 * MIB),
    )(here, got, *o_blocks)


def swapped(block, axis, distance):
    return lax.ppermute(block, axis, [(i, i ^ distance) for i in range(lax.axis_size(axis))])


def shards(tokens, q_weight, k_weight, v_weight, o_weight, rand_blocks, global_pos):
    tok_rows = tokens.shape[0]
    per_shard = tok_rows // BLOCK
    far_count, heads, parts = (lax.axis_size(axis) for axis in ("far", "near", "head"))
    far, near, here = (lax.axis_index(axis).astype(jnp.int32) for axis in ("far", "near", "head"))
    place = jnp.stack([near, far])

    o_blocks, order = [o_weight], [0]
    distance = parts // 2
    while distance:
        o_blocks = o_blocks + [swapped(block, "head", distance) for block in o_blocks]
        order = order + [d ^ distance for d in order]
        distance //= 2

    own_kv, *sent = project(place, rand_blocks, tokens, q_weight, k_weight, v_weight)
    messages = [sent[0]] + [swapped(sent[d], "near", d) for d in range(1, heads)]

    inner = jnp.arange(tok_rows, dtype=jnp.int32)
    spots = jnp.arange(far_count * heads * tok_rows, dtype=jnp.int32)
    listed = jnp.any(spots[None, :] == global_pos[:, None], axis=0)
    listed = listed.astype(jnp.float32).reshape(-1, BLOCK)
    group = far * heads + (near ^ jnp.arange(heads, dtype=jnp.int32))
    own = (group[:, None] * tok_rows + inner[None, :]).reshape(-1)
    is_global = jnp.any(own[:, None] == global_pos[None, :], axis=1, keepdims=True)
    is_global = is_global.astype(jnp.float32)

    everyone = functools.partial(attend, place, rand_blocks.shape[1], listed, is_global, messages)
    if far_count == 2:
        own_far = swapped(own_kv, "far", 1)
        rest_far = swapped(pack(tok_rows, messages[1:]), "far", 1)
        plan = [(d, 0, "own", d) for d in range(heads)] + [(heads, 0, "other", 0)]
        old = everyone([], messages + [own_far], plan, 1, 0)
        plan = [(0, (d - 1) * tok_rows, "other", d) for d in range(1, heads)]
        out = everyone(old, [rest_far], plan, 1, parts)
    else:
        kvs = lax.all_gather(pack(tok_rows, messages), "far", tiled=True)
        plan = [(0, d * tok_rows, "step", d) for d in range(heads)]
        out = everyone([], [kvs], plan, far_count, parts)
    got = lax.all_to_all(out, ("near", "head"), 0, 0, tiled=True)
    return mix(here.reshape(1), got, o_blocks, order)


def solution(mesh):
    count, parts = mesh.devices.shape
    tm = ("far", "near")
    placed = (
        P(tm, None),
        P(None, "head"),
        P(None, "head"),
        P(None, "head"),
        P("head", None),
        P(tm, None),
        P(),
    )

    def run(tokens, q_weight, *rest):
        heads = q_weight.shape[1] // HEAD_DIM // parts
        split = Mesh(mesh.devices.reshape(count // heads, heads, parts), (*tm, "head"))
        body = jax.shard_map(
            shards, mesh=split, in_specs=placed, out_specs=P((*tm, "head"), None), check_vma=False
        )
        return body(tokens, q_weight, *rest)

    return run
```

```python
import functools
import math

import jax
import jax.numpy as jnp
from jax import lax
from jax.experimental import pallas as pl
from jax.experimental.pallas import tpu as pltpu
from jax.sharding import Mesh
from jax.sharding import PartitionSpec as P

HEAD_DIM = 64
BLOCK = 128
LANES = 128
DIGIT = 128
TILE_ROWS = 16
NEVER = -1e30
MIB = 1024 * 1024
VMEM = pl.BlockSpec(memory_space=pltpu.VMEM)
SMEM = pl.BlockSpec(memory_space=pltpu.SMEM)
ANY = pl.BlockSpec(memory_space=pl.ANY)


def low_half():
    return lax.broadcasted_iota(jnp.int32, (1, LANES), 1) < HEAD_DIM


def half_turn(block):
    return pltpu.roll(block, HEAD_DIM, 1)


def project_kernel(chunks, near_ref, rand_ref, t_hbm, q_hbm, k_hbm, v_hbm, own_ref, *refs):
    sent_refs, (t_ref, w_ref, all_ref, sems) = refs[:-4], refs[-4:]
    rows, depth = t_ref.shape
    feats = w_ref.shape[2]
    heads = feats // HEAD_DIM
    part = depth // chunks
    copies = []
    for c in range(chunks):
        at = slice(c * part, (c + 1) * part)
        group = [pltpu.make_async_copy(t_hbm.at[:, at], t_ref.at[:, at], sems.at[c, 0])]
        for i, w_hbm in enumerate((q_hbm, k_hbm, v_hbm)):
            group.append(pltpu.make_async_copy(w_hbm.at[at, :], w_ref.at[i, at, :], sems.at[c, 1 + i]))
        for i, copy in enumerate(group):
            copy.start(priority=i % 2)
        copies.append(group)
    totals = [None] * 3
    for c in range(chunks):
        at = slice(c * part, (c + 1) * part)
        for copy in copies[c]:
            copy.wait()
        for i in range(3):
            term = jnp.dot(t_ref[:, at], w_ref[i, at, :], preferred_element_type=jnp.float32)
            totals[i] = term if c == 0 else totals[i] + term
    q, k, v = totals
    low = low_half()
    for pair in range(heads // 2):
        at = slice(pair * LANES, (pair + 1) * LANES)
        q2, k2, v2 = q[:, at], k[:, at], v[:, at]
        top, bottom = q2[: rows // 2], q2[rows // 2 :]
        kv = (jnp.where(low, k2, half_turn(v2)), jnp.where(low, half_turn(k2), v2))
        qs = (jnp.where(low, top, half_turn(bottom)), jnp.where(low, half_turn(top), bottom))
        for odd in range(2):
            all_ref[2 * pair + odd, :rows, :] = kv[odd].astype(jnp.bfloat16)
            all_ref[2 * pair + odd, rows : rows + rows // 2, :] = qs[odd].astype(jnp.bfloat16)
    near = near_ref[0]
    digit_rows = sent_refs[0].shape[0] - rows - rows // 2
    row = lax.broadcasted_iota(jnp.int32, (digit_rows, LANES), 0)
    digits = jnp.zeros((digit_rows, LANES), jnp.float32)
    picks = rand_ref.shape[1]
    for j in range(rand_ref.shape[0]):
        for r in range(picks):
            at = 2 * (j * picks + r)
            value = rand_ref[j, r]
            digits = jnp.where(row == at, (value // DIGIT).astype(jnp.float32), digits)
            digits = jnp.where(row == at + 1, (value % DIGIT).astype(jnp.float32), digits)
    own_ref[...] = all_ref[near, :rows, :]
    for d in range(heads):
        sent_refs[d][: rows + rows // 2, :] = all_ref[near ^ d]
        sent_refs[d][rows + rows // 2 :, :] = digits.astype(jnp.bfloat16)


def project(near, rand_blocks, tokens, q_weight, k_weight, v_weight):
    rows, depth = tokens.shape
    feats = k_weight.shape[1]
    heads = feats // HEAD_DIM
    chunks = 4
    message = rows + rows // 2
    digit_rows = -(-2 * rand_blocks.size // TILE_ROWS) * TILE_ROWS
    return pl.pallas_call(
        functools.partial(project_kernel, chunks),
        in_specs=[SMEM, SMEM, ANY, ANY, ANY, ANY],
        out_specs=[VMEM] * (1 + heads),
        out_shape=[jax.ShapeDtypeStruct((rows, LANES), jnp.bfloat16)]
        + [jax.ShapeDtypeStruct((message + digit_rows, LANES), jnp.bfloat16)] * heads,
        scratch_shapes=[
            pltpu.VMEM((rows, depth), jnp.bfloat16),
            pltpu.VMEM((3, depth, feats), jnp.bfloat16),
            pltpu.VMEM((heads, message, LANES), jnp.bfloat16),
            pltpu.SemaphoreType.DMA((chunks, 4)),
        ],
        compiler_params=pltpu.CompilerParams(vmem_limit_bytes=56 * MIB),
        cost_estimate=pl.CostEstimate(
            flops=6 * rows * depth * feats, bytes_accessed=2 * depth * (rows + 3 * feats), transcendentals=0
        ),
    )(near, rand_blocks, tokens, q_weight, k_weight, v_weight)


def pack_kernel(*refs):
    out_ref = refs[-1]
    rows = out_ref.shape[0] // (len(refs) - 1)
    for i, ref in enumerate(refs[:-1]):
        out_ref[i * rows : (i + 1) * rows, :] = ref[:rows, :]


def pack(rows, messages):
    return pl.pallas_call(
        pack_kernel,
        in_specs=[VMEM] * len(messages),
        out_specs=VMEM,
        out_shape=jax.ShapeDtypeStruct((rows * len(messages), LANES), jnp.bfloat16),
        compiler_params=pltpu.CompilerParams(vmem_limit_bytes=32 * MIB),
    )(*messages)


def stage_kernel(o_hbm, after_ref, out_ref, sem):
    copy = pltpu.make_async_copy(o_hbm, out_ref, sem)
    copy.start()
    copy.wait()


def stage(o_weight, after):
    return pl.pallas_call(
        stage_kernel,
        in_specs=[ANY, ANY],
        out_specs=VMEM,
        out_shape=jax.ShapeDtypeStruct(o_weight.shape, o_weight.dtype),
        scratch_shapes=[pltpu.SemaphoreType.DMA],
        compiler_params=pltpu.CompilerParams(vmem_limit_bytes=32 * MIB),
    )(o_weight, after)


def prepare(heads, picks, near, far, span, messages, q_ref, block_ref, pick_ref):
    per_shard = span // BLOCK
    low = low_half()
    for d in range(heads):
        packed = messages[d][span : span + span // 2, :].astype(jnp.float32)
        top = jnp.where(low, packed, 0.0)
        bottom = jnp.where(low, half_turn(packed), 0.0)
        q_ref[d * span : d * span + span // 2, :] = top.astype(q_ref.dtype)
        q_ref[d * span + span // 2 : (d + 1) * span, :] = bottom.astype(q_ref.dtype)
        rand = messages[d][span + span // 2 :, :].astype(jnp.float32)
        for j in range(per_shard):
            row = slice(d * per_shard + j, d * per_shard + j + 1)
            block = (far * heads + (near ^ d)) * per_shard + j
            block_ref[row, :] = jnp.full((1, LANES), block, jnp.int32)
            for r in range(picks):
                at = 2 * (j * picks + r)
                pick = rand[at : at + 1, :] * DIGIT + rand[at + 1 : at + 2, :]
                pick_ref[r, row, :] = pick.astype(jnp.int32)


def fill_bias(heads, groups, near, listed_ref, block_ref, pick_ref, bias_ref):
    per_shard = block_ref.shape[0] // heads
    blocks = block_ref[...]
    picks = [pick_ref[r] for r in range(pick_ref.shape[0])]
    for g, there in enumerate(groups):
        for d in range(heads):
            for b in range(per_shard):
                key_block = (there * heads + (near ^ d)) * per_shard + b
                away = key_block - blocks
                times = listed_ref[pl.ds(key_block, 1), :] + jnp.where((away >= -2) & (away <= 1), 1.0, 0.0)
                for pick in picks:
                    times = times + jnp.where(pick == key_block, 1.0, 0.0)
                at = ((g * heads + d) * per_shard + b) * BLOCK
                bias_ref[:, at : at + BLOCK] = jnp.where(
                    times > 0, jnp.log2(jnp.maximum(times, 1.0)), NEVER
                )


def attend_rows(rows, tile, span, q_ref, glob_ref, bias_ref, keys, peak, total):
    per_shard = span // BLOCK
    scale = HEAD_DIM ** (-0.5) * math.log2(math.e)
    low = low_half()
    q = q_ref[rows, :]
    glob = jnp.broadcast_to(glob_ref[rows, :] > 0, (span, span))
    scores = []
    for key_ref, first, column in keys:
        s = lax.dot_general(
            q,
            key_ref[first : first + span, :],
            (((1,), (1,)), ((), ())),
            preferred_element_type=jnp.float32,
        )
        halves = []
        for j in range(per_shard):
            at = slice(j * BLOCK, (j + 1) * BLOCK)
            bias = bias_ref[pl.ds(tile * per_shard + j, 1), column : column + span]
            halves.append(s[at, :] * scale + jnp.where(glob[at, :], 0.0, bias))
        scores.append(jnp.concatenate(halves, axis=0))
    best = jnp.max(functools.reduce(jnp.maximum, scores), axis=1, keepdims=True)
    new = jnp.broadcast_to(best, (span, LANES)) if peak is None else jnp.maximum(peak, best)
    if total is not None:
        total = total * jnp.exp2(peak - new)
    for s, (key_ref, first, _) in zip(scores, keys):
        e = jnp.exp2(s - new[:, :1]).astype(jnp.bfloat16)
        v = jnp.where(low, jnp.ones((), jnp.bfloat16), key_ref[first : first + span, :])
        term = jnp.dot(e, v, preferred_element_type=jnp.float32)
        total = term if total is None else total + term
    return new, total


def finish(heads, parts, near, span, sums, out_ref):
    low = low_half()
    total = sums[...]
    sums[...] = total / half_turn(total)
    piece = span // parts
    for other in range(heads):
        for part in range(parts):
            first = pl.multiple_of((near ^ other) * span, span) + part * piece
            top = sums[pl.ds(first, piece // 2), :]
            bottom = sums[pl.ds(first + piece // 2, piece // 2), :]
            packed = jnp.where(low, half_turn(top), bottom)
            out_ref[other * parts + part] = packed.astype(out_ref.dtype)


def tile_rows(tile, span):
    return pl.ds(pl.multiple_of(tile * span, span), span)


def open_kernel(heads, picks, near_ref, far_ref, listed_ref, glob_ref, *refs):
    messages, (peaks, sums, q_ref, bias_ref, block_ref, pick_ref) = refs[:heads], refs[heads:]
    span = glob_ref.shape[0] // heads
    near, far = near_ref[0], far_ref[0]
    prepare(heads, picks, near, far, span, messages, q_ref, block_ref, pick_ref)
    fill_bias(heads, [far, far ^ 1], near, listed_ref, block_ref, pick_ref, bias_ref)
    keys = [(messages[d], 0, d * span) for d in range(heads)]

    def one_tile(tile, carry):
        rows = tile_rows(tile, span)
        new, total = attend_rows(rows, tile, span, q_ref, glob_ref, bias_ref, keys, None, None)
        peaks[rows, :] = new
        sums[rows, :] = total
        return carry

    lax.fori_loop(0, heads, one_tile, 0)


def more_kernel(heads, columns, parts, near_ref, glob_ref, q_ref, bias_ref, peak_in, sum_in, *refs):
    kv_refs, refs = refs[: len(columns)], refs[len(columns) :]
    if parts:
        out_ref, sums = refs
        peaks = None
    else:
        peaks, sums = refs
    span = glob_ref.shape[0] // heads
    keys = [(ref, 0, column) for ref, column in zip(kv_refs, columns)]

    def one_tile(tile, carry):
        rows = tile_rows(tile, span)
        new, total = attend_rows(
            rows, tile, span, q_ref, glob_ref, bias_ref, keys, peak_in[rows, :], sum_in[rows, :]
        )
        if peaks is not None:
            peaks[rows, :] = new
        sums[rows, :] = total
        return carry

    lax.fori_loop(0, heads, one_tile, 0)
    if parts:
        finish(heads, parts, near_ref[0], span, sums, out_ref)


def whole_kernel(
    heads, picks, parts, near_ref, far_ref, listed_ref, glob_ref, kv_ref, *refs
):
    messages, refs = refs[:heads], refs[heads:]
    out_ref, peaks, sums, q_ref, bias_ref, block_ref, pick_ref = refs
    span = glob_ref.shape[0] // heads
    near, far = near_ref[0], far_ref[0]
    step = pl.program_id(0)

    @pl.when(step == 0)
    def _():
        peaks[...] = jnp.full_like(peaks, NEVER)
        sums[...] = jnp.zeros_like(sums)
        prepare(heads, picks, near, far, span, messages, q_ref, block_ref, pick_ref)

    fill_bias(heads, [step], near, listed_ref, block_ref, pick_ref, bias_ref)
    keys = [(kv_ref, d * span, d * span) for d in range(heads)]

    def one_tile(tile, carry):
        rows = tile_rows(tile, span)
        new, total = attend_rows(
            rows, tile, span, q_ref, glob_ref, bias_ref, keys, peaks[rows, :], sums[rows, :]
        )
        peaks[rows, :] = new
        sums[rows, :] = total
        return carry

    lax.fori_loop(0, heads, one_tile, 0)

    @pl.when(step == pl.num_programs(0) - 1)
    def _():
        finish(heads, parts, near, span, sums, out_ref)


def attend_cost(rows, keys):
    return pl.CostEstimate(
        flops=4 * rows * keys * LANES, bytes_accessed=4 * (rows + keys) * LANES, transcendentals=rows * keys
    )


def open_attend(near, far, picks, listed, is_global, messages):
    heads, rows = len(messages), is_global.shape[0]
    blocks = rows // BLOCK
    state = jax.ShapeDtypeStruct((rows, LANES), jnp.float32)
    return pl.pallas_call(
        functools.partial(open_kernel, heads, picks),
        in_specs=[SMEM, SMEM] + [VMEM] * (2 + heads),
        out_specs=[VMEM] * 4,
        out_shape=[
            state,
            state,
            jax.ShapeDtypeStruct((rows, LANES), jnp.bfloat16),
            jax.ShapeDtypeStruct((blocks, 2 * rows), jnp.float32),
        ],
        scratch_shapes=[
            pltpu.VMEM((blocks, LANES), jnp.int32),
            pltpu.VMEM((picks, blocks, LANES), jnp.int32),
        ],
        compiler_params=pltpu.CompilerParams(vmem_limit_bytes=24 * MIB),
        cost_estimate=attend_cost(rows, rows),
    )(near, far, listed, is_global, *messages)


def more_attend(near, is_global, heads, q, bias, old, kvs, columns, parts):
    rows = is_global.shape[0]
    span = rows // heads
    state = jax.ShapeDtypeStruct((rows, LANES), jnp.float32)
    if parts:
        out_shape = jax.ShapeDtypeStruct((heads * parts, span // parts // 2, LANES), jnp.bfloat16)
        out_specs, scratch = VMEM, [pltpu.VMEM((rows, LANES), jnp.float32)]
    else:
        out_shape, out_specs, scratch = [state] * 2, [VMEM] * 2, []
    return pl.pallas_call(
        functools.partial(more_kernel, heads, columns, parts),
        in_specs=[SMEM] + [VMEM] * (5 + len(kvs)),
        out_specs=out_specs,
        out_shape=out_shape,
        scratch_shapes=scratch,
        compiler_params=pltpu.CompilerParams(vmem_limit_bytes=24 * MIB),
        cost_estimate=attend_cost(rows, span * len(kvs)),
    )(near, is_global, q, bias, *old, *kvs)


def whole_attend(near, far, picks, listed, is_global, messages, kvs, parts):
    heads, rows = len(messages), is_global.shape[0]
    blocks, steps = rows // BLOCK, kvs.shape[0] // rows
    return pl.pallas_call(
        functools.partial(whole_kernel, heads, picks, parts),
        grid=(steps,),
        in_specs=[SMEM, SMEM, VMEM, VMEM, pl.BlockSpec((rows, LANES), lambda s: (s, 0))] + [VMEM] * heads,
        out_specs=VMEM,
        out_shape=jax.ShapeDtypeStruct((heads * parts, rows // heads // parts // 2, LANES), jnp.bfloat16),
        scratch_shapes=[
            pltpu.VMEM((rows, LANES), jnp.float32),
            pltpu.VMEM((rows, LANES), jnp.float32),
            pltpu.VMEM((rows, LANES), jnp.bfloat16),
            pltpu.VMEM((blocks, rows), jnp.float32),
            pltpu.VMEM((blocks, LANES), jnp.int32),
            pltpu.VMEM((picks, blocks, LANES), jnp.int32),
        ],
        compiler_params=pltpu.CompilerParams(vmem_limit_bytes=24 * MIB),
        cost_estimate=attend_cost(rows, kvs.shape[0]),
    )(near, far, listed, is_global, kvs, *messages)


def mix_kernel(near_count, order, here_ref, got_ref, *refs):
    parts = len(order)
    half = got_ref.shape[1]
    low = low_half()
    total = None
    for i, d in enumerate(order):
        source = here_ref[0] ^ d
        columns = []
        for near in range(0, near_count, 2):
            even = got_ref[near * parts + source].astype(jnp.float32)
            odd = got_ref[(near + 1) * parts + source].astype(jnp.float32)
            top = jnp.where(low, even, half_turn(odd))
            bottom = jnp.where(low, half_turn(even), odd)
            columns.append(jnp.concatenate([top, bottom], axis=0).astype(jnp.bfloat16))
        rows = jnp.concatenate(columns, axis=1)
        term = jnp.dot(rows, refs[i][...], preferred_element_type=jnp.float32)
        total = term if total is None else total + term
    refs[parts][...] = total.astype(refs[parts].dtype)


def mix(here, got, o_blocks, order):
    parts = len(o_blocks)
    return pl.pallas_call(
        functools.partial(mix_kernel, got.shape[0] // parts, order),
        out_shape=jax.ShapeDtypeStruct((2 * got.shape[1], o_blocks[0].shape[1]), jnp.bfloat16),
        in_specs=[SMEM] + [VMEM] * (1 + parts),
        out_specs=VMEM,
        compiler_params=pltpu.CompilerParams(vmem_limit_bytes=32 * MIB),
    )(here, got, *o_blocks)


def swapped(block, axis, distance):
    return lax.ppermute(block, axis, [(i, i ^ distance) for i in range(lax.axis_size(axis))])


def shards(tokens, q_weight, k_weight, v_weight, o_weight, rand_blocks, global_pos):
    tok_rows = tokens.shape[0]
    far_count, heads, parts = (lax.axis_size(axis) for axis in ("far", "near", "head"))
    far, near, here = (lax.axis_index(axis).astype(jnp.int32) for axis in ("far", "near", "head"))
    near_at, far_at, here_at = (at.reshape(1) for at in (near, far, here))
    picks = rand_blocks.shape[1]

    own_kv, *sent = project(near_at, rand_blocks, tokens, q_weight, k_weight, v_weight)
    messages = [sent[0]] + [swapped(sent[d], "near", d) for d in range(1, heads)]

    o_blocks, order = [stage(o_weight, messages[1])], [0]
    distance = parts // 2
    while distance:
        o_blocks = o_blocks + [swapped(block, "head", distance) for block in o_blocks]
        order = order + [d ^ distance for d in order]
        distance //= 2

    inner = jnp.arange(tok_rows, dtype=jnp.int32)
    spots = jnp.arange(far_count * heads * tok_rows, dtype=jnp.int32)
    listed = jnp.any(spots[None, :] == global_pos[:, None], axis=0)
    listed = listed.astype(jnp.float32).reshape(-1, BLOCK)
    group = far * heads + (near ^ jnp.arange(heads, dtype=jnp.int32))
    own = (group[:, None] * tok_rows + inner[None, :]).reshape(-1)
    is_global = jnp.any(own[:, None] == global_pos[None, :], axis=1, keepdims=True)
    is_global = is_global.astype(jnp.float32)

    if far_count == 2:
        apart = [swapped(own_kv, "far", 1)]
        apart += [swapped(pack(tok_rows, [message]), "far", 1) for message in messages[1:]]
        *old, q, bias = open_attend(near_at, far_at, picks, listed, is_global, messages)
        columns = [(heads + d) * tok_rows for d in range(heads)]
        more = functools.partial(more_attend, near_at, is_global, heads, q, bias)
        old = more(old, apart[:-1], columns[:-1], 0)
        out = more(old, apart[-1:], columns[-1:], parts)
    else:
        kvs = lax.all_gather(pack(tok_rows, messages), "far", tiled=True)
        out = whole_attend(near_at, far_at, picks, listed, is_global, messages, kvs, parts)
    got = lax.all_to_all(out, ("near", "head"), 0, 0, tiled=True)
    return mix(here_at, got, o_blocks, order)


def solution(mesh):
    count, parts = mesh.devices.shape
    tm = ("far", "near")
    placed = (
        P(tm, None),
        P(None, "head"),
        P(None, "head"),
        P(None, "head"),
        P("head", None),
        P(tm, None),
        P(),
    )

    def run(tokens, q_weight, *rest):
        heads = q_weight.shape[1] // HEAD_DIM // parts
        split = Mesh(mesh.devices.reshape(count // heads, heads, parts), (*tm, "head"))
        body = jax.shard_map(
            shards, mesh=split, in_specs=placed, out_specs=P((*tm, "head"), None), check_vma=False
        )
        return body(tokens, q_weight, *rest)

    return run
```

```python
import functools
import math

import jax
import jax.numpy as jnp
from jax import lax
from jax.experimental import pallas as pl
from jax.experimental.pallas import tpu as pltpu
from jax.sharding import Mesh
from jax.sharding import PartitionSpec as P

HEAD_DIM = 64
BLOCK = 128
LANES = 128
DIGIT = 128
TILE_ROWS = 16
NEVER = -1e30
MIB = 1024 * 1024
VMEM = pl.BlockSpec(memory_space=pltpu.VMEM)
SMEM = pl.BlockSpec(memory_space=pltpu.SMEM)
HBM = pl.BlockSpec(memory_space=pltpu.HBM)
ANY = pl.BlockSpec(memory_space=pl.ANY)


def low_half():
    return lax.broadcasted_iota(jnp.int32, (1, LANES), 1) < HEAD_DIM


def half_turn(block):
    return pltpu.roll(block, HEAD_DIM, 1)


def project_kernel(chunks, near_ref, rand_ref, t_hbm, q_hbm, k_hbm, v_hbm, own_ref, *refs):
    sent_refs, (t_ref, w_ref, all_ref, sems) = refs[:-4], refs[-4:]
    rows, depth = t_ref.shape
    feats = w_ref.shape[2]
    heads = feats // HEAD_DIM
    part = depth // chunks
    copies = []
    for c in range(chunks):
        at = slice(c * part, (c + 1) * part)
        group = [pltpu.make_async_copy(t_hbm.at[:, at], t_ref.at[:, at], sems.at[c, 0])]
        for i, w_hbm in enumerate((q_hbm, k_hbm, v_hbm)):
            group.append(pltpu.make_async_copy(w_hbm.at[at, :], w_ref.at[i, at, :], sems.at[c, 1 + i]))
        for copy in group:
            copy.start()
        copies.append(group)
    totals = [None] * 3
    for c in range(chunks):
        at = slice(c * part, (c + 1) * part)
        for copy in copies[c]:
            copy.wait()
        for i in range(3):
            term = jnp.dot(t_ref[:, at], w_ref[i, at, :], preferred_element_type=jnp.float32)
            totals[i] = term if c == 0 else totals[i] + term
    q, k, v = totals
    low = low_half()
    for pair in range(heads // 2):
        at = slice(pair * LANES, (pair + 1) * LANES)
        q2, k2, v2 = q[:, at], k[:, at], v[:, at]
        top, bottom = q2[: rows // 2], q2[rows // 2 :]
        kv = (jnp.where(low, k2, half_turn(v2)), jnp.where(low, half_turn(k2), v2))
        qs = (jnp.where(low, top, half_turn(bottom)), jnp.where(low, half_turn(top), bottom))
        for odd in range(2):
            all_ref[2 * pair + odd, :rows, :] = kv[odd].astype(jnp.bfloat16)
            all_ref[2 * pair + odd, rows : rows + rows // 2, :] = qs[odd].astype(jnp.bfloat16)
    near = near_ref[0]
    digit_rows = sent_refs[0].shape[0] - rows - rows // 2
    row = lax.broadcasted_iota(jnp.int32, (digit_rows, LANES), 0)
    digits = jnp.zeros((digit_rows, LANES), jnp.float32)
    picks = rand_ref.shape[1]
    for j in range(rand_ref.shape[0]):
        for r in range(picks):
            at = 2 * (j * picks + r)
            value = rand_ref[j, r]
            digits = jnp.where(row == at, (value // DIGIT).astype(jnp.float32), digits)
            digits = jnp.where(row == at + 1, (value % DIGIT).astype(jnp.float32), digits)
    own_ref[...] = all_ref[near, :rows, :]
    for d in range(heads):
        sent_refs[d][: rows + rows // 2, :] = all_ref[near ^ d]
        sent_refs[d][rows + rows // 2 :, :] = digits.astype(jnp.bfloat16)


def project(near, rand_blocks, tokens, q_weight, k_weight, v_weight):
    rows, depth = tokens.shape
    feats = k_weight.shape[1]
    heads = feats // HEAD_DIM
    chunks = 4
    message = rows + rows // 2
    digit_rows = -(-2 * rand_blocks.size // TILE_ROWS) * TILE_ROWS
    return pl.pallas_call(
        functools.partial(project_kernel, chunks),
        in_specs=[SMEM, SMEM, HBM, HBM, HBM, HBM],
        out_specs=[VMEM] * (1 + heads),
        out_shape=[jax.ShapeDtypeStruct((rows, LANES), jnp.bfloat16)]
        + [jax.ShapeDtypeStruct((message + digit_rows, LANES), jnp.bfloat16)] * heads,
        scratch_shapes=[
            pltpu.VMEM((rows, depth), jnp.bfloat16),
            pltpu.VMEM((3, depth, feats), jnp.bfloat16),
            pltpu.VMEM((heads, message, LANES), jnp.bfloat16),
            pltpu.SemaphoreType.DMA((chunks, 4)),
        ],
        compiler_params=pltpu.CompilerParams(vmem_limit_bytes=16 * MIB),
        cost_estimate=pl.CostEstimate(
            flops=6 * rows * depth * feats, bytes_accessed=2 * depth * (rows + 3 * feats), transcendentals=0
        ),
    )(near, rand_blocks, tokens, q_weight, k_weight, v_weight)


def pack_kernel(*refs):
    out_ref = refs[-1]
    rows = out_ref.shape[0] // (len(refs) - 1)
    for i, ref in enumerate(refs[:-1]):
        out_ref[i * rows : (i + 1) * rows, :] = ref[:rows, :]


def pack(rows, messages):
    return pl.pallas_call(
        pack_kernel,
        in_specs=[VMEM] * len(messages),
        out_specs=VMEM,
        out_shape=jax.ShapeDtypeStruct((rows * len(messages), LANES), jnp.bfloat16),
        compiler_params=pltpu.CompilerParams(vmem_limit_bytes=32 * MIB),
    )(*messages)


def stage_kernel(o_hbm, *refs):
    out_ref, sem = refs[-2:]
    copy = pltpu.make_async_copy(o_hbm, out_ref, sem)
    copy.start()
    copy.wait()


def stage(o_weight, after):
    return pl.pallas_call(
        stage_kernel,
        in_specs=[HBM] + [ANY] * len(after),
        out_specs=VMEM,
        out_shape=jax.ShapeDtypeStruct(o_weight.shape, o_weight.dtype),
        scratch_shapes=[pltpu.SemaphoreType.DMA],
        compiler_params=pltpu.CompilerParams(vmem_limit_bytes=32 * MIB),
    )(o_weight, *after)


def prepare(heads, picks, near, far, span, messages, q_ref, block_ref, pick_ref):
    per_shard = span // BLOCK
    low = low_half()
    for d in range(heads):
        packed = messages[d][span : span + span // 2, :].astype(jnp.float32)
        top = jnp.where(low, packed, 0.0)
        bottom = jnp.where(low, half_turn(packed), 0.0)
        q_ref[d * span : d * span + span // 2, :] = top.astype(q_ref.dtype)
        q_ref[d * span + span // 2 : (d + 1) * span, :] = bottom.astype(q_ref.dtype)
        rand = messages[d][span + span // 2 :, :].astype(jnp.float32)
        for j in range(per_shard):
            row = slice(d * per_shard + j, d * per_shard + j + 1)
            block = (far * heads + (near ^ d)) * per_shard + j
            block_ref[row, :] = jnp.full((1, LANES), block, jnp.int32)
            for r in range(picks):
                at = 2 * (j * picks + r)
                pick = rand[at : at + 1, :] * DIGIT + rand[at + 1 : at + 2, :]
                pick_ref[r, row, :] = pick.astype(jnp.int32)


def fill_bias(heads, groups, near, listed_ref, block_ref, pick_ref, bias_ref):
    per_shard = block_ref.shape[0] // heads
    blocks = block_ref[...]
    picks = [pick_ref[r] for r in range(pick_ref.shape[0])]
    for g, there in enumerate(groups):
        for d in range(heads):
            for b in range(per_shard):
                key_block = (there * heads + (near ^ d)) * per_shard + b
                away = key_block - blocks
                times = listed_ref[pl.ds(key_block, 1), :] + jnp.where((away >= -2) & (away <= 1), 1.0, 0.0)
                for pick in picks:
                    times = times + jnp.where(pick == key_block, 1.0, 0.0)
                at = ((g * heads + d) * per_shard + b) * BLOCK
                bias_ref[:, at : at + BLOCK] = jnp.where(
                    times > 0, jnp.log2(jnp.maximum(times, 1.0)), NEVER
                )


def attend_rows(rows, tile, span, q_ref, glob_ref, bias_ref, keys, peak, total):
    per_shard = span // BLOCK
    scale = HEAD_DIM ** (-0.5) * math.log2(math.e)
    low = low_half()
    q = q_ref[rows, :]
    glob = jnp.broadcast_to(glob_ref[rows, :] > 0, (span, span))
    scores = []
    for key_ref, first, column in keys:
        s = lax.dot_general(
            q,
            key_ref[first : first + span, :],
            (((1,), (1,)), ((), ())),
            preferred_element_type=jnp.float32,
        )
        halves = []
        for j in range(per_shard):
            at = slice(j * BLOCK, (j + 1) * BLOCK)
            bias = bias_ref[tile * per_shard + j : tile * per_shard + j + 1, column : column + span]
            halves.append(s[at, :] * scale + jnp.where(glob[at, :], 0.0, bias))
        scores.append(jnp.concatenate(halves, axis=0))
    best = jnp.max(functools.reduce(jnp.maximum, scores), axis=1, keepdims=True)
    new = jnp.broadcast_to(best, (span, LANES)) if peak is None else jnp.maximum(peak, best)
    if total is not None:
        total = total * jnp.exp2(peak - new)
    for s, (key_ref, first, _) in zip(scores, keys):
        e = jnp.exp2(s - new[:, :1]).astype(jnp.bfloat16)
        v = jnp.where(low, jnp.ones((), jnp.bfloat16), key_ref[first : first + span, :])
        term = jnp.dot(e, v, preferred_element_type=jnp.float32)
        total = term if total is None else total + term
    return new, total


def finish(heads, parts, near, span, sums, out_ref):
    low = low_half()
    total = sums[...]
    sums[...] = total / half_turn(total)
    piece = span // parts
    for other in range(heads):
        for part in range(parts):
            first = pl.multiple_of((near ^ other) * span, span) + part * piece
            top = sums[pl.ds(first, piece // 2), :]
            bottom = sums[pl.ds(first + piece // 2, piece // 2), :]
            packed = jnp.where(low, half_turn(top), bottom)
            out_ref[other * parts + part] = packed.astype(out_ref.dtype)


def tile_rows(tile, span):
    return slice(tile * span, (tile + 1) * span)


def open_kernel(heads, picks, near_ref, far_ref, listed_ref, glob_ref, *refs):
    messages, (peaks, sums, q_ref, bias_ref, block_ref, pick_ref) = refs[:heads], refs[heads:]
    span = glob_ref.shape[0] // heads
    near, far = near_ref[0], far_ref[0]
    prepare(heads, picks, near, far, span, messages, q_ref, block_ref, pick_ref)
    fill_bias(heads, [far, far ^ 1], near, listed_ref, block_ref, pick_ref, bias_ref)
    keys = [(messages[d], 0, d * span) for d in range(heads)]

    for tile in range(heads):
        rows = tile_rows(tile, span)
        new, total = attend_rows(rows, tile, span, q_ref, glob_ref, bias_ref, keys, None, None)
        peaks[rows, :] = new
        sums[rows, :] = total


def more_kernel(heads, columns, parts, near_ref, glob_ref, q_ref, bias_ref, peak_in, sum_in, *refs):
    kv_refs, refs = refs[: len(columns)], refs[len(columns) :]
    if parts:
        out_ref, sums = refs
        peaks = None
    else:
        peaks, sums = refs
    span = glob_ref.shape[0] // heads
    keys = [(ref, 0, column) for ref, column in zip(kv_refs, columns)]

    for tile in range(heads):
        rows = tile_rows(tile, span)
        new, total = attend_rows(
            rows, tile, span, q_ref, glob_ref, bias_ref, keys, peak_in[rows, :], sum_in[rows, :]
        )
        if peaks is not None:
            peaks[rows, :] = new
        sums[rows, :] = total
    if parts:
        finish(heads, parts, near_ref[0], span, sums, out_ref)


def whole_kernel(
    heads, picks, parts, near_ref, far_ref, listed_ref, glob_ref, kv_ref, *refs
):
    messages, refs = refs[:heads], refs[heads:]
    out_ref, peaks, sums, q_ref, bias_ref, block_ref, pick_ref = refs
    span = glob_ref.shape[0] // heads
    near, far = near_ref[0], far_ref[0]
    step = pl.program_id(0)

    @pl.when(step == 0)
    def _():
        peaks[...] = jnp.full_like(peaks, NEVER)
        sums[...] = jnp.zeros_like(sums)
        prepare(heads, picks, near, far, span, messages, q_ref, block_ref, pick_ref)

    fill_bias(heads, [step], near, listed_ref, block_ref, pick_ref, bias_ref)
    keys = [(kv_ref, d * span, d * span) for d in range(heads)]

    for tile in range(heads):
        rows = tile_rows(tile, span)
        new, total = attend_rows(
            rows, tile, span, q_ref, glob_ref, bias_ref, keys, peaks[rows, :], sums[rows, :]
        )
        peaks[rows, :] = new
        sums[rows, :] = total

    @pl.when(step == pl.num_programs(0) - 1)
    def _():
        finish(heads, parts, near, span, sums, out_ref)


def attend_cost(rows, keys):
    return pl.CostEstimate(
        flops=4 * rows * keys * LANES, bytes_accessed=4 * (rows + keys) * LANES, transcendentals=rows * keys
    )


def open_attend(near, far, picks, listed, is_global, messages):
    heads, rows = len(messages), is_global.shape[0]
    blocks = rows // BLOCK
    state = jax.ShapeDtypeStruct((rows, LANES), jnp.float32)
    return pl.pallas_call(
        functools.partial(open_kernel, heads, picks),
        in_specs=[SMEM, SMEM] + [VMEM] * (2 + heads),
        out_specs=[VMEM] * 4,
        out_shape=[
            state,
            state,
            jax.ShapeDtypeStruct((rows, LANES), jnp.bfloat16),
            jax.ShapeDtypeStruct((blocks, 2 * rows), jnp.float32),
        ],
        scratch_shapes=[
            pltpu.VMEM((blocks, LANES), jnp.int32),
            pltpu.VMEM((picks, blocks, LANES), jnp.int32),
        ],
        compiler_params=pltpu.CompilerParams(vmem_limit_bytes=24 * MIB),
        cost_estimate=attend_cost(rows, rows),
    )(near, far, listed, is_global, *messages)


def more_attend(near, is_global, heads, q, bias, old, kvs, columns, parts):
    rows = is_global.shape[0]
    span = rows // heads
    state = jax.ShapeDtypeStruct((rows, LANES), jnp.float32)
    if parts:
        out_shape = jax.ShapeDtypeStruct((heads * parts, span // parts // 2, LANES), jnp.bfloat16)
        out_specs, scratch = VMEM, [pltpu.VMEM((rows, LANES), jnp.float32)]
    else:
        out_shape, out_specs, scratch = [state] * 2, [VMEM] * 2, []
    return pl.pallas_call(
        functools.partial(more_kernel, heads, columns, parts),
        in_specs=[SMEM] + [VMEM] * (5 + len(kvs)),
        out_specs=out_specs,
        out_shape=out_shape,
        scratch_shapes=scratch,
        compiler_params=pltpu.CompilerParams(vmem_limit_bytes=24 * MIB),
        cost_estimate=attend_cost(rows, span * len(kvs)),
    )(near, is_global, q, bias, *old, *kvs)


def whole_attend(near, far, picks, listed, is_global, messages, kvs, parts):
    heads, rows = len(messages), is_global.shape[0]
    blocks, steps = rows // BLOCK, kvs.shape[0] // rows
    return pl.pallas_call(
        functools.partial(whole_kernel, heads, picks, parts),
        grid=(steps,),
        in_specs=[SMEM, SMEM, VMEM, VMEM, pl.BlockSpec((rows, LANES), lambda s: (s, 0))] + [VMEM] * heads,
        out_specs=VMEM,
        out_shape=jax.ShapeDtypeStruct((heads * parts, rows // heads // parts // 2, LANES), jnp.bfloat16),
        scratch_shapes=[
            pltpu.VMEM((rows, LANES), jnp.float32),
            pltpu.VMEM((rows, LANES), jnp.float32),
            pltpu.VMEM((rows, LANES), jnp.bfloat16),
            pltpu.VMEM((blocks, rows), jnp.float32),
            pltpu.VMEM((blocks, LANES), jnp.int32),
            pltpu.VMEM((picks, blocks, LANES), jnp.int32),
        ],
        compiler_params=pltpu.CompilerParams(vmem_limit_bytes=24 * MIB),
        cost_estimate=attend_cost(rows, kvs.shape[0]),
    )(near, far, listed, is_global, kvs, *messages)


def mix_kernel(near_count, order, here_ref, got_ref, *refs):
    parts = len(order)
    half = got_ref.shape[1]
    low = low_half()
    total = None
    for i, d in enumerate(order):
        source = here_ref[0] ^ d
        columns = []
        for near in range(0, near_count, 2):
            even = got_ref[near * parts + source].astype(jnp.float32)
            odd = got_ref[(near + 1) * parts + source].astype(jnp.float32)
            top = jnp.where(low, even, half_turn(odd))
            bottom = jnp.where(low, half_turn(even), odd)
            columns.append(jnp.concatenate([top, bottom], axis=0).astype(jnp.bfloat16))
        rows = jnp.concatenate(columns, axis=1)
        term = jnp.dot(rows, refs[i][...], preferred_element_type=jnp.float32)
        total = term if total is None else total + term
    refs[parts][...] = total.astype(refs[parts].dtype)


def mix(here, got, o_blocks, order):
    parts = len(o_blocks)
    return pl.pallas_call(
        functools.partial(mix_kernel, got.shape[0] // parts, order),
        out_shape=jax.ShapeDtypeStruct((2 * got.shape[1], o_blocks[0].shape[1]), jnp.bfloat16),
        in_specs=[SMEM] + [VMEM] * (1 + parts),
        out_specs=VMEM,
        compiler_params=pltpu.CompilerParams(vmem_limit_bytes=32 * MIB),
    )(here, got, *o_blocks)


def swapped(block, axis, distance):
    return lax.ppermute(block, axis, [(i, i ^ distance) for i in range(lax.axis_size(axis))])


def shards(tokens, q_weight, k_weight, v_weight, o_weight, rand_blocks, global_pos):
    tok_rows = tokens.shape[0]
    far_count, heads, parts = (lax.axis_size(axis) for axis in ("far", "near", "head"))
    far, near, here = (lax.axis_index(axis).astype(jnp.int32) for axis in ("far", "near", "head"))
    near_at, far_at, here_at = (at.reshape(1) for at in (near, far, here))
    picks = rand_blocks.shape[1]

    own_kv, *sent = project(near_at, rand_blocks, tokens, q_weight, k_weight, v_weight)
    messages = [sent[0]] + [swapped(sent[d], "near", d) for d in range(1, heads)]

    inner = jnp.arange(tok_rows, dtype=jnp.int32)
    spots = jnp.arange(far_count * heads * tok_rows, dtype=jnp.int32)
    listed = jnp.any(spots[None, :] == global_pos[:, None], axis=0)
    listed = listed.astype(jnp.float32).reshape(-1, BLOCK)
    group = far * heads + (near ^ jnp.arange(heads, dtype=jnp.int32))
    own = (group[:, None] * tok_rows + inner[None, :]).reshape(-1)
    is_global = jnp.any(own[:, None] == global_pos[None, :], axis=1, keepdims=True)
    is_global = is_global.astype(jnp.float32)

    if far_count == 2:
        packed = [pack(tok_rows, [message]) for message in messages[1:]]
        apart = [swapped(block, "far", 1) for block in [own_kv] + packed]
        *old, q, bias = open_attend(near_at, far_at, picks, listed, is_global, messages)
        columns = [(heads + d) * tok_rows for d in range(heads)]
        more = functools.partial(more_attend, near_at, is_global, heads, q, bias)
        old = more(old, apart[:-1], columns[:-1], 0)
        out = more(old, apart[-1:], columns[-1:], parts)
    else:
        packed = [pack(tok_rows, messages)]
        kvs = lax.all_gather(packed[0], "far", tiled=True)
        out = whole_attend(near_at, far_at, picks, listed, is_global, messages, kvs, parts)
    o_blocks, order = [stage(o_weight, packed)], [0]
    distance = parts // 2
    while distance:
        o_blocks = o_blocks + [swapped(block, "head", distance) for block in o_blocks]
        order = order + [d ^ distance for d in order]
        distance //= 2

    got = lax.all_to_all(out, ("near", "head"), 0, 0, tiled=True)
    return mix(here_at, got, o_blocks, order)


def solution(mesh):
    count, parts = mesh.devices.shape
    tm = ("far", "near")
    placed = (
        P(tm, None),
        P(None, "head"),
        P(None, "head"),
        P(None, "head"),
        P("head", None),
        P(tm, None),
        P(),
    )

    def run(tokens, q_weight, *rest):
        heads = q_weight.shape[1] // HEAD_DIM // parts
        split = Mesh(mesh.devices.reshape(count // heads, heads, parts), (*tm, "head"))
        body = jax.shard_map(
            shards, mesh=split, in_specs=placed, out_specs=P((*tm, "head"), None), check_vma=False
        )
        return body(tokens, q_weight, *rest)

    return run
```

```python
import functools
import math

import jax
import jax.numpy as jnp
from jax import lax
from jax.experimental import pallas as pl
from jax.experimental.pallas import tpu as pltpu
from jax.sharding import Mesh
from jax.sharding import PartitionSpec as P

HEAD_DIM = 64
BLOCK = 128
LANES = 128
DIGIT = 128
TILE_ROWS = 16
NEVER = -1e30
CORES = 2
MIB = 1024 * 1024
VMEM = pl.BlockSpec(memory_space=pltpu.VMEM)
SMEM = pl.BlockSpec(memory_space=pltpu.SMEM)
HBM = pl.BlockSpec(memory_space=pltpu.HBM)
ANY = pl.BlockSpec(memory_space=pl.ANY)


def low_half():
    return lax.broadcasted_iota(jnp.int32, (1, LANES), 1) < HEAD_DIM


def half_turn(block):
    return pltpu.roll(block, HEAD_DIM, 1)


def own_half(near):
    return lax.broadcasted_iota(jnp.int32, (1, LANES), 1) // HEAD_DIM == near % 2


def project_kernel(cuts, near_ref, rand_ref, t_hbm, q_hbm, k_hbm, v_hbm, own_ref, *refs):
    sent_refs, (t_ref, q_ref, k_ref, v_ref, all_ref, sems) = refs[:-6], refs[-6:]
    rows = t_ref.shape[0]
    heads = k_ref.shape[1] // HEAD_DIM
    copies = []
    for i, (source, target) in enumerate(
        ((t_hbm, t_ref), (k_hbm, k_ref), (v_hbm, v_ref), (q_hbm, q_ref))
    ):
        part = source.shape[0] // cuts
        group = []
        for c in range(cuts):
            at = slice(c * part, (c + 1) * part)
            copy = pltpu.make_async_copy(source.at[at, :], target.at[at, :], sems.at[i, c])
            copy.start()
            group.append(copy)
        copies.append(group)

    def product(i, weight_ref):
        for copy in copies[i]:
            copy.wait()
        return jnp.dot(t_ref[...], weight_ref[...], preferred_element_type=jnp.float32)

    for copy in copies[0]:
        copy.wait()
    low = low_half()
    k = product(1, k_ref)
    v = product(2, v_ref)
    for pair in range(heads // 2):
        at = slice(pair * LANES, (pair + 1) * LANES)
        key, value = k[:, at], half_turn(v[:, at])
        all_ref[2 * pair, :rows, :] = jnp.where(low, key, value).astype(jnp.bfloat16)
        all_ref[2 * pair + 1, :rows, :] = jnp.where(low, value, key).astype(jnp.bfloat16)
    q = product(3, q_ref)
    for pair in range(heads // 2):
        at = slice(pair * LANES, (pair + 1) * LANES)
        top, bottom = q[: rows // 2, at], half_turn(q[rows // 2 :, at])
        all_ref[2 * pair, rows:, :] = jnp.where(low, top, bottom).astype(jnp.bfloat16)
        all_ref[2 * pair + 1, rows:, :] = jnp.where(low, bottom, top).astype(jnp.bfloat16)
    near = near_ref[0]
    digit_rows = sent_refs[0].shape[0] - rows - rows // 2
    row = lax.broadcasted_iota(jnp.int32, (digit_rows, LANES), 0)
    digits = jnp.zeros((digit_rows, LANES), jnp.float32)
    picks = rand_ref.shape[1]
    for j in range(rand_ref.shape[0]):
        for r in range(picks):
            at = 2 * (j * picks + r)
            value = rand_ref[j, r]
            digits = jnp.where(row == at, (value // DIGIT).astype(jnp.float32), digits)
            digits = jnp.where(row == at + 1, (value % DIGIT).astype(jnp.float32), digits)
    digits = digits.astype(jnp.bfloat16)
    own_ref[...] = all_ref[near, :rows, :]
    for d in range(heads):
        sent_refs[d][: rows + rows // 2, :] = all_ref[near ^ d]
        sent_refs[d][rows + rows // 2 :, :] = digits


def project(near, rand_blocks, tokens, q_weight, k_weight, v_weight):
    rows, depth = tokens.shape
    feats = k_weight.shape[1]
    heads = feats // HEAD_DIM
    cuts = 2
    message = rows + rows // 2
    digit_rows = -(-2 * rand_blocks.size // TILE_ROWS) * TILE_ROWS
    return pl.pallas_call(
        functools.partial(project_kernel, cuts),
        in_specs=[SMEM, SMEM, HBM, HBM, HBM, HBM],
        out_specs=[VMEM] * (1 + heads),
        out_shape=[jax.ShapeDtypeStruct((rows, LANES), jnp.bfloat16)]
        + [jax.ShapeDtypeStruct((message + digit_rows, LANES), jnp.bfloat16)] * heads,
        scratch_shapes=[
            pltpu.VMEM((rows, depth), jnp.bfloat16),
            pltpu.VMEM((depth, feats), jnp.bfloat16),
            pltpu.VMEM((depth, feats), jnp.bfloat16),
            pltpu.VMEM((depth, feats), jnp.bfloat16),
            pltpu.VMEM((heads, message, LANES), jnp.bfloat16),
            pltpu.SemaphoreType.DMA((4, cuts)),
        ],
        compiler_params=pltpu.CompilerParams(vmem_limit_bytes=60 * MIB),
        cost_estimate=pl.CostEstimate(
            flops=6 * rows * depth * feats, bytes_accessed=2 * depth * (rows + 3 * feats), transcendentals=0
        ),
    )(near, rand_blocks, tokens, q_weight, k_weight, v_weight)


def pack_kernel(*refs):
    out_ref = refs[-1]
    rows = out_ref.shape[0] // (len(refs) - 1)
    for i, ref in enumerate(refs[:-1]):
        out_ref[i * rows : (i + 1) * rows, :] = ref[:rows, :]


def pack(rows, messages):
    return pl.pallas_call(
        pack_kernel,
        in_specs=[VMEM] * len(messages),
        out_specs=VMEM,
        out_shape=jax.ShapeDtypeStruct((rows * len(messages), LANES), jnp.bfloat16),
        compiler_params=pltpu.CompilerParams(vmem_limit_bytes=32 * MIB),
    )(*messages)


def stage_kernel(o_hbm, *refs):
    out_ref, sem = refs[-2:]
    copy = pltpu.make_async_copy(o_hbm, out_ref, sem)
    copy.start()
    copy.wait()


def stage(o_weight, after):
    return pl.pallas_call(
        stage_kernel,
        in_specs=[HBM] + [ANY] * len(after),
        out_specs=VMEM,
        out_shape=jax.ShapeDtypeStruct(o_weight.shape, o_weight.dtype),
        scratch_shapes=[pltpu.SemaphoreType.DMA],
        compiler_params=pltpu.CompilerParams(vmem_limit_bytes=32 * MIB),
    )(o_weight, *after)


def prepare(heads, picks, near, far, span, messages, listed_ref, q_ref, free_ref, block_ref, pick_ref):
    per_shard = span // BLOCK
    mine = own_half(near)
    for d in range(heads):
        packed = messages[d][span : span + span // 2, :].astype(jnp.float32)
        top = jnp.where(mine, packed, 0.0)
        bottom = jnp.where(mine, half_turn(packed), 0.0)
        q_ref[d * span : d * span + span // 2, :] = top.astype(q_ref.dtype)
        q_ref[d * span + span // 2 : (d + 1) * span, :] = bottom.astype(q_ref.dtype)
        rand = messages[d][span + span // 2 :, :].astype(jnp.float32)
        for j in range(per_shard):
            row = slice(d * per_shard + j, d * per_shard + j + 1)
            block = (far * heads + (near ^ d)) * per_shard + j
            block_ref[row, :] = jnp.full((1, LANES), block, jnp.int32)
            flags = jnp.broadcast_to(listed_ref[pl.ds(block, 1), :], (BLOCK, BLOCK))
            at = (d * per_shard + j) * BLOCK
            free_ref[at : at + BLOCK, :] = 1.0 - jnp.transpose(flags)
            for r in range(picks):
                at = 2 * (j * picks + r)
                pick = rand[at : at + 1, :] * DIGIT + rand[at + 1 : at + 2, :]
                pick_ref[r, row, :] = pick.astype(jnp.int32)


def fill_bias(heads, groups, near, listed_ref, block_ref, pick_ref, bias_ref):
    per_shard = block_ref.shape[0] // heads
    blocks = block_ref[...]
    picks = [pick_ref[r] for r in range(pick_ref.shape[0])]
    for g, there in enumerate(groups):
        for d in range(heads):
            for b in range(per_shard):
                key_block = (there * heads + (near ^ d)) * per_shard + b
                away = key_block - blocks
                times = listed_ref[pl.ds(key_block, 1), :] + jnp.where((away >= -2) & (away <= 1), 1.0, 0.0)
                for pick in picks:
                    times = times + jnp.where(pick == key_block, 1.0, 0.0)
                at = ((g * heads + d) * per_shard + b) * BLOCK
                bias_ref[:, at : at + BLOCK] = jnp.where(
                    times > 0, jnp.log2(jnp.maximum(times, 1.0)), NEVER
                )


def attend_rows(near, tile, span, q_ref, free_ref, bias_ref, keys, peak, total):
    per_shard = span // BLOCK
    scale = HEAD_DIM ** (-0.5) * math.log2(math.e)
    mine = own_half(near)
    q = q_ref[tile * span : (tile + 1) * span, :]
    scores = [[] for _ in range(per_shard)]
    for key_ref, first, column in keys:
        s = lax.dot_general(
            q,
            key_ref[first : first + span, :],
            (((1,), (1,)), ((), ())),
            preferred_element_type=jnp.float32,
        )
        for j in range(per_shard):
            block = tile * per_shard + j
            free = free_ref[block * BLOCK : (block + 1) * BLOCK, :]
            for b in range(per_shard):
                bias = bias_ref[block : block + 1, column + b * BLOCK : column + (b + 1) * BLOCK]
                part = s[j * BLOCK : (j + 1) * BLOCK, b * BLOCK : (b + 1) * BLOCK]
                scores[j].append(part * scale + free * bias)
    peaks, weights = [], []
    for j in range(per_shard):
        best = jnp.max(functools.reduce(jnp.maximum, scores[j]), axis=1, keepdims=True)
        best = jnp.broadcast_to(best, (BLOCK, LANES))
        if peak is not None:
            best = jnp.maximum(peak[j * BLOCK : (j + 1) * BLOCK, :], best)
        peaks.append(best)
        weights.append([jnp.exp2(part - best).astype(jnp.bfloat16) for part in scores[j]])
    new = jnp.concatenate(peaks, axis=0)
    if total is not None:
        total = total * jnp.exp2(peak - new)
    for i, (key_ref, first, _) in enumerate(keys):
        e = jnp.concatenate(
            [
                jnp.concatenate(weights[j][i * per_shard : (i + 1) * per_shard], axis=1)
                for j in range(per_shard)
            ],
            axis=0,
        )
        v = jnp.where(mine, jnp.ones((), jnp.bfloat16), key_ref[first : first + span, :])
        term = jnp.dot(e, v, preferred_element_type=jnp.float32)
        total = term if total is None else total + term
    return new, total


def finish(heads, parts, near, span, sums, out_ref):
    mine = own_half(near)
    piece = span // parts
    for other in range(heads):
        for part in range(parts):
            first = pl.multiple_of((near ^ other) * span, span) + part * piece
            top = sums[pl.ds(first, piece // 2), :]
            bottom = sums[pl.ds(first + piece // 2, piece // 2), :]
            values = jnp.where(mine, half_turn(top), bottom)
            totals = jnp.where(mine, top, half_turn(bottom))
            out_ref[other * parts + part] = (values / totals).astype(out_ref.dtype)


def open_kernel(heads, picks, near_ref, far_ref, listed_ref, *refs):
    messages, refs = refs[:heads], refs[heads:]
    peaks, sums, q_ref, free_ref, bias_ref, block_ref, pick_ref = refs
    span = q_ref.shape[0] // heads
    near, far = near_ref[0], far_ref[0]
    prepare(heads, picks, near, far, span, messages, listed_ref, q_ref, free_ref, block_ref, pick_ref)
    fill_bias(heads, [far, far ^ 1], near, listed_ref, block_ref, pick_ref, bias_ref)
    keys = [(messages[d], 0, d * span) for d in range(heads)]
    for tile in range(heads):
        rows = slice(tile * span, (tile + 1) * span)
        peaks[rows, :], sums[rows, :] = attend_rows(
            near, tile, span, q_ref, free_ref, bias_ref, keys, None, None
        )


def more_kernel(heads, columns, parts, near_ref, q_ref, free_ref, bias_ref, peak_in, sum_in, *refs):
    kv_refs, refs = refs[: len(columns)], refs[len(columns) :]
    if parts:
        out_ref, sums = refs
        peaks = None
    else:
        peaks, sums = refs
    span = q_ref.shape[0] // heads
    near = near_ref[0]
    keys = [(ref, 0, column) for ref, column in zip(kv_refs, columns)]
    for tile in range(heads):
        rows = slice(tile * span, (tile + 1) * span)
        new, sums[rows, :] = attend_rows(
            near, tile, span, q_ref, free_ref, bias_ref, keys, peak_in[rows, :], sum_in[rows, :]
        )
        if peaks is not None:
            peaks[rows, :] = new
    if parts:
        finish(heads, parts, near, span, sums, out_ref)


def whole_kernel(heads, picks, parts, near_ref, far_ref, listed_ref, kv_ref, *refs):
    messages, refs = refs[:heads], refs[heads:]
    out_ref, peaks, sums, q_ref, free_ref, bias_ref, block_ref, pick_ref = refs
    span = q_ref.shape[0] // heads
    near, far = near_ref[0], far_ref[0]
    step = pl.program_id(0)

    @pl.when(step == 0)
    def _():
        peaks[...] = jnp.full_like(peaks, NEVER)
        sums[...] = jnp.zeros_like(sums)
        prepare(heads, picks, near, far, span, messages, listed_ref, q_ref, free_ref, block_ref, pick_ref)

    fill_bias(heads, [step], near, listed_ref, block_ref, pick_ref, bias_ref)
    keys = [(kv_ref, d * span, d * span) for d in range(heads)]
    for tile in range(heads):
        rows = slice(tile * span, (tile + 1) * span)
        peaks[rows, :], sums[rows, :] = attend_rows(
            near, tile, span, q_ref, free_ref, bias_ref, keys, peaks[rows, :], sums[rows, :]
        )

    @pl.when(step == pl.num_programs(0) - 1)
    def _():
        finish(heads, parts, near, span, sums, out_ref)


def attend_cost(rows, keys):
    return pl.CostEstimate(
        flops=4 * rows * keys * LANES, bytes_accessed=4 * (rows + keys) * LANES, transcendentals=rows * keys
    )


def open_attend(near, far, picks, listed, messages, span):
    heads = len(messages)
    rows = heads * span
    blocks = rows // BLOCK
    state = jax.ShapeDtypeStruct((rows, LANES), jnp.float32)
    return pl.pallas_call(
        functools.partial(open_kernel, heads, picks),
        in_specs=[SMEM, SMEM] + [VMEM] * (1 + heads),
        out_specs=[VMEM] * 5,
        out_shape=[
            state,
            state,
            jax.ShapeDtypeStruct((rows, LANES), jnp.bfloat16),
            state,
            jax.ShapeDtypeStruct((blocks, 2 * rows), jnp.float32),
        ],
        scratch_shapes=[
            pltpu.VMEM((blocks, LANES), jnp.int32),
            pltpu.VMEM((picks, blocks, LANES), jnp.int32),
        ],
        compiler_params=pltpu.CompilerParams(vmem_limit_bytes=24 * MIB),
        cost_estimate=attend_cost(rows, rows),
    )(near, far, listed, *messages)


def more_attend(near, heads, queries, old, kvs, columns, parts):
    rows = queries[0].shape[0]
    span = rows // heads
    state = jax.ShapeDtypeStruct((rows, LANES), jnp.float32)
    if parts:
        out_shape = jax.ShapeDtypeStruct((heads * parts, span // parts // 2, LANES), jnp.bfloat16)
        out_specs, scratch = VMEM, [pltpu.VMEM((rows, LANES), jnp.float32)]
    else:
        out_shape, out_specs, scratch = [state] * 2, [VMEM] * 2, []
    return pl.pallas_call(
        functools.partial(more_kernel, heads, columns, parts),
        in_specs=[SMEM] + [VMEM] * (5 + len(kvs)),
        out_specs=out_specs,
        out_shape=out_shape,
        scratch_shapes=scratch,
        compiler_params=pltpu.CompilerParams(vmem_limit_bytes=24 * MIB),
        cost_estimate=attend_cost(rows, span * len(kvs)),
    )(near, *queries, *old, *kvs)


def whole_attend(near, far, picks, listed, messages, kvs, span, parts):
    heads = len(messages)
    rows = heads * span
    blocks, steps = rows // BLOCK, kvs.shape[0] // rows
    return pl.pallas_call(
        functools.partial(whole_kernel, heads, picks, parts),
        grid=(steps,),
        in_specs=[SMEM, SMEM, VMEM, pl.BlockSpec((rows, LANES), lambda s: (s, 0))] + [VMEM] * heads,
        out_specs=VMEM,
        out_shape=jax.ShapeDtypeStruct((heads * parts, span // parts // 2, LANES), jnp.bfloat16),
        scratch_shapes=[
            pltpu.VMEM((rows, LANES), jnp.float32),
            pltpu.VMEM((rows, LANES), jnp.float32),
            pltpu.VMEM((rows, LANES), jnp.bfloat16),
            pltpu.VMEM((rows, LANES), jnp.float32),
            pltpu.VMEM((blocks, rows), jnp.float32),
            pltpu.VMEM((blocks, LANES), jnp.int32),
            pltpu.VMEM((picks, blocks, LANES), jnp.int32),
        ],
        compiler_params=pltpu.CompilerParams(vmem_limit_bytes=24 * MIB),
        cost_estimate=attend_cost(rows, kvs.shape[0]),
    )(near, far, listed, kvs, *messages)


def mix_kernel(near_count, parts, wide_ref, core_ref, got_ref, *refs):
    o_refs, (keep_ref, send_ref, all_ref) = refs[:parts], refs[parts:]
    low = low_half()
    total = None
    for i in range(parts):
        source = wide_ref[0] ^ i
        columns = []
        for near in range(0, near_count, 2):
            even = got_ref[near * parts + source].astype(jnp.float32)
            odd = got_ref[(near + 1) * parts + source].astype(jnp.float32)
            top = jnp.where(low, even, odd)
            bottom = half_turn(jnp.where(low, odd, even))
            columns.append(jnp.concatenate([top, bottom], axis=0).astype(jnp.bfloat16))
        rows = jnp.concatenate(columns, axis=1)
        term = jnp.dot(rows, o_refs[i][...], preferred_element_type=jnp.float32)
        total = term if total is None else total + term
    half = total.shape[0] // 2
    all_ref[0] = total[:half]
    all_ref[1] = total[half:]
    keep_ref[...] = all_ref[core_ref[0]]
    send_ref[...] = all_ref[core_ref[0] ^ 1]


def mix(wide, core, got, o_blocks):
    parts = len(o_blocks)
    half = jax.ShapeDtypeStruct((got.shape[1], o_blocks[0].shape[1]), jnp.float32)
    return pl.pallas_call(
        functools.partial(mix_kernel, got.shape[0] // parts, parts),
        out_shape=[half] * 2,
        in_specs=[SMEM, SMEM] + [VMEM] * (1 + parts),
        out_specs=[VMEM] * 2,
        scratch_shapes=[pltpu.VMEM((2, *half.shape), half.dtype)],
        compiler_params=pltpu.CompilerParams(vmem_limit_bytes=24 * MIB),
    )(wide, core, got, *o_blocks)


def swapped(block, axis, distance):
    return lax.ppermute(block, axis, [(i, i ^ distance) for i in range(lax.axis_size(axis))])


def shards(tokens, q_weight, k_weight, v_weight, o_weight, rand_blocks, global_pos):
    tok_rows = tokens.shape[0]
    far_count, heads, parts = (lax.axis_size(axis) for axis in ("far", "near", "wide"))
    near, far, wide, core = (
        lax.axis_index(axis).astype(jnp.int32).reshape(1) for axis in ("near", "far", "wide", "core")
    )
    picks = rand_blocks.shape[1]

    own_kv, *sent = project(near, rand_blocks, tokens, q_weight, k_weight, v_weight)
    messages = [sent[0]] + [swapped(sent[d], "near", d) for d in range(1, heads)]

    spots = jnp.arange(far_count * heads * tok_rows, dtype=jnp.int32)
    listed = jnp.any(spots[None, :] == global_pos[:, None], axis=0)
    listed = listed.astype(jnp.float32).reshape(-1, BLOCK)

    if far_count == 2:
        packed = [pack(tok_rows, [message]) for message in messages[1:]]
        apart = [swapped(block, "far", 1) for block in [own_kv] + packed]
        peaks, sums, *queries = open_attend(near, far, picks, listed, messages, tok_rows)
        columns = [(heads + d) * tok_rows for d in range(heads)]
        more = functools.partial(more_attend, near, heads, queries)
        old = more([peaks, sums], apart[:-1], columns[:-1], 0)
        out = more(old, apart[-1:], columns[-1:], parts)
    else:
        packed = [pack(tok_rows, messages)]
        kvs = lax.all_gather(packed[0], "far", tiled=True)
        out = whole_attend(near, far, picks, listed, messages, kvs, tok_rows, parts)

    o_own = stage(o_weight, packed)
    o_blocks = [o_own] + [swapped(o_own, "wide", d) for d in range(1, parts)]
    got = lax.all_to_all(out, ("near", "wide"), 0, 0, tiled=True)
    keep, send = mix(wide, core, got, o_blocks)
    return (keep + swapped(send, "core", 1)).astype(jnp.bfloat16)


def solution(mesh):
    count, columns = mesh.devices.shape
    tm, head = ("far", "near"), ("wide", "core")
    placed = (
        P(tm, None),
        P(None, head),
        P(None, head),
        P(None, head),
        P(head, None),
        P(tm, None),
        P(),
    )

    def run(tokens, q_weight, *rest):
        heads = q_weight.shape[1] // HEAD_DIM // columns
        split = Mesh(
            mesh.devices.reshape(count // heads, heads, columns // CORES, CORES), (*tm, *head)
        )
        body = jax.shard_map(
            shards, mesh=split, in_specs=placed, out_specs=P((*tm, *head), None), check_vma=False
        )
        return body(tokens, q_weight, *rest)

    return run
```

```python
import functools
import math

import jax
import jax.numpy as jnp
from jax import lax
from jax.experimental import pallas as pl
from jax.experimental.pallas import tpu as pltpu
from jax.sharding import Mesh
from jax.sharding import PartitionSpec as P

HEAD_DIM = 64
BLOCK = 128
LANES = 128
DIGIT_BITS = 7
DIGIT = 1 << DIGIT_BITS
TILE_ROWS = 16
NEVER = -1e30
CORES = 2
MIB = 1024 * 1024
VMEM = pl.BlockSpec(memory_space=pltpu.VMEM)
SMEM = pl.BlockSpec(memory_space=pltpu.SMEM)
HBM = pl.BlockSpec(memory_space=pltpu.HBM)
ANY = pl.BlockSpec(memory_space=pl.ANY)


def low_half():
    return lax.broadcasted_iota(jnp.int32, (1, LANES), 1) < HEAD_DIM


def half_turn(block):
    return pltpu.roll(block, HEAD_DIM, 1)


def own_half(near):
    return lax.broadcasted_iota(jnp.int32, (1, LANES), 1) // HEAD_DIM == (near & 1)


def project_kernel(cuts, near_ref, rand_ref, t_hbm, q_hbm, k_hbm, v_hbm, *refs):
    t_ref, q_ref, k_ref, v_ref, all_ref, sems = refs[-6:]
    rows = t_ref.shape[0]
    heads = k_ref.shape[1] // HEAD_DIM
    far_refs, sent_refs = refs[:heads], refs[heads : 2 * heads]
    copies = []
    for i, (source, target) in enumerate(
        ((t_hbm, t_ref), (k_hbm, k_ref), (v_hbm, v_ref), (q_hbm, q_ref))
    ):
        part = source.shape[0] // cuts
        group = []
        for c in range(cuts):
            at = slice(c * part, (c + 1) * part)
            copy = pltpu.make_async_copy(source.at[at, :], target.at[at, :], sems.at[i, c])
            copy.start()
            group.append(copy)
        copies.append(group)

    def product(i, weight_ref):
        for copy in copies[i]:
            copy.wait()
        return jnp.dot(t_ref[...], weight_ref[...], preferred_element_type=jnp.float32)

    for copy in copies[0]:
        copy.wait()
    low = low_half()
    k = product(1, k_ref)
    v = product(2, v_ref)
    for pair in range(heads // 2):
        at = slice(pair * LANES, (pair + 1) * LANES)
        key, value = k[:, at], half_turn(v[:, at])
        all_ref[2 * pair, :rows, :] = jnp.where(low, key, value).astype(jnp.bfloat16)
        all_ref[2 * pair + 1, :rows, :] = jnp.where(low, value, key).astype(jnp.bfloat16)
    q = product(3, q_ref)
    for pair in range(heads // 2):
        at = slice(pair * LANES, (pair + 1) * LANES)
        top, bottom = q[: rows // 2, at], half_turn(q[rows // 2 :, at])
        all_ref[2 * pair, rows:, :] = jnp.where(low, top, bottom).astype(jnp.bfloat16)
        all_ref[2 * pair + 1, rows:, :] = jnp.where(low, bottom, top).astype(jnp.bfloat16)
    near = near_ref[0]
    digit_rows = sent_refs[0].shape[0] - rows - rows // 2
    row = lax.broadcasted_iota(jnp.int32, (digit_rows, LANES), 0)
    digits = jnp.zeros((digit_rows, LANES), jnp.float32)
    picks = rand_ref.shape[1]
    for j in range(rand_ref.shape[0]):
        for r in range(picks):
            at = 2 * (j * picks + r)
            value = rand_ref[j, r]
            digits = jnp.where(row == at, (value >> DIGIT_BITS).astype(jnp.float32), digits)
            digits = jnp.where(row == at + 1, (value & (DIGIT - 1)).astype(jnp.float32), digits)
    digits = digits.astype(jnp.bfloat16)
    for d in range(heads):
        far_refs[d][...] = all_ref[near ^ d, :rows, :]
        sent_refs[d][: rows + rows // 2, :] = all_ref[near ^ d]
        sent_refs[d][rows + rows // 2 :, :] = digits


def project(near, rand_blocks, tokens, q_weight, k_weight, v_weight):
    rows, depth = tokens.shape
    feats = k_weight.shape[1]
    heads = feats // HEAD_DIM
    cuts = 2
    message = rows + rows // 2
    digit_rows = -(-2 * rand_blocks.size // TILE_ROWS) * TILE_ROWS
    pinned = [
        pltpu.with_memory_space_constraint(array, pltpu.HBM)
        for array in (rand_blocks, tokens, q_weight, k_weight, v_weight)
    ]
    return pl.pallas_call(
        functools.partial(project_kernel, cuts),
        in_specs=[SMEM, SMEM, HBM, HBM, HBM, HBM],
        out_specs=[VMEM] * (2 * heads),
        out_shape=[jax.ShapeDtypeStruct((rows, LANES), jnp.bfloat16)] * heads
        + [jax.ShapeDtypeStruct((message + digit_rows, LANES), jnp.bfloat16)] * heads,
        scratch_shapes=[
            pltpu.VMEM((rows, depth), jnp.bfloat16),
            pltpu.VMEM((depth, feats), jnp.bfloat16),
            pltpu.VMEM((depth, feats), jnp.bfloat16),
            pltpu.VMEM((depth, feats), jnp.bfloat16),
            pltpu.VMEM((heads, message, LANES), jnp.bfloat16),
            pltpu.SemaphoreType.DMA((4, cuts)),
        ],
        compiler_params=pltpu.CompilerParams(vmem_limit_bytes=24 * MIB),
        cost_estimate=pl.CostEstimate(
            flops=6 * rows * depth * feats, bytes_accessed=2 * depth * (rows + 3 * feats), transcendentals=0
        ),
    )(near, *pinned)


def pack_kernel(*refs):
    out_ref = refs[-1]
    rows = out_ref.shape[0] // (len(refs) - 1)
    for i, ref in enumerate(refs[:-1]):
        out_ref[i * rows : (i + 1) * rows, :] = ref[:rows, :]


def pack(rows, messages):
    return pl.pallas_call(
        pack_kernel,
        in_specs=[VMEM] * len(messages),
        out_specs=VMEM,
        out_shape=jax.ShapeDtypeStruct((rows * len(messages), LANES), jnp.bfloat16),
        compiler_params=pltpu.CompilerParams(vmem_limit_bytes=32 * MIB),
    )(*messages)


def stage_kernel(o_hbm, *refs):
    out_ref, sem = refs[-2:]
    copy = pltpu.make_async_copy(o_hbm, out_ref, sem)
    copy.start()
    copy.wait()


def stage(o_weight, after):
    return pl.pallas_call(
        stage_kernel,
        in_specs=[HBM] + [ANY] * len(after),
        out_specs=VMEM,
        out_shape=jax.ShapeDtypeStruct(o_weight.shape, o_weight.dtype),
        scratch_shapes=[pltpu.SemaphoreType.DMA],
        compiler_params=pltpu.CompilerParams(vmem_limit_bytes=32 * MIB),
    )(o_weight, *after)


def prepare(heads, picks, near, far, span, messages, listed_ref, q_ref, free_ref, block_ref, pick_ref):
    per_shard = span // BLOCK
    mine = own_half(near)
    for d in range(heads):
        packed = messages[d][span : span + span // 2, :].astype(jnp.float32)
        top = jnp.where(mine, packed, 0.0)
        bottom = jnp.where(mine, half_turn(packed), 0.0)
        q_ref[d * span : d * span + span // 2, :] = top.astype(q_ref.dtype)
        q_ref[d * span + span // 2 : (d + 1) * span, :] = bottom.astype(q_ref.dtype)
        rand = messages[d][span + span // 2 :, :].astype(jnp.float32)
        for j in range(per_shard):
            row = slice(d * per_shard + j, d * per_shard + j + 1)
            block = (far * heads + (near ^ d)) * per_shard + j
            block_ref[row, :] = jnp.full((1, LANES), block, jnp.int32)
            flags = jnp.broadcast_to(listed_ref[pl.ds(block, 1), :], (BLOCK, BLOCK))
            at = (d * per_shard + j) * BLOCK
            free_ref[at : at + BLOCK, :] = 1.0 - jnp.transpose(flags)
            for r in range(picks):
                at = 2 * (j * picks + r)
                pick = rand[at : at + 1, :] * DIGIT + rand[at + 1 : at + 2, :]
                pick_ref[r, row, :] = pick.astype(jnp.int32)


def fill_bias(heads, groups, near, listed_ref, block_ref, pick_ref, bias_ref):
    per_shard = block_ref.shape[0] // heads
    blocks = block_ref[...]
    picks = [pick_ref[r] for r in range(pick_ref.shape[0])]
    for g, there in enumerate(groups):
        for d in range(heads):
            for b in range(per_shard):
                key_block = (there * heads + (near ^ d)) * per_shard + b
                away = key_block - blocks
                times = listed_ref[pl.ds(key_block, 1), :] + jnp.where((away >= -2) & (away <= 1), 1.0, 0.0)
                for pick in picks:
                    times = times + jnp.where(pick == key_block, 1.0, 0.0)
                at = ((g * heads + d) * per_shard + b) * BLOCK
                bias_ref[:, at : at + BLOCK] = jnp.where(
                    times > 0, jnp.log2(jnp.maximum(times, 1.0)), NEVER
                )


def attend_rows(near, tile, span, q_ref, free_ref, bias_ref, keys, peak, total):
    per_shard = span // BLOCK
    scale = HEAD_DIM ** (-0.5) * math.log2(math.e)
    mine = own_half(near)
    q = q_ref[tile * span : (tile + 1) * span, :]
    scores = [[] for _ in range(per_shard)]
    for key_ref, first, column in keys:
        s = lax.dot_general(
            q,
            key_ref[first : first + span, :],
            (((1,), (1,)), ((), ())),
            preferred_element_type=jnp.float32,
        )
        for j in range(per_shard):
            block = tile * per_shard + j
            free = free_ref[block * BLOCK : (block + 1) * BLOCK, :]
            for b in range(per_shard):
                bias = bias_ref[block : block + 1, column + b * BLOCK : column + (b + 1) * BLOCK]
                part = s[j * BLOCK : (j + 1) * BLOCK, b * BLOCK : (b + 1) * BLOCK]
                scores[j].append(part * scale + free * bias)
    peaks, weights = [], []
    for j in range(per_shard):
        best = jnp.max(functools.reduce(jnp.maximum, scores[j]), axis=1, keepdims=True)
        best = jnp.broadcast_to(best, (BLOCK, LANES))
        if peak is not None:
            best = jnp.maximum(peak[j * BLOCK : (j + 1) * BLOCK, :], best)
        peaks.append(best)
        weights.append([jnp.exp2(part - best).astype(jnp.bfloat16) for part in scores[j]])
    new = jnp.concatenate(peaks, axis=0)
    if total is not None:
        total = total * jnp.exp2(peak - new)
    for i, (key_ref, first, _) in enumerate(keys):
        e = jnp.concatenate(
            [
                jnp.concatenate(weights[j][i * per_shard : (i + 1) * per_shard], axis=1)
                for j in range(per_shard)
            ],
            axis=0,
        )
        v = jnp.where(mine, jnp.ones((), jnp.bfloat16), key_ref[first : first + span, :])
        term = jnp.dot(e, v, preferred_element_type=jnp.float32)
        total = term if total is None else total + term
    return new, total


def finish(heads, parts, near, span, sums, out_ref):
    mine = own_half(near)
    piece = span // parts
    for other in range(heads):
        for part in range(parts):
            first = pl.multiple_of((near ^ other) * span, span) + part * piece
            top = sums[pl.ds(first, piece // 2), :]
            bottom = sums[pl.ds(first + piece // 2, piece // 2), :]
            values = jnp.where(mine, half_turn(top), bottom)
            totals = jnp.where(mine, top, half_turn(bottom))
            out_ref[other * parts + part] = (values / totals).astype(out_ref.dtype)


def open_kernel(heads, picks, near_ref, far_ref, listed_ref, *refs):
    messages, refs = refs[:heads], refs[heads:]
    peaks, sums, q_ref, free_ref, bias_ref, block_ref, pick_ref = refs
    span = q_ref.shape[0] // heads
    near, far = near_ref[0], far_ref[0]
    prepare(heads, picks, near, far, span, messages, listed_ref, q_ref, free_ref, block_ref, pick_ref)
    fill_bias(heads, [far, far ^ 1], near, listed_ref, block_ref, pick_ref, bias_ref)
    keys = [(messages[d], 0, d * span) for d in range(heads)]
    for tile in range(heads):
        rows = slice(tile * span, (tile + 1) * span)
        peaks[rows, :], sums[rows, :] = attend_rows(
            near, tile, span, q_ref, free_ref, bias_ref, keys, None, None
        )


def more_kernel(heads, columns, parts, near_ref, q_ref, free_ref, bias_ref, peak_in, sum_in, *refs):
    kv_refs, refs = refs[: len(columns)], refs[len(columns) :]
    if parts:
        out_ref, sums = refs
        peaks = None
    else:
        peaks, sums = refs
    span = q_ref.shape[0] // heads
    near = near_ref[0]
    keys = [(ref, 0, column) for ref, column in zip(kv_refs, columns)]
    for tile in range(heads):
        rows = slice(tile * span, (tile + 1) * span)
        new, sums[rows, :] = attend_rows(
            near, tile, span, q_ref, free_ref, bias_ref, keys, peak_in[rows, :], sum_in[rows, :]
        )
        if peaks is not None:
            peaks[rows, :] = new
    if parts:
        finish(heads, parts, near, span, sums, out_ref)


def whole_kernel(heads, picks, parts, near_ref, far_ref, listed_ref, kv_ref, *refs):
    messages, refs = refs[:heads], refs[heads:]
    out_ref, peaks, sums, q_ref, free_ref, bias_ref, block_ref, pick_ref = refs
    span = q_ref.shape[0] // heads
    near, far = near_ref[0], far_ref[0]
    step = pl.program_id(0)

    @pl.when(step == 0)
    def _():
        peaks[...] = jnp.full_like(peaks, NEVER)
        sums[...] = jnp.zeros_like(sums)
        prepare(heads, picks, near, far, span, messages, listed_ref, q_ref, free_ref, block_ref, pick_ref)

    fill_bias(heads, [step], near, listed_ref, block_ref, pick_ref, bias_ref)
    keys = [(kv_ref, d * span, d * span) for d in range(heads)]
    for tile in range(heads):
        rows = slice(tile * span, (tile + 1) * span)
        peaks[rows, :], sums[rows, :] = attend_rows(
            near, tile, span, q_ref, free_ref, bias_ref, keys, peaks[rows, :], sums[rows, :]
        )

    @pl.when(step == pl.num_programs(0) - 1)
    def _():
        finish(heads, parts, near, span, sums, out_ref)


def attend_cost(rows, keys):
    return pl.CostEstimate(
        flops=4 * rows * keys * LANES, bytes_accessed=4 * (rows + keys) * LANES, transcendentals=rows * keys
    )


def open_attend(near, far, picks, listed, messages, span):
    heads = len(messages)
    rows = heads * span
    blocks = rows // BLOCK
    state = jax.ShapeDtypeStruct((rows, LANES), jnp.float32)
    return pl.pallas_call(
        functools.partial(open_kernel, heads, picks),
        in_specs=[SMEM, SMEM] + [VMEM] * (1 + heads),
        out_specs=[VMEM] * 5,
        out_shape=[
            state,
            state,
            jax.ShapeDtypeStruct((rows, LANES), jnp.bfloat16),
            state,
            jax.ShapeDtypeStruct((blocks, 2 * rows), jnp.float32),
        ],
        scratch_shapes=[
            pltpu.VMEM((blocks, LANES), jnp.int32),
            pltpu.VMEM((picks, blocks, LANES), jnp.int32),
        ],
        compiler_params=pltpu.CompilerParams(vmem_limit_bytes=24 * MIB),
        cost_estimate=attend_cost(rows, rows),
    )(near, far, listed, *messages)


def more_attend(near, heads, queries, old, kvs, columns, parts):
    rows = queries[0].shape[0]
    span = rows // heads
    state = jax.ShapeDtypeStruct((rows, LANES), jnp.float32)
    if parts:
        out_shape = jax.ShapeDtypeStruct((heads * parts, span // parts // 2, LANES), jnp.bfloat16)
        out_specs, scratch = VMEM, [pltpu.VMEM((rows, LANES), jnp.float32)]
    else:
        out_shape, out_specs, scratch = [state] * 2, [VMEM] * 2, []
    return pl.pallas_call(
        functools.partial(more_kernel, heads, columns, parts),
        in_specs=[SMEM] + [VMEM] * (5 + len(kvs)),
        out_specs=out_specs,
        out_shape=out_shape,
        scratch_shapes=scratch,
        compiler_params=pltpu.CompilerParams(vmem_limit_bytes=24 * MIB),
        cost_estimate=attend_cost(rows, span * len(kvs)),
    )(near, *queries, *old, *kvs)


def whole_attend(near, far, picks, listed, messages, kvs, span, parts):
    heads = len(messages)
    rows = heads * span
    blocks, steps = rows // BLOCK, kvs.shape[0] // rows
    return pl.pallas_call(
        functools.partial(whole_kernel, heads, picks, parts),
        grid=(steps,),
        in_specs=[SMEM, SMEM, VMEM, pl.BlockSpec((rows, LANES), lambda s: (s, 0))] + [VMEM] * heads,
        out_specs=VMEM,
        out_shape=jax.ShapeDtypeStruct((heads * parts, span // parts // 2, LANES), jnp.bfloat16),
        scratch_shapes=[
            pltpu.VMEM((rows, LANES), jnp.float32),
            pltpu.VMEM((rows, LANES), jnp.float32),
            pltpu.VMEM((rows, LANES), jnp.bfloat16),
            pltpu.VMEM((rows, LANES), jnp.float32),
            pltpu.VMEM((blocks, rows), jnp.float32),
            pltpu.VMEM((blocks, LANES), jnp.int32),
            pltpu.VMEM((picks, blocks, LANES), jnp.int32),
        ],
        compiler_params=pltpu.CompilerParams(vmem_limit_bytes=24 * MIB),
        cost_estimate=attend_cost(rows, kvs.shape[0]),
    )(near, far, listed, kvs, *messages)


def pick_kernel(parts, wide_ref, got_ref, *out_refs):
    for d, out_ref in enumerate(out_refs, 1):
        for near in range(out_ref.shape[0]):
            out_ref[near] = got_ref[near * parts + (wide_ref[0] ^ d)]


def pick(wide, got, parts):
    shape = jax.ShapeDtypeStruct((got.shape[0] // parts, *got.shape[1:]), got.dtype)
    return pl.pallas_call(
        functools.partial(pick_kernel, parts),
        in_specs=[SMEM, VMEM],
        out_specs=[VMEM] * (parts - 1),
        out_shape=[shape] * (parts - 1),
        compiler_params=pltpu.CompilerParams(vmem_limit_bytes=24 * MIB),
    )(wide, got)


def mix_kernel(near_count, parts, wide_ref, core_ref, got_ref, *refs):
    apart_refs, o_refs, (keep_ref, send_ref, all_ref) = (
        refs[: parts - 1],
        refs[parts - 1 : 2 * parts - 1],
        refs[2 * parts - 1 :],
    )
    low = low_half()
    total = None
    for i in range(parts):
        columns = []
        for near in range(0, near_count, 2):
            if i == 0:
                even, odd = (got_ref[at * parts + wide_ref[0]] for at in (near, near + 1))
            else:
                even, odd = (apart_refs[i - 1][at] for at in (near, near + 1))
            even, odd = even.astype(jnp.float32), odd.astype(jnp.float32)
            top = jnp.where(low, even, odd)
            bottom = half_turn(jnp.where(low, odd, even))
            columns.append(jnp.concatenate([top, bottom], axis=0).astype(jnp.bfloat16))
        rows = jnp.concatenate(columns, axis=1)
        term = jnp.dot(rows, o_refs[i][...], preferred_element_type=jnp.float32)
        total = term if total is None else total + term
    half = total.shape[0] // 2
    all_ref[0] = total[:half]
    all_ref[1] = total[half:]
    keep_ref[...] = all_ref[core_ref[0]]
    send_ref[...] = all_ref[core_ref[0] ^ 1]


def mix(wide, core, got, apart, o_blocks):
    parts = len(o_blocks)
    half = jax.ShapeDtypeStruct((got.shape[1], o_blocks[0].shape[1]), jnp.float32)
    return pl.pallas_call(
        functools.partial(mix_kernel, got.shape[0] // parts, parts),
        out_shape=[half] * 2,
        in_specs=[SMEM, SMEM] + [VMEM] * (2 * parts),
        out_specs=[VMEM] * 2,
        scratch_shapes=[pltpu.VMEM((2, *half.shape), half.dtype)],
        compiler_params=pltpu.CompilerParams(vmem_limit_bytes=24 * MIB),
    )(wide, core, got, *apart, *o_blocks)


def swapped(block, axis, distance):
    return lax.ppermute(block, axis, [(i, i ^ distance) for i in range(lax.axis_size(axis))])


def shards(tokens, q_weight, k_weight, v_weight, o_weight, rand_blocks, global_pos):
    tok_rows = tokens.shape[0]
    far_count, heads, parts = (lax.axis_size(axis) for axis in ("far", "near", "wide"))
    near, far, wide, core = (
        lax.axis_index(axis).astype(jnp.int32).reshape(1) for axis in ("near", "far", "wide", "core")
    )
    picks = rand_blocks.shape[1]

    ready = project(near, rand_blocks, tokens, q_weight, k_weight, v_weight)
    leaving, sent = ready[:heads], ready[heads:]
    messages = [sent[0]] + [swapped(sent[d], "near", d) for d in range(1, heads)]

    spots = jnp.arange(far_count * heads * tok_rows, dtype=jnp.int32)
    listed = jnp.any(spots[None, :] == global_pos[:, None], axis=0)
    listed = listed.astype(jnp.float32).reshape(-1, BLOCK)

    if far_count == 2:
        apart = [swapped(leaving[d], ("far", "near"), heads + d) for d in range(heads)]
        peaks, sums, *queries = open_attend(near, far, picks, listed, messages, tok_rows)
        columns = [(heads + d) * tok_rows for d in range(heads)]
        more = functools.partial(more_attend, near, heads, queries)
        old = more([peaks, sums], apart[:-1], columns[:-1], 0)
        out = more(old, apart[-1:], columns[-1:], parts)
    else:
        kvs = lax.all_gather(pack(tok_rows, messages), "far", tiled=True)
        out = whole_attend(near, far, picks, listed, messages, kvs, tok_rows, parts)

    o_own = stage(o_weight, messages[1:])
    o_blocks = [o_own] + [swapped(o_own, "wide", d) for d in range(1, parts)]
    got = lax.all_to_all(out, "near", 0, 0, tiled=True)
    apart = [swapped(part, "wide", d) for d, part in enumerate(pick(wide, got, parts), 1)]
    keep, send = mix(wide, core, got, apart, o_blocks)
    return (keep + swapped(send, "core", 1)).astype(jnp.bfloat16)


def solution(mesh):
    count, columns = mesh.devices.shape
    tm, head = ("far", "near"), ("wide", "core")
    placed = (
        P(tm, None),
        P(None, head),
        P(None, head),
        P(None, head),
        P(head, None),
        P(tm, None),
        P(),
    )

    def run(tokens, q_weight, *rest):
        heads = q_weight.shape[1] // HEAD_DIM // columns
        split = Mesh(
            mesh.devices.reshape(count // heads, heads, columns // CORES, CORES), (*tm, *head)
        )
        body = jax.shard_map(
            shards, mesh=split, in_specs=placed, out_specs=P((*tm, *head), None), check_vma=False
        )
        return body(tokens, q_weight, *rest)

    return run
```

```python
import functools
import math

import jax
import jax.numpy as jnp
from jax import lax
from jax.experimental import pallas as pl
from jax.experimental.pallas import tpu as pltpu
from jax.sharding import Mesh
from jax.sharding import PartitionSpec as P

HEAD_DIM = 64
BLOCK = 128
LANES = 128
DIGIT_BITS = 7
DIGIT = 1 << DIGIT_BITS
TILE_ROWS = 16
NEVER = -1e30
CORES = 2
MIB = 1024 * 1024
VMEM = pl.BlockSpec(memory_space=pltpu.VMEM)
SMEM = pl.BlockSpec(memory_space=pltpu.SMEM)
HBM = pl.BlockSpec(memory_space=pltpu.HBM)


def low_half():
    return lax.broadcasted_iota(jnp.int32, (1, LANES), 1) < HEAD_DIM


def half_turn(block):
    return pltpu.roll(block, HEAD_DIM, 1)


def own_half(near):
    return lax.broadcasted_iota(jnp.int32, (1, LANES), 1) // HEAD_DIM == (near & 1)


def project_kernel(cuts, near_ref, rand_ref, pos_ref, t_hbm, q_hbm, k_hbm, v_hbm, *refs):
    listed_ref, t_ref, q_ref, k_ref, v_ref, all_ref, sems = refs[-7:]
    rows = t_ref.shape[0]
    heads = k_ref.shape[1] // HEAD_DIM
    far_refs, sent_refs = refs[:heads], refs[heads : 2 * heads]
    copies = []
    for i, (source, target) in enumerate(
        ((t_hbm, t_ref), (k_hbm, k_ref), (v_hbm, v_ref), (q_hbm, q_ref))
    ):
        part = source.shape[0] // cuts
        group = []
        for c in range(cuts):
            at = slice(c * part, (c + 1) * part)
            copy = pltpu.make_async_copy(source.at[at, :], target.at[at, :], sems.at[i, c])
            copy.start()
            group.append(copy)
        copies.append(group)

    spots = lax.broadcasted_iota(jnp.int32, listed_ref.shape, 0) * BLOCK
    spots = spots + lax.broadcasted_iota(jnp.int32, listed_ref.shape, 1)
    listed_ref[...] = lax.fori_loop(
        0,
        pos_ref.shape[0],
        lambda i, flags: jnp.where(spots == pos_ref[i], 1.0, flags),
        jnp.zeros(listed_ref.shape, jnp.float32),
        unroll=16,
    )

    def product(i, weight_ref):
        for copy in copies[i]:
            copy.wait()
        return jnp.dot(t_ref[...], weight_ref[...], preferred_element_type=jnp.float32)

    for copy in copies[0]:
        copy.wait()
    low = low_half()
    k = product(1, k_ref)
    v = product(2, v_ref)
    for pair in range(heads // 2):
        at = slice(pair * LANES, (pair + 1) * LANES)
        key, value = k[:, at], half_turn(v[:, at])
        all_ref[2 * pair, :rows, :] = jnp.where(low, key, value).astype(jnp.bfloat16)
        all_ref[2 * pair + 1, :rows, :] = jnp.where(low, value, key).astype(jnp.bfloat16)
    q = product(3, q_ref)
    for pair in range(heads // 2):
        at = slice(pair * LANES, (pair + 1) * LANES)
        top, bottom = q[: rows // 2, at], half_turn(q[rows // 2 :, at])
        all_ref[2 * pair, rows:, :] = jnp.where(low, top, bottom).astype(jnp.bfloat16)
        all_ref[2 * pair + 1, rows:, :] = jnp.where(low, bottom, top).astype(jnp.bfloat16)
    near = near_ref[0]
    digit_rows = sent_refs[0].shape[0] - rows - rows // 2
    row = lax.broadcasted_iota(jnp.int32, (digit_rows, LANES), 0)
    digits = jnp.zeros((digit_rows, LANES), jnp.float32)
    picks = rand_ref.shape[1]
    for j in range(rand_ref.shape[0]):
        for r in range(picks):
            at = 2 * (j * picks + r)
            value = rand_ref[j, r]
            digits = jnp.where(row == at, (value >> DIGIT_BITS).astype(jnp.float32), digits)
            digits = jnp.where(row == at + 1, (value & (DIGIT - 1)).astype(jnp.float32), digits)
    digits = digits.astype(jnp.bfloat16)
    for d in range(heads):
        far_refs[d][...] = all_ref[near ^ d, :rows, :]
        sent_refs[d][: rows + rows // 2, :] = all_ref[near ^ d]
        sent_refs[d][rows + rows // 2 :, :] = digits


def project(near, blocks, global_pos, rand_blocks, tokens, q_weight, k_weight, v_weight):
    rows, depth = tokens.shape
    feats = k_weight.shape[1]
    heads = feats // HEAD_DIM
    cuts = 2
    message = rows + rows // 2
    digit_rows = -(-2 * rand_blocks.size // TILE_ROWS) * TILE_ROWS
    pinned = [
        pltpu.with_memory_space_constraint(array, pltpu.HBM)
        for array in (rand_blocks, global_pos, tokens, q_weight, k_weight, v_weight)
    ]
    return pl.pallas_call(
        functools.partial(project_kernel, cuts),
        in_specs=[SMEM, SMEM, SMEM, HBM, HBM, HBM, HBM],
        out_specs=[VMEM] * (2 * heads + 1),
        out_shape=[jax.ShapeDtypeStruct((rows, LANES), jnp.bfloat16)] * heads
        + [jax.ShapeDtypeStruct((message + digit_rows, LANES), jnp.bfloat16)] * heads
        + [jax.ShapeDtypeStruct((blocks, LANES), jnp.float32)],
        scratch_shapes=[
            pltpu.VMEM((rows, depth), jnp.bfloat16),
            pltpu.VMEM((depth, feats), jnp.bfloat16),
            pltpu.VMEM((depth, feats), jnp.bfloat16),
            pltpu.VMEM((depth, feats), jnp.bfloat16),
            pltpu.VMEM((heads, message, LANES), jnp.bfloat16),
            pltpu.SemaphoreType.DMA((4, cuts)),
        ],
        compiler_params=pltpu.CompilerParams(vmem_limit_bytes=24 * MIB),
        cost_estimate=pl.CostEstimate(
            flops=6 * rows * depth * feats, bytes_accessed=2 * depth * (rows + 3 * feats), transcendentals=0
        ),
    )(near, *pinned)


def pack_kernel(*refs):
    out_ref = refs[-1]
    rows = out_ref.shape[0] // (len(refs) - 1)
    for i, ref in enumerate(refs[:-1]):
        out_ref[i * rows : (i + 1) * rows, :] = ref[:rows, :]


def pack(rows, messages):
    return pl.pallas_call(
        pack_kernel,
        in_specs=[VMEM] * len(messages),
        out_specs=VMEM,
        out_shape=jax.ShapeDtypeStruct((rows * len(messages), LANES), jnp.bfloat16),
        compiler_params=pltpu.CompilerParams(vmem_limit_bytes=32 * MIB),
    )(*messages)


def prepare(heads, picks, near, far, span, messages, listed_ref, q_ref, free_ref, block_ref, pick_ref):
    per_shard = span // BLOCK
    mine = own_half(near)
    for d in range(heads):
        packed = messages[d][span : span + span // 2, :].astype(jnp.float32)
        top = jnp.where(mine, packed, 0.0)
        bottom = jnp.where(mine, half_turn(packed), 0.0)
        q_ref[d * span : d * span + span // 2, :] = top.astype(q_ref.dtype)
        q_ref[d * span + span // 2 : (d + 1) * span, :] = bottom.astype(q_ref.dtype)
        rand = messages[d][span + span // 2 :, :].astype(jnp.float32)
        for j in range(per_shard):
            row = slice(d * per_shard + j, d * per_shard + j + 1)
            block = (far * heads + (near ^ d)) * per_shard + j
            block_ref[row, :] = jnp.full((1, LANES), block, jnp.int32)
            flags = jnp.broadcast_to(listed_ref[pl.ds(block, 1), :], (BLOCK, BLOCK))
            at = (d * per_shard + j) * BLOCK
            free_ref[at : at + BLOCK, :] = 1.0 - jnp.transpose(flags)
            for r in range(picks):
                at = 2 * (j * picks + r)
                pick = rand[at : at + 1, :] * DIGIT + rand[at + 1 : at + 2, :]
                pick_ref[r, row, :] = pick.astype(jnp.int32)


def fill_bias(heads, groups, near, listed_ref, block_ref, pick_ref, bias_ref):
    per_shard = block_ref.shape[0] // heads
    blocks = block_ref[...]
    picks = [pick_ref[r] for r in range(pick_ref.shape[0])]
    for g, there in enumerate(groups):
        for d in range(heads):
            for b in range(per_shard):
                key_block = (there * heads + (near ^ d)) * per_shard + b
                away = key_block - blocks
                times = listed_ref[pl.ds(key_block, 1), :] + jnp.where((away >= -2) & (away <= 1), 1.0, 0.0)
                for pick in picks:
                    times = times + jnp.where(pick == key_block, 1.0, 0.0)
                at = ((g * heads + d) * per_shard + b) * BLOCK
                bias_ref[:, at : at + BLOCK] = jnp.where(
                    times > 0, jnp.log2(jnp.maximum(times, 1.0)), NEVER
                )


def attend_rows(near, tile, span, q_ref, free_ref, bias_ref, keys, peak, total):
    per_shard = span // BLOCK
    scale = HEAD_DIM ** (-0.5) * math.log2(math.e)
    mine = own_half(near)
    q = q_ref[tile * span : (tile + 1) * span, :]
    scores = [[] for _ in range(per_shard)]
    for key_ref, first, column in keys:
        s = lax.dot_general(
            q,
            key_ref[first : first + span, :],
            (((1,), (1,)), ((), ())),
            preferred_element_type=jnp.float32,
        )
        for j in range(per_shard):
            block = tile * per_shard + j
            free = free_ref[block * BLOCK : (block + 1) * BLOCK, :]
            for b in range(per_shard):
                bias = bias_ref[block : block + 1, column + b * BLOCK : column + (b + 1) * BLOCK]
                part = s[j * BLOCK : (j + 1) * BLOCK, b * BLOCK : (b + 1) * BLOCK]
                scores[j].append(part * scale + free * bias)
    peaks, weights = [], []
    for j in range(per_shard):
        best = jnp.max(functools.reduce(jnp.maximum, scores[j]), axis=1, keepdims=True)
        best = jnp.broadcast_to(best, (BLOCK, LANES))
        if peak is not None:
            best = jnp.maximum(peak[j * BLOCK : (j + 1) * BLOCK, :], best)
        peaks.append(best)
        weights.append([jnp.exp2(part - best).astype(jnp.bfloat16) for part in scores[j]])
    new = jnp.concatenate(peaks, axis=0)
    if total is not None:
        total = total * jnp.exp2(peak - new)
    for i, (key_ref, first, _) in enumerate(keys):
        e = jnp.concatenate(
            [
                jnp.concatenate(weights[j][i * per_shard : (i + 1) * per_shard], axis=1)
                for j in range(per_shard)
            ],
            axis=0,
        )
        v = jnp.where(mine, jnp.ones((), jnp.bfloat16), key_ref[first : first + span, :])
        term = jnp.dot(e, v, preferred_element_type=jnp.float32)
        total = term if total is None else total + term
    return new, total


def finish(parts, near, span, sums, out_refs):
    mine = own_half(near)
    piece = span // parts
    for d, out_ref in enumerate(out_refs):
        for part in range(parts):
            first = d * span + part * piece
            top = sums[first : first + piece // 2, :]
            bottom = sums[first + piece // 2 : first + piece, :]
            values = jnp.where(mine, half_turn(top), bottom)
            totals = jnp.where(mine, top, half_turn(bottom))
            out_ref[part] = (values / totals).astype(out_ref.dtype)


def open_kernel(heads, picks, near_ref, far_ref, listed_ref, *refs):
    messages, refs = refs[:heads], refs[heads:]
    peaks, sums, q_ref, free_ref, bias_ref, block_ref, pick_ref = refs
    span = q_ref.shape[0] // heads
    near, far = near_ref[0], far_ref[0]
    prepare(heads, picks, near, far, span, messages, listed_ref, q_ref, free_ref, block_ref, pick_ref)
    fill_bias(heads, [far, far ^ 1], near, listed_ref, block_ref, pick_ref, bias_ref)
    keys = [(messages[d], 0, d * span) for d in range(heads)]
    for tile in range(heads):
        rows = slice(tile * span, (tile + 1) * span)
        peaks[rows, :], sums[rows, :] = attend_rows(
            near, tile, span, q_ref, free_ref, bias_ref, keys, None, None
        )


def more_kernel(heads, columns, parts, near_ref, q_ref, free_ref, bias_ref, peak_in, sum_in, *refs):
    kv_refs, out_refs, (sums,) = refs[: len(columns)], refs[len(columns) : -1], refs[-1:]
    span = q_ref.shape[0] // heads
    near = near_ref[0]
    keys = [(ref, 0, column) for ref, column in zip(kv_refs, columns)]
    for tile in range(heads):
        rows = slice(tile * span, (tile + 1) * span)
        _, sums[rows, :] = attend_rows(
            near, tile, span, q_ref, free_ref, bias_ref, keys, peak_in[rows, :], sum_in[rows, :]
        )
    finish(parts, near, span, sums, out_refs)


def whole_kernel(heads, picks, parts, near_ref, far_ref, listed_ref, kv_ref, *refs):
    messages, refs = refs[:heads], refs[heads:]
    out_refs, refs = refs[:heads], refs[heads:]
    peaks, sums, q_ref, free_ref, bias_ref, block_ref, pick_ref = refs
    span = q_ref.shape[0] // heads
    near, far = near_ref[0], far_ref[0]
    step = pl.program_id(0)

    @pl.when(step == 0)
    def _():
        peaks[...] = jnp.full_like(peaks, NEVER)
        sums[...] = jnp.zeros_like(sums)
        prepare(heads, picks, near, far, span, messages, listed_ref, q_ref, free_ref, block_ref, pick_ref)

    fill_bias(heads, [step], near, listed_ref, block_ref, pick_ref, bias_ref)
    keys = [(kv_ref, d * span, d * span) for d in range(heads)]
    for tile in range(heads):
        rows = slice(tile * span, (tile + 1) * span)
        peaks[rows, :], sums[rows, :] = attend_rows(
            near, tile, span, q_ref, free_ref, bias_ref, keys, peaks[rows, :], sums[rows, :]
        )

    @pl.when(step == pl.num_programs(0) - 1)
    def _():
        finish(parts, near, span, sums, out_refs)


def attend_cost(rows, keys):
    return pl.CostEstimate(
        flops=4 * rows * keys * LANES, bytes_accessed=4 * (rows + keys) * LANES, transcendentals=rows * keys
    )


def open_attend(near, far, picks, listed, messages, span):
    heads = len(messages)
    rows = heads * span
    blocks = rows // BLOCK
    state = jax.ShapeDtypeStruct((rows, LANES), jnp.float32)
    return pl.pallas_call(
        functools.partial(open_kernel, heads, picks),
        in_specs=[SMEM, SMEM] + [VMEM] * (1 + heads),
        out_specs=[VMEM] * 5,
        out_shape=[
            state,
            state,
            jax.ShapeDtypeStruct((rows, LANES), jnp.bfloat16),
            state,
            jax.ShapeDtypeStruct((blocks, 2 * rows), jnp.float32),
        ],
        scratch_shapes=[
            pltpu.VMEM((blocks, LANES), jnp.int32),
            pltpu.VMEM((picks, blocks, LANES), jnp.int32),
        ],
        compiler_params=pltpu.CompilerParams(vmem_limit_bytes=24 * MIB),
        cost_estimate=attend_cost(rows, rows),
    )(near, far, listed, *messages)


def piece_shapes(heads, parts, span):
    return [jax.ShapeDtypeStruct((parts, span // parts // 2, LANES), jnp.bfloat16)] * heads


def more_attend(near, heads, queries, old, kvs, columns, parts):
    rows = queries[0].shape[0]
    span = rows // heads
    return pl.pallas_call(
        functools.partial(more_kernel, heads, columns, parts),
        in_specs=[SMEM] + [VMEM] * (5 + len(kvs)),
        out_specs=[VMEM] * heads,
        out_shape=piece_shapes(heads, parts, span),
        scratch_shapes=[pltpu.VMEM((rows, LANES), jnp.float32)],
        compiler_params=pltpu.CompilerParams(vmem_limit_bytes=24 * MIB),
        cost_estimate=attend_cost(rows, span * len(kvs)),
    )(near, *queries, *old, *kvs)


def whole_attend(near, far, picks, listed, messages, kvs, span, parts):
    heads = len(messages)
    rows = heads * span
    blocks, steps = rows // BLOCK, kvs.shape[0] // rows
    return pl.pallas_call(
        functools.partial(whole_kernel, heads, picks, parts),
        grid=(steps,),
        in_specs=[SMEM, SMEM, VMEM, pl.BlockSpec((rows, LANES), lambda s: (s, 0))] + [VMEM] * heads,
        out_specs=[VMEM] * heads,
        out_shape=piece_shapes(heads, parts, span),
        scratch_shapes=[
            pltpu.VMEM((rows, LANES), jnp.float32),
            pltpu.VMEM((rows, LANES), jnp.float32),
            pltpu.VMEM((rows, LANES), jnp.bfloat16),
            pltpu.VMEM((rows, LANES), jnp.float32),
            pltpu.VMEM((blocks, rows), jnp.float32),
            pltpu.VMEM((blocks, LANES), jnp.int32),
            pltpu.VMEM((picks, blocks, LANES), jnp.int32),
        ],
        compiler_params=pltpu.CompilerParams(vmem_limit_bytes=24 * MIB),
        cost_estimate=attend_cost(rows, kvs.shape[0]),
    )(near, far, listed, kvs, *messages)


def pick_kernel(heads, near_ref, wide_ref, *refs):
    for part, out_ref in enumerate(refs[heads:]):
        for d in range(heads):
            out_ref[near_ref[0] ^ d] = refs[d][wide_ref[0] ^ part]


def pick(near, wide, pieces):
    heads, parts = len(pieces), pieces[0].shape[0]
    shape = jax.ShapeDtypeStruct((heads, *pieces[0].shape[1:]), pieces[0].dtype)
    return pl.pallas_call(
        functools.partial(pick_kernel, heads),
        in_specs=[SMEM, SMEM] + [VMEM] * heads,
        out_specs=[VMEM] * parts,
        out_shape=[shape] * parts,
        compiler_params=pltpu.CompilerParams(vmem_limit_bytes=24 * MIB),
    )(near, wide, *pieces)


def mix_kernel(parts, core_ref, *refs):
    low = low_half()
    total = None
    for i in range(parts):
        got_ref, o_ref = refs[i], refs[parts + i]
        columns = []
        for near in range(0, got_ref.shape[0], 2):
            even, odd = got_ref[near].astype(jnp.float32), got_ref[near + 1].astype(jnp.float32)
            top = jnp.where(low, even, odd)
            bottom = half_turn(jnp.where(low, odd, even))
            columns.append(jnp.concatenate([top, bottom], axis=0).astype(jnp.bfloat16))
        rows = jnp.concatenate(columns, axis=1)
        term = jnp.dot(rows, o_ref[...], preferred_element_type=jnp.float32)
        total = term if total is None else total + term
    keep_ref, send_ref, all_ref = refs[2 * parts :]
    half = total.shape[0] // 2
    all_ref[0] = total[:half]
    all_ref[1] = total[half:]
    keep_ref[...] = all_ref[core_ref[0]]
    send_ref[...] = all_ref[core_ref[0] ^ 1]


def mix(core, got, o_blocks):
    parts = len(o_blocks)
    half = jax.ShapeDtypeStruct((got[0].shape[1], o_blocks[0].shape[1]), jnp.float32)
    return pl.pallas_call(
        functools.partial(mix_kernel, parts),
        out_shape=[half] * 2,
        in_specs=[SMEM] + [VMEM] * (2 * parts),
        out_specs=[VMEM] * 2,
        scratch_shapes=[pltpu.VMEM((2, *half.shape), half.dtype)],
        compiler_params=pltpu.CompilerParams(vmem_limit_bytes=24 * MIB),
    )(core, *got, *o_blocks)


def swapped(block, axis, distance):
    return lax.ppermute(block, axis, [(i, i ^ distance) for i in range(lax.axis_size(axis))])


def shards(tokens, q_weight, k_weight, v_weight, o_weight, rand_blocks, global_pos):
    tok_rows = tokens.shape[0]
    far_count, heads, parts = (lax.axis_size(axis) for axis in ("far", "near", "wide"))
    near, far, wide, core = (
        lax.axis_index(axis).astype(jnp.int32).reshape(1) for axis in ("near", "far", "wide", "core")
    )
    picks = rand_blocks.shape[1]

    blocks = far_count * heads * tok_rows // BLOCK
    *ready, listed = project(
        near, blocks, global_pos, rand_blocks, tokens, q_weight, k_weight, v_weight
    )
    leaving, sent = ready[:heads], ready[heads:]
    messages = [sent[0]] + [swapped(sent[d], "near", d) for d in range(1, heads)]

    if far_count == 2:
        apart = [swapped(leaving[d], ("far", "near"), heads + d) for d in range(heads)]
        peaks, sums, *queries = open_attend(near, far, picks, listed, messages, tok_rows)
        columns = [(heads + d) * tok_rows for d in range(heads)]
        pieces = more_attend(near, heads, queries, [peaks, sums], apart, columns, parts)
    else:
        kvs = lax.all_gather(pack(tok_rows, messages), "far", tiled=True)
        pieces = whole_attend(near, far, picks, listed, messages, kvs, tok_rows, parts)

    o_blocks = [o_weight] + [swapped(o_weight, "wide", d) for d in range(1, parts)]
    pieces = [pieces[0]] + [swapped(pieces[d], "near", d) for d in range(1, heads)]
    mine, *theirs = pick(near, wide, pieces)
    theirs = [swapped(block, "wide", d) for d, block in enumerate(theirs, 1)]
    keep, send = mix(core, [mine] + theirs, o_blocks)
    return (keep + swapped(send, "core", 1)).astype(jnp.bfloat16)


def solution(mesh):
    count, columns = mesh.devices.shape
    tm, head = ("far", "near"), ("wide", "core")
    placed = (
        P(tm, None),
        P(None, head),
        P(None, head),
        P(None, head),
        P(head, None),
        P(tm, None),
        P(),
    )

    def run(tokens, q_weight, *rest):
        heads = q_weight.shape[1] // HEAD_DIM // columns
        split = Mesh(
            mesh.devices.reshape(count // heads, heads, columns // CORES, CORES), (*tm, *head)
        )
        body = jax.shard_map(
            shards, mesh=split, in_specs=placed, out_specs=P((*tm, *head), None), check_vma=False
        )
        return body(tokens, q_weight, *rest)

    return run
```

```python
import functools
import math

import jax
import jax.numpy as jnp
from jax import lax
from jax.experimental import pallas as pl
from jax.experimental.pallas import tpu as pltpu
from jax.sharding import Mesh
from jax.sharding import PartitionSpec as P

HEAD_DIM = 64
BLOCK = 128
LANES = 128
DIGIT_BITS = 7
DIGIT = 1 << DIGIT_BITS
TILE_ROWS = 16
NEVER = -1e30
MIB = 1024 * 1024
VMEM = pl.BlockSpec(memory_space=pltpu.VMEM)
SMEM = pl.BlockSpec(memory_space=pltpu.SMEM)
HBM = pl.BlockSpec(memory_space=pltpu.HBM)
ANY = pl.BlockSpec(memory_space=pl.ANY)


def low_half():
    return lax.broadcasted_iota(jnp.int32, (1, LANES), 1) < HEAD_DIM


def half_turn(block):
    return pltpu.roll(block, HEAD_DIM, 1)


def own_half(near):
    return lax.broadcasted_iota(jnp.int32, (1, LANES), 1) // HEAD_DIM == (near & 1)


def project_kernel(cuts, near_ref, rand_ref, pos_ref, t_hbm, q_hbm, k_hbm, v_hbm, *refs):
    listed_ref, t_ref, q_ref, k_ref, v_ref, all_ref, sems = refs[-7:]
    rows = t_ref.shape[0]
    heads = k_ref.shape[1] // HEAD_DIM
    far_refs, sent_refs = refs[:heads], refs[heads : 2 * heads]
    copies = []
    for i, (source, target) in enumerate(
        ((t_hbm, t_ref), (k_hbm, k_ref), (v_hbm, v_ref), (q_hbm, q_ref))
    ):
        part = source.shape[0] // cuts
        group = []
        for c in range(cuts):
            at = slice(c * part, (c + 1) * part)
            copy = pltpu.make_async_copy(source.at[at, :], target.at[at, :], sems.at[i, c])
            copy.start()
            group.append(copy)
        copies.append(group)

    spots = lax.broadcasted_iota(jnp.int32, listed_ref.shape, 0) * BLOCK
    spots = spots + lax.broadcasted_iota(jnp.int32, listed_ref.shape, 1)
    listed_ref[...] = lax.fori_loop(
        0,
        pos_ref.shape[0],
        lambda i, flags: jnp.where(spots == pos_ref[i], 1.0, flags),
        jnp.zeros(listed_ref.shape, jnp.float32),
        unroll=16,
    )

    def product(i, weight_ref):
        for copy in copies[i]:
            copy.wait()
        return jnp.dot(t_ref[...], weight_ref[...], preferred_element_type=jnp.float32)

    for copy in copies[0]:
        copy.wait()
    low = low_half()
    k = product(1, k_ref)
    v = product(2, v_ref)
    for pair in range(heads // 2):
        at = slice(pair * LANES, (pair + 1) * LANES)
        key, value = k[:, at], half_turn(v[:, at])
        all_ref[2 * pair, :rows, :] = jnp.where(low, key, value).astype(jnp.bfloat16)
        all_ref[2 * pair + 1, :rows, :] = jnp.where(low, value, key).astype(jnp.bfloat16)
    q = product(3, q_ref)
    for pair in range(heads // 2):
        at = slice(pair * LANES, (pair + 1) * LANES)
        top, bottom = q[: rows // 2, at], half_turn(q[rows // 2 :, at])
        all_ref[2 * pair, rows:, :] = jnp.where(low, top, bottom).astype(jnp.bfloat16)
        all_ref[2 * pair + 1, rows:, :] = jnp.where(low, bottom, top).astype(jnp.bfloat16)
    near = near_ref[0]
    digit_rows = sent_refs[0].shape[0] - rows - rows // 2
    row = lax.broadcasted_iota(jnp.int32, (digit_rows, LANES), 0)
    digits = jnp.zeros((digit_rows, LANES), jnp.float32)
    picks = rand_ref.shape[1]
    for j in range(rand_ref.shape[0]):
        for r in range(picks):
            at = 2 * (j * picks + r)
            value = rand_ref[j, r]
            digits = jnp.where(row == at, (value >> DIGIT_BITS).astype(jnp.float32), digits)
            digits = jnp.where(row == at + 1, (value & (DIGIT - 1)).astype(jnp.float32), digits)
    digits = digits.astype(jnp.bfloat16)
    for d in range(heads):
        far_refs[d][...] = all_ref[near ^ d, :rows, :]
        sent_refs[d][: rows + rows // 2, :] = all_ref[near ^ d]
        sent_refs[d][rows + rows // 2 :, :] = digits


def project(near, blocks, global_pos, rand_blocks, tokens, q_weight, k_weight, v_weight):
    rows, depth = tokens.shape
    feats = k_weight.shape[1]
    heads = feats // HEAD_DIM
    cuts = 2
    message = rows + rows // 2
    digit_rows = -(-2 * rand_blocks.size // TILE_ROWS) * TILE_ROWS
    pinned = [
        pltpu.with_memory_space_constraint(array, pltpu.HBM)
        for array in (rand_blocks, global_pos, tokens, q_weight, k_weight, v_weight)
    ]
    return pl.pallas_call(
        functools.partial(project_kernel, cuts),
        in_specs=[SMEM, SMEM, SMEM, HBM, HBM, HBM, HBM],
        out_specs=[VMEM] * (2 * heads + 1),
        out_shape=[jax.ShapeDtypeStruct((rows, LANES), jnp.bfloat16)] * heads
        + [jax.ShapeDtypeStruct((message + digit_rows, LANES), jnp.bfloat16)] * heads
        + [jax.ShapeDtypeStruct((blocks, LANES), jnp.float32)],
        scratch_shapes=[
            pltpu.VMEM((rows, depth), jnp.bfloat16),
            pltpu.VMEM((depth, feats), jnp.bfloat16),
            pltpu.VMEM((depth, feats), jnp.bfloat16),
            pltpu.VMEM((depth, feats), jnp.bfloat16),
            pltpu.VMEM((heads, message, LANES), jnp.bfloat16),
            pltpu.SemaphoreType.DMA((4, cuts)),
        ],
        compiler_params=pltpu.CompilerParams(vmem_limit_bytes=24 * MIB),
        cost_estimate=pl.CostEstimate(
            flops=6 * rows * depth * feats, bytes_accessed=2 * depth * (rows + 3 * feats), transcendentals=0
        ),
    )(near, *pinned)


def pack_kernel(*refs):
    out_ref = refs[-1]
    rows = out_ref.shape[0] // (len(refs) - 1)
    for i, ref in enumerate(refs[:-1]):
        out_ref[i * rows : (i + 1) * rows, :] = ref[:rows, :]


def pack(rows, messages):
    return pl.pallas_call(
        pack_kernel,
        in_specs=[VMEM] * len(messages),
        out_specs=VMEM,
        out_shape=jax.ShapeDtypeStruct((rows * len(messages), LANES), jnp.bfloat16),
        compiler_params=pltpu.CompilerParams(vmem_limit_bytes=32 * MIB),
    )(*messages)


def gather_kernel(count, *refs):
    out_ref, sems = refs[-2:]
    first, copies = 0, []
    for i, ref in enumerate(refs[:count]):
        at = slice(first, first + ref.shape[0])
        copies.append(pltpu.make_async_copy(ref, out_ref.at[at, :], sems.at[i]))
        first += ref.shape[0]
    for copy in copies:
        copy.start()
    for copy in copies:
        copy.wait()


def gather(blocks, after):
    rows = sum(block.shape[0] for block in blocks)
    return pl.pallas_call(
        functools.partial(gather_kernel, len(blocks)),
        in_specs=[ANY] * (len(blocks) + len(after)),
        out_specs=VMEM,
        out_shape=jax.ShapeDtypeStruct((rows, blocks[0].shape[1]), blocks[0].dtype),
        scratch_shapes=[pltpu.SemaphoreType.DMA((len(blocks),))],
        compiler_params=pltpu.CompilerParams(vmem_limit_bytes=24 * MIB),
    )(*blocks, *after)


def prepare(heads, picks, near, far, span, messages, listed_ref, q_ref, free_ref, block_ref, pick_ref):
    per_shard = span // BLOCK
    mine = own_half(near)
    for d in range(heads):
        packed = messages[d][span : span + span // 2, :].astype(jnp.float32)
        top = jnp.where(mine, packed, 0.0)
        bottom = jnp.where(mine, half_turn(packed), 0.0)
        q_ref[d * span : d * span + span // 2, :] = top.astype(q_ref.dtype)
        q_ref[d * span + span // 2 : (d + 1) * span, :] = bottom.astype(q_ref.dtype)
        rand = messages[d][span + span // 2 :, :].astype(jnp.float32)
        for j in range(per_shard):
            row = slice(d * per_shard + j, d * per_shard + j + 1)
            block = (far * heads + (near ^ d)) * per_shard + j
            block_ref[row, :] = jnp.full((1, LANES), block, jnp.int32)
            flags = jnp.broadcast_to(listed_ref[pl.ds(block, 1), :], (BLOCK, BLOCK))
            at = (d * per_shard + j) * BLOCK
            free_ref[at : at + BLOCK, :] = 1.0 - jnp.transpose(flags)
            for r in range(picks):
                at = 2 * (j * picks + r)
                pick = rand[at : at + 1, :] * DIGIT + rand[at + 1 : at + 2, :]
                pick_ref[r, row, :] = pick.astype(jnp.int32)


def fill_bias(heads, groups, near, listed_ref, block_ref, pick_ref, bias_ref):
    per_shard = block_ref.shape[0] // heads
    blocks = block_ref[...]
    picks = [pick_ref[r] for r in range(pick_ref.shape[0])]
    for g, there in enumerate(groups):
        for d in range(heads):
            for b in range(per_shard):
                key_block = (there * heads + (near ^ d)) * per_shard + b
                away = key_block - blocks
                times = listed_ref[pl.ds(key_block, 1), :] + jnp.where((away >= -2) & (away <= 1), 1.0, 0.0)
                for pick in picks:
                    times = times + jnp.where(pick == key_block, 1.0, 0.0)
                at = ((g * heads + d) * per_shard + b) * BLOCK
                bias_ref[:, at : at + BLOCK] = jnp.where(
                    times > 0, jnp.log2(jnp.maximum(times, 1.0)), NEVER
                )


def attend_rows(near, tile, span, q_ref, free_ref, bias_ref, keys, peak, total):
    per_shard = span // BLOCK
    scale = HEAD_DIM ** (-0.5) * math.log2(math.e)
    mine = own_half(near)
    q = q_ref[tile * span : (tile + 1) * span, :]
    scores = [[] for _ in range(per_shard)]
    for key_ref, first, column in keys:
        s = lax.dot_general(
            q,
            key_ref[first : first + span, :],
            (((1,), (1,)), ((), ())),
            preferred_element_type=jnp.float32,
        )
        for j in range(per_shard):
            block = tile * per_shard + j
            free = free_ref[block * BLOCK : (block + 1) * BLOCK, :]
            for b in range(per_shard):
                bias = bias_ref[block : block + 1, column + b * BLOCK : column + (b + 1) * BLOCK]
                part = s[j * BLOCK : (j + 1) * BLOCK, b * BLOCK : (b + 1) * BLOCK]
                scores[j].append(part * scale + free * bias)
    peaks, weights = [], []
    for j in range(per_shard):
        best = jnp.max(functools.reduce(jnp.maximum, scores[j]), axis=1, keepdims=True)
        best = jnp.broadcast_to(best, (BLOCK, LANES))
        if peak is not None:
            best = jnp.maximum(peak[j * BLOCK : (j + 1) * BLOCK, :], best)
        peaks.append(best)
        weights.append([jnp.exp2(part - best).astype(jnp.bfloat16) for part in scores[j]])
    new = jnp.concatenate(peaks, axis=0)
    if total is not None:
        total = total * jnp.exp2(peak - new)
    for i, (key_ref, first, _) in enumerate(keys):
        e = jnp.concatenate(
            [
                jnp.concatenate(weights[j][i * per_shard : (i + 1) * per_shard], axis=1)
                for j in range(per_shard)
            ],
            axis=0,
        )
        v = jnp.where(mine, jnp.ones((), jnp.bfloat16), key_ref[first : first + span, :])
        term = jnp.dot(e, v, preferred_element_type=jnp.float32)
        total = term if total is None else total + term
    return new, total


def finish(heads, parts, near, span, sums, out_ref):
    mine = own_half(near)
    piece = span // parts
    for d in range(heads):
        for part in range(parts):
            first = d * span + part * piece
            top = sums[first : first + piece // 2, :]
            bottom = sums[first + piece // 2 : first + piece, :]
            values = jnp.where(mine, half_turn(top), bottom)
            totals = jnp.where(mine, top, half_turn(bottom))
            out_ref[(near ^ d) * parts + part] = (values / totals).astype(out_ref.dtype)


def open_kernel(heads, picks, near_ref, far_ref, listed_ref, *refs):
    messages, refs = refs[:heads], refs[heads:]
    peaks, sums, q_ref, free_ref, bias_ref, block_ref, pick_ref = refs
    span = q_ref.shape[0] // heads
    near, far = near_ref[0], far_ref[0]
    prepare(heads, picks, near, far, span, messages, listed_ref, q_ref, free_ref, block_ref, pick_ref)
    fill_bias(heads, [far, far ^ 1], near, listed_ref, block_ref, pick_ref, bias_ref)
    keys = [(messages[d], 0, d * span) for d in range(heads)]
    for tile in range(heads):
        rows = slice(tile * span, (tile + 1) * span)
        peaks[rows, :], sums[rows, :] = attend_rows(
            near, tile, span, q_ref, free_ref, bias_ref, keys, None, None
        )


def more_kernel(heads, columns, parts, near_ref, q_ref, free_ref, bias_ref, peak_in, sum_in, *refs):
    kv_refs, (out_ref, sums) = refs[: len(columns)], refs[len(columns) :]
    span = q_ref.shape[0] // heads
    near = near_ref[0]
    keys = [(ref, 0, column) for ref, column in zip(kv_refs, columns)]
    for tile in range(heads):
        rows = slice(tile * span, (tile + 1) * span)
        _, sums[rows, :] = attend_rows(
            near, tile, span, q_ref, free_ref, bias_ref, keys, peak_in[rows, :], sum_in[rows, :]
        )
    finish(heads, parts, near, span, sums, out_ref)


def whole_kernel(heads, picks, parts, near_ref, far_ref, listed_ref, kv_ref, *refs):
    messages, refs = refs[:heads], refs[heads:]
    out_ref, peaks, sums, q_ref, free_ref, bias_ref, block_ref, pick_ref = refs
    span = q_ref.shape[0] // heads
    near, far = near_ref[0], far_ref[0]
    step = pl.program_id(0)

    @pl.when(step == 0)
    def _():
        peaks[...] = jnp.full_like(peaks, NEVER)
        sums[...] = jnp.zeros_like(sums)
        prepare(heads, picks, near, far, span, messages, listed_ref, q_ref, free_ref, block_ref, pick_ref)

    fill_bias(heads, [step], near, listed_ref, block_ref, pick_ref, bias_ref)
    keys = [(kv_ref, d * span, d * span) for d in range(heads)]
    for tile in range(heads):
        rows = slice(tile * span, (tile + 1) * span)
        peaks[rows, :], sums[rows, :] = attend_rows(
            near, tile, span, q_ref, free_ref, bias_ref, keys, peaks[rows, :], sums[rows, :]
        )

    @pl.when(step == pl.num_programs(0) - 1)
    def _():
        finish(heads, parts, near, span, sums, out_ref)


def attend_cost(rows, keys):
    return pl.CostEstimate(
        flops=4 * rows * keys * LANES, bytes_accessed=4 * (rows + keys) * LANES, transcendentals=rows * keys
    )


def open_attend(near, far, picks, listed, messages, span):
    heads = len(messages)
    rows = heads * span
    blocks = rows // BLOCK
    state = jax.ShapeDtypeStruct((rows, LANES), jnp.float32)
    return pl.pallas_call(
        functools.partial(open_kernel, heads, picks),
        in_specs=[SMEM, SMEM] + [VMEM] * (1 + heads),
        out_specs=[VMEM] * 5,
        out_shape=[
            state,
            state,
            jax.ShapeDtypeStruct((rows, LANES), jnp.bfloat16),
            state,
            jax.ShapeDtypeStruct((blocks, 2 * rows), jnp.float32),
        ],
        scratch_shapes=[
            pltpu.VMEM((blocks, LANES), jnp.int32),
            pltpu.VMEM((picks, blocks, LANES), jnp.int32),
        ],
        compiler_params=pltpu.CompilerParams(vmem_limit_bytes=24 * MIB),
        cost_estimate=attend_cost(rows, rows),
    )(near, far, listed, *messages)


def piece_shape(heads, parts, span):
    return jax.ShapeDtypeStruct((heads * parts, span // parts // 2, LANES), jnp.bfloat16)


def more_attend(near, heads, queries, old, kvs, columns, parts):
    rows = queries[0].shape[0]
    span = rows // heads
    return pl.pallas_call(
        functools.partial(more_kernel, heads, columns, parts),
        in_specs=[SMEM] + [VMEM] * (5 + len(kvs)),
        out_specs=VMEM,
        out_shape=piece_shape(heads, parts, span),
        scratch_shapes=[pltpu.VMEM((rows, LANES), jnp.float32)],
        compiler_params=pltpu.CompilerParams(vmem_limit_bytes=24 * MIB),
        cost_estimate=attend_cost(rows, span * len(kvs)),
    )(near, *queries, *old, *kvs)


def whole_attend(near, far, picks, listed, messages, kvs, span, parts):
    heads = len(messages)
    rows = heads * span
    blocks, steps = rows // BLOCK, kvs.shape[0] // rows
    return pl.pallas_call(
        functools.partial(whole_kernel, heads, picks, parts),
        grid=(steps,),
        in_specs=[SMEM, SMEM, VMEM, pl.BlockSpec((rows, LANES), lambda s: (s, 0))] + [VMEM] * heads,
        out_specs=VMEM,
        out_shape=piece_shape(heads, parts, span),
        scratch_shapes=[
            pltpu.VMEM((rows, LANES), jnp.float32),
            pltpu.VMEM((rows, LANES), jnp.float32),
            pltpu.VMEM((rows, LANES), jnp.bfloat16),
            pltpu.VMEM((rows, LANES), jnp.float32),
            pltpu.VMEM((blocks, rows), jnp.float32),
            pltpu.VMEM((blocks, LANES), jnp.int32),
            pltpu.VMEM((picks, blocks, LANES), jnp.int32),
        ],
        compiler_params=pltpu.CompilerParams(vmem_limit_bytes=24 * MIB),
        cost_estimate=attend_cost(rows, kvs.shape[0]),
    )(near, far, listed, kvs, *messages)


def mix_kernel(near_count, order, here_ref, got_ref, *refs):
    parts = len(order)
    low = low_half()
    depth = refs[0].shape[0]
    blocks = []
    for ref in refs[:-1]:
        blocks += [ref.at[first : first + depth, :] for first in range(0, ref.shape[0], depth)]
    total = None
    for i, d in enumerate(order):
        source = here_ref[0] ^ d
        columns = []
        for near in range(0, near_count, 2):
            even, odd = (got_ref[at * parts + source].astype(jnp.float32) for at in (near, near + 1))
            top = jnp.where(low, even, odd)
            bottom = half_turn(jnp.where(low, odd, even))
            columns.append(jnp.concatenate([top, bottom], axis=0).astype(jnp.bfloat16))
        rows = jnp.concatenate(columns, axis=1)
        term = jnp.dot(rows, blocks[i][...], preferred_element_type=jnp.float32)
        total = term if total is None else total + term
    refs[-1][...] = total.astype(refs[-1].dtype)


def mix(here, got, o_blocks, order):
    parts = len(order)
    return pl.pallas_call(
        functools.partial(mix_kernel, got.shape[0] // parts, order),
        out_shape=jax.ShapeDtypeStruct((2 * got.shape[1], o_blocks[0].shape[1]), jnp.bfloat16),
        in_specs=[SMEM] + [VMEM] * (1 + len(o_blocks)),
        out_specs=VMEM,
        compiler_params=pltpu.CompilerParams(vmem_limit_bytes=24 * MIB),
    )(here, got, *o_blocks)


def swapped(block, axis, distance):
    return lax.ppermute(block, axis, [(i, i ^ distance) for i in range(lax.axis_size(axis))])


def shards(tokens, q_weight, k_weight, v_weight, o_weight, rand_blocks, global_pos):
    tok_rows = tokens.shape[0]
    far_count, heads, parts = (lax.axis_size(axis) for axis in ("far", "near", "head"))
    near, far, here = (
        lax.axis_index(axis).astype(jnp.int32).reshape(1) for axis in ("near", "far", "head")
    )
    picks = rand_blocks.shape[1]

    blocks = far_count * heads * tok_rows // BLOCK
    *ready, listed = project(
        near, blocks, global_pos, rand_blocks, tokens, q_weight, k_weight, v_weight
    )
    leaving, sent = ready[:heads], ready[heads:]
    messages = [sent[0]] + [swapped(sent[d], "near", d) for d in range(1, heads)]

    if far_count == 2:
        apart = [swapped(leaving[d], ("far", "near"), heads + d) for d in range(heads)]
        peaks, sums, *queries = open_attend(near, far, picks, listed, messages, tok_rows)
        columns = [(heads + d) * tok_rows for d in range(heads)]
        pieces = more_attend(near, heads, queries, [peaks, sums], apart, columns, parts)
    else:
        kvs = lax.all_gather(pack(tok_rows, messages), "far", tiled=True)
        pieces = whole_attend(near, far, picks, listed, messages, kvs, tok_rows, parts)

    distance = parts // 2
    o_blocks = [o_weight, swapped(o_weight, "head", distance)]
    order = [0, distance]
    while distance > 1:
        distance //= 2
        o_blocks.append(swapped(gather(o_blocks, [pieces]), "head", distance))
        order = order + [d ^ distance for d in order]
    got = lax.all_to_all(pieces, ("near", "head"), 0, 0, tiled=True)
    return mix(here, got, o_blocks, order)


def solution(mesh):
    count, columns = mesh.devices.shape
    tm = ("far", "near")
    placed = (
        P(tm, None),
        P(None, "head"),
        P(None, "head"),
        P(None, "head"),
        P("head", None),
        P(tm, None),
        P(),
    )

    def run(tokens, q_weight, *rest):
        heads = q_weight.shape[1] // HEAD_DIM // columns
        split = Mesh(mesh.devices.reshape(count // heads, heads, columns), (*tm, "head"))
        body = jax.shard_map(
            shards, mesh=split, in_specs=placed, out_specs=P((*tm, "head"), None), check_vma=False
        )
        return body(tokens, q_weight, *rest)

    return run
```

```python
import functools
import math

import jax
import jax.numpy as jnp
from jax import lax
from jax.experimental import pallas as pl
from jax.experimental.pallas import tpu as pltpu
from jax.sharding import Mesh
from jax.sharding import PartitionSpec as P

HEAD_DIM = 64
BLOCK = 128
LANES = 128
DIGIT_BITS = 7
DIGIT = 1 << DIGIT_BITS
TILE_ROWS = 16
NEVER = -1e30
MIB = 1024 * 1024
VMEM = pl.BlockSpec(memory_space=pltpu.VMEM)
SMEM = pl.BlockSpec(memory_space=pltpu.SMEM)
HBM = pl.BlockSpec(memory_space=pltpu.HBM)
ANY = pl.BlockSpec(memory_space=pl.ANY)


def low_half():
    return lax.broadcasted_iota(jnp.int32, (1, LANES), 1) < HEAD_DIM


def half_turn(block):
    return pltpu.roll(block, HEAD_DIM, 1)


def own_half(near):
    return lax.broadcasted_iota(jnp.int32, (1, LANES), 1) // HEAD_DIM == (near & 1)


def project_kernel(cuts, near_ref, rand_ref, pos_ref, t_hbm, q_hbm, k_hbm, v_hbm, *refs):
    listed_ref, t_ref, q_ref, k_ref, v_ref, all_ref, sems = refs[-7:]
    rows = t_ref.shape[0]
    heads = k_ref.shape[1] // HEAD_DIM
    far_refs, sent_refs = refs[:heads], refs[heads : 2 * heads]
    copies = []
    for i, (source, target) in enumerate(
        ((t_hbm, t_ref), (k_hbm, k_ref), (v_hbm, v_ref), (q_hbm, q_ref))
    ):
        part = source.shape[0] // cuts
        group = []
        for c in range(cuts):
            at = slice(c * part, (c + 1) * part)
            copy = pltpu.make_async_copy(source.at[at, :], target.at[at, :], sems.at[i, c])
            copy.start()
            group.append(copy)
        copies.append(group)

    spots = lax.broadcasted_iota(jnp.int32, listed_ref.shape, 0) * BLOCK
    spots = spots + lax.broadcasted_iota(jnp.int32, listed_ref.shape, 1)
    listed_ref[...] = lax.fori_loop(
        0,
        pos_ref.shape[0],
        lambda i, flags: jnp.where(spots == pos_ref[i], 1.0, flags),
        jnp.zeros(listed_ref.shape, jnp.float32),
        unroll=16,
    )

    def product(i, weight_ref):
        for copy in copies[i]:
            copy.wait()
        return jnp.dot(t_ref[...], weight_ref[...], preferred_element_type=jnp.float32)

    for copy in copies[0]:
        copy.wait()
    low = low_half()
    k = product(1, k_ref)
    v = product(2, v_ref)
    for pair in range(heads // 2):
        at = slice(pair * LANES, (pair + 1) * LANES)
        key, value = k[:, at], half_turn(v[:, at])
        all_ref[2 * pair, :rows, :] = jnp.where(low, key, value).astype(jnp.bfloat16)
        all_ref[2 * pair + 1, :rows, :] = jnp.where(low, value, key).astype(jnp.bfloat16)
    q = product(3, q_ref)
    for pair in range(heads // 2):
        at = slice(pair * LANES, (pair + 1) * LANES)
        top, bottom = q[: rows // 2, at], half_turn(q[rows // 2 :, at])
        all_ref[2 * pair, rows:, :] = jnp.where(low, top, bottom).astype(jnp.bfloat16)
        all_ref[2 * pair + 1, rows:, :] = jnp.where(low, bottom, top).astype(jnp.bfloat16)
    near = near_ref[0]
    digit_rows = sent_refs[0].shape[0] - rows - rows // 2
    row = lax.broadcasted_iota(jnp.int32, (digit_rows, LANES), 0)
    digits = jnp.zeros((digit_rows, LANES), jnp.float32)
    picks = rand_ref.shape[1]
    for j in range(rand_ref.shape[0]):
        for r in range(picks):
            at = 2 * (j * picks + r)
            value = rand_ref[j, r]
            digits = jnp.where(row == at, (value >> DIGIT_BITS).astype(jnp.float32), digits)
            digits = jnp.where(row == at + 1, (value & (DIGIT - 1)).astype(jnp.float32), digits)
    digits = digits.astype(jnp.bfloat16)
    for d in range(heads):
        far_refs[d][...] = all_ref[near ^ d, :rows, :]
        sent_refs[d][: rows + rows // 2, :] = all_ref[near ^ d]
        sent_refs[d][rows + rows // 2 :, :] = digits


def project(near, blocks, global_pos, rand_blocks, tokens, q_weight, k_weight, v_weight):
    rows, depth = tokens.shape
    feats = k_weight.shape[1]
    heads = feats // HEAD_DIM
    cuts = 2
    message = rows + rows // 2
    digit_rows = -(-2 * rand_blocks.size // TILE_ROWS) * TILE_ROWS
    pinned = [
        pltpu.with_memory_space_constraint(array, pltpu.HBM)
        for array in (rand_blocks, global_pos, tokens, q_weight, k_weight, v_weight)
    ]
    return pl.pallas_call(
        functools.partial(project_kernel, cuts),
        in_specs=[SMEM, SMEM, SMEM, HBM, HBM, HBM, HBM],
        out_specs=[VMEM] * (2 * heads + 1),
        out_shape=[jax.ShapeDtypeStruct((rows, LANES), jnp.bfloat16)] * heads
        + [jax.ShapeDtypeStruct((message + digit_rows, LANES), jnp.bfloat16)] * heads
        + [jax.ShapeDtypeStruct((blocks, LANES), jnp.float32)],
        scratch_shapes=[
            pltpu.VMEM((rows, depth), jnp.bfloat16),
            pltpu.VMEM((depth, feats), jnp.bfloat16),
            pltpu.VMEM((depth, feats), jnp.bfloat16),
            pltpu.VMEM((depth, feats), jnp.bfloat16),
            pltpu.VMEM((heads, message, LANES), jnp.bfloat16),
            pltpu.SemaphoreType.DMA((4, cuts)),
        ],
        compiler_params=pltpu.CompilerParams(vmem_limit_bytes=24 * MIB),
        cost_estimate=pl.CostEstimate(
            flops=6 * rows * depth * feats, bytes_accessed=2 * depth * (rows + 3 * feats), transcendentals=0
        ),
    )(near, *pinned)


def pack_kernel(*refs):
    out_ref = refs[-1]
    rows = out_ref.shape[0] // (len(refs) - 1)
    for i, ref in enumerate(refs[:-1]):
        out_ref[i * rows : (i + 1) * rows, :] = ref[:rows, :]


def pack(rows, messages):
    return pl.pallas_call(
        pack_kernel,
        in_specs=[VMEM] * len(messages),
        out_specs=VMEM,
        out_shape=jax.ShapeDtypeStruct((rows * len(messages), LANES), jnp.bfloat16),
        compiler_params=pltpu.CompilerParams(vmem_limit_bytes=32 * MIB),
    )(*messages)


def gather_kernel(count, *refs):
    out_ref, sems = refs[-2:]
    first, copies = 0, []
    for i, ref in enumerate(refs[:count]):
        at = slice(first, first + ref.shape[0])
        copies.append(pltpu.make_async_copy(ref, out_ref.at[at, :], sems.at[i]))
        first += ref.shape[0]
    for copy in copies:
        copy.start()
    for copy in copies:
        copy.wait()


def gather(blocks, after):
    rows = sum(block.shape[0] for block in blocks)
    return pl.pallas_call(
        functools.partial(gather_kernel, len(blocks)),
        in_specs=[ANY] * (len(blocks) + len(after)),
        out_specs=VMEM,
        out_shape=jax.ShapeDtypeStruct((rows, blocks[0].shape[1]), blocks[0].dtype),
        scratch_shapes=[pltpu.SemaphoreType.DMA((len(blocks),))],
        compiler_params=pltpu.CompilerParams(vmem_limit_bytes=24 * MIB),
    )(*blocks, *after)


def prepare(heads, picks, near, far, span, messages, listed_ref, q_ref, free_ref, block_ref, pick_ref):
    per_shard = span // BLOCK
    mine = own_half(near)
    for d in range(heads):
        packed = messages[d][span : span + span // 2, :].astype(jnp.float32)
        top = jnp.where(mine, packed, 0.0)
        bottom = jnp.where(mine, half_turn(packed), 0.0)
        q_ref[d * span : d * span + span // 2, :] = top.astype(q_ref.dtype)
        q_ref[d * span + span // 2 : (d + 1) * span, :] = bottom.astype(q_ref.dtype)
        rand = messages[d][span + span // 2 :, :].astype(jnp.float32)
        for j in range(per_shard):
            row = slice(d * per_shard + j, d * per_shard + j + 1)
            block = (far * heads + (near ^ d)) * per_shard + j
            block_ref[row, :] = jnp.full((1, LANES), block, jnp.int32)
            flags = jnp.broadcast_to(listed_ref[pl.ds(block, 1), :], (BLOCK, BLOCK))
            at = (d * per_shard + j) * BLOCK
            free_ref[at : at + BLOCK, :] = 1.0 - jnp.transpose(flags)
            for r in range(picks):
                at = 2 * (j * picks + r)
                pick = rand[at : at + 1, :] * DIGIT + rand[at + 1 : at + 2, :]
                pick_ref[r, row, :] = pick.astype(jnp.int32)


def fill_bias(heads, groups, near, listed_ref, block_ref, pick_ref, bias_ref):
    per_shard = block_ref.shape[0] // heads
    blocks = block_ref[...]
    picks = [pick_ref[r] for r in range(pick_ref.shape[0])]
    for g, there in enumerate(groups):
        for d in range(heads):
            for b in range(per_shard):
                key_block = (there * heads + (near ^ d)) * per_shard + b
                away = key_block - blocks
                times = listed_ref[pl.ds(key_block, 1), :] + jnp.where((away >= -2) & (away <= 1), 1.0, 0.0)
                for pick in picks:
                    times = times + jnp.where(pick == key_block, 1.0, 0.0)
                at = ((g * heads + d) * per_shard + b) * BLOCK
                bias_ref[:, at : at + BLOCK] = jnp.where(
                    times > 0, jnp.log2(jnp.maximum(times, 1.0)), NEVER
                )


def attend_rows(near, tile, span, q_ref, free_ref, bias_ref, keys, peak, total):
    per_shard = span // BLOCK
    scale = HEAD_DIM ** (-0.5) * math.log2(math.e)
    mine = own_half(near)
    q = q_ref[tile * span : (tile + 1) * span, :]
    scores = [[] for _ in range(per_shard)]
    for key_ref, first, column in keys:
        s = lax.dot_general(
            q,
            key_ref[first : first + span, :],
            (((1,), (1,)), ((), ())),
            preferred_element_type=jnp.float32,
        )
        for j in range(per_shard):
            block = tile * per_shard + j
            free = free_ref[block * BLOCK : (block + 1) * BLOCK, :]
            for b in range(per_shard):
                bias = bias_ref[block : block + 1, column + b * BLOCK : column + (b + 1) * BLOCK]
                part = s[j * BLOCK : (j + 1) * BLOCK, b * BLOCK : (b + 1) * BLOCK]
                scores[j].append(part * scale + free * bias)
    peaks, weights = [], []
    for j in range(per_shard):
        best = jnp.max(functools.reduce(jnp.maximum, scores[j]), axis=1, keepdims=True)
        best = jnp.broadcast_to(best, (BLOCK, LANES))
        if peak is not None:
            best = jnp.maximum(peak[j * BLOCK : (j + 1) * BLOCK, :], best)
        peaks.append(best)
        weights.append([jnp.exp2(part - best).astype(jnp.bfloat16) for part in scores[j]])
    new = jnp.concatenate(peaks, axis=0)
    if total is not None:
        total = total * jnp.exp2(peak - new)
    for i, (key_ref, first, _) in enumerate(keys):
        e = jnp.concatenate(
            [
                jnp.concatenate(weights[j][i * per_shard : (i + 1) * per_shard], axis=1)
                for j in range(per_shard)
            ],
            axis=0,
        )
        v = jnp.where(mine, jnp.ones((), jnp.bfloat16), key_ref[first : first + span, :])
        term = jnp.dot(e, v, preferred_element_type=jnp.float32)
        total = term if total is None else total + term
    return new, total


def finish(heads, parts, near, span, sums, out_ref):
    mine = own_half(near)
    piece = span // parts
    for d in range(heads):
        for part in range(parts):
            first = d * span + part * piece
            top = sums[first : first + piece // 2, :]
            bottom = sums[first + piece // 2 : first + piece, :]
            values = jnp.where(mine, half_turn(top), bottom)
            totals = jnp.where(mine, top, half_turn(bottom))
            out_ref[(near ^ d) * parts + part] = (values / totals).astype(out_ref.dtype)


def open_kernel(heads, picks, near_ref, far_ref, listed_ref, *refs):
    messages, refs = refs[:heads], refs[heads:]
    peaks, sums, q_ref, free_ref, bias_ref, block_ref, pick_ref = refs
    span = q_ref.shape[0] // heads
    near, far = near_ref[0], far_ref[0]
    prepare(heads, picks, near, far, span, messages, listed_ref, q_ref, free_ref, block_ref, pick_ref)
    fill_bias(heads, [far, far ^ 1], near, listed_ref, block_ref, pick_ref, bias_ref)
    keys = [(messages[d], 0, d * span) for d in range(heads)]
    for tile in range(heads):
        rows = slice(tile * span, (tile + 1) * span)
        peaks[rows, :], sums[rows, :] = attend_rows(
            near, tile, span, q_ref, free_ref, bias_ref, keys, None, None
        )


def more_kernel(heads, columns, parts, near_ref, q_ref, free_ref, bias_ref, peak_in, sum_in, *refs):
    kv_refs, (out_ref, sums) = refs[: len(columns)], refs[len(columns) :]
    span = q_ref.shape[0] // heads
    near = near_ref[0]
    keys = [(ref, 0, column) for ref, column in zip(kv_refs, columns)]
    for tile in range(heads):
        rows = slice(tile * span, (tile + 1) * span)
        _, sums[rows, :] = attend_rows(
            near, tile, span, q_ref, free_ref, bias_ref, keys, peak_in[rows, :], sum_in[rows, :]
        )
    finish(heads, parts, near, span, sums, out_ref)


def whole_kernel(heads, picks, parts, near_ref, far_ref, listed_ref, kv_ref, *refs):
    messages, refs = refs[:heads], refs[heads:]
    out_ref, peaks, sums, q_ref, free_ref, bias_ref, block_ref, pick_ref = refs
    span = q_ref.shape[0] // heads
    near, far = near_ref[0], far_ref[0]
    step = pl.program_id(0)

    @pl.when(step == 0)
    def _():
        peaks[...] = jnp.full_like(peaks, NEVER)
        sums[...] = jnp.zeros_like(sums)
        prepare(heads, picks, near, far, span, messages, listed_ref, q_ref, free_ref, block_ref, pick_ref)

    fill_bias(heads, [step], near, listed_ref, block_ref, pick_ref, bias_ref)
    keys = [(kv_ref, d * span, d * span) for d in range(heads)]
    for tile in range(heads):
        rows = slice(tile * span, (tile + 1) * span)
        peaks[rows, :], sums[rows, :] = attend_rows(
            near, tile, span, q_ref, free_ref, bias_ref, keys, peaks[rows, :], sums[rows, :]
        )

    @pl.when(step == pl.num_programs(0) - 1)
    def _():
        finish(heads, parts, near, span, sums, out_ref)


def attend_cost(rows, keys):
    return pl.CostEstimate(
        flops=4 * rows * keys * LANES, bytes_accessed=4 * (rows + keys) * LANES, transcendentals=rows * keys
    )


def open_attend(near, far, picks, listed, messages, span):
    heads = len(messages)
    rows = heads * span
    blocks = rows // BLOCK
    state = jax.ShapeDtypeStruct((rows, LANES), jnp.float32)
    return pl.pallas_call(
        functools.partial(open_kernel, heads, picks),
        in_specs=[SMEM, SMEM] + [VMEM] * (1 + heads),
        out_specs=[VMEM] * 5,
        out_shape=[
            state,
            state,
            jax.ShapeDtypeStruct((rows, LANES), jnp.bfloat16),
            state,
            jax.ShapeDtypeStruct((blocks, 2 * rows), jnp.float32),
        ],
        scratch_shapes=[
            pltpu.VMEM((blocks, LANES), jnp.int32),
            pltpu.VMEM((picks, blocks, LANES), jnp.int32),
        ],
        compiler_params=pltpu.CompilerParams(vmem_limit_bytes=24 * MIB),
        cost_estimate=attend_cost(rows, rows),
    )(near, far, listed, *messages)


def piece_shape(heads, parts, span):
    return jax.ShapeDtypeStruct((heads * parts, span // parts // 2, LANES), jnp.bfloat16)


def more_attend(near, heads, queries, old, kvs, columns, parts):
    rows = queries[0].shape[0]
    span = rows // heads
    return pl.pallas_call(
        functools.partial(more_kernel, heads, columns, parts),
        in_specs=[SMEM] + [VMEM] * (5 + len(kvs)),
        out_specs=VMEM,
        out_shape=piece_shape(heads, parts, span),
        scratch_shapes=[pltpu.VMEM((rows, LANES), jnp.float32)],
        compiler_params=pltpu.CompilerParams(vmem_limit_bytes=24 * MIB),
        cost_estimate=attend_cost(20 * rows, span * len(kvs)),
    )(near, *queries, *old, *kvs)


def whole_attend(near, far, picks, listed, messages, kvs, span, parts):
    heads = len(messages)
    rows = heads * span
    blocks, steps = rows // BLOCK, kvs.shape[0] // rows
    return pl.pallas_call(
        functools.partial(whole_kernel, heads, picks, parts),
        grid=(steps,),
        in_specs=[SMEM, SMEM, VMEM, pl.BlockSpec((rows, LANES), lambda s: (s, 0))] + [VMEM] * heads,
        out_specs=VMEM,
        out_shape=piece_shape(heads, parts, span),
        scratch_shapes=[
            pltpu.VMEM((rows, LANES), jnp.float32),
            pltpu.VMEM((rows, LANES), jnp.float32),
            pltpu.VMEM((rows, LANES), jnp.bfloat16),
            pltpu.VMEM((rows, LANES), jnp.float32),
            pltpu.VMEM((blocks, rows), jnp.float32),
            pltpu.VMEM((blocks, LANES), jnp.int32),
            pltpu.VMEM((picks, blocks, LANES), jnp.int32),
        ],
        compiler_params=pltpu.CompilerParams(vmem_limit_bytes=24 * MIB),
        cost_estimate=attend_cost(rows, kvs.shape[0]),
    )(near, far, listed, kvs, *messages)


def mix_kernel(near_count, order, here_ref, got_ref, *refs):
    parts = len(order)
    low = low_half()
    depth = refs[0].shape[0]
    blocks = []
    for ref in refs[:-1]:
        blocks += [ref.at[first : first + depth, :] for first in range(0, ref.shape[0], depth)]
    total = None
    for i, d in enumerate(order):
        source = here_ref[0] ^ d
        columns = []
        for near in range(0, near_count, 2):
            even, odd = (got_ref[at * parts + source].astype(jnp.float32) for at in (near, near + 1))
            top = jnp.where(low, even, odd)
            bottom = half_turn(jnp.where(low, odd, even))
            columns.append(jnp.concatenate([top, bottom], axis=0).astype(jnp.bfloat16))
        rows = jnp.concatenate(columns, axis=1)
        term = jnp.dot(rows, blocks[i][...], preferred_element_type=jnp.float32)
        total = term if total is None else total + term
    refs[-1][...] = total.astype(refs[-1].dtype)


def mix(here, got, o_blocks, order):
    parts = len(order)
    return pl.pallas_call(
        functools.partial(mix_kernel, got.shape[0] // parts, order),
        out_shape=jax.ShapeDtypeStruct((2 * got.shape[1], o_blocks[0].shape[1]), jnp.bfloat16),
        in_specs=[SMEM] + [VMEM] * (1 + len(o_blocks)),
        out_specs=VMEM,
        compiler_params=pltpu.CompilerParams(vmem_limit_bytes=24 * MIB),
    )(here, got, *o_blocks)


def swapped(block, axis, distance):
    return lax.ppermute(block, axis, [(i, i ^ distance) for i in range(lax.axis_size(axis))])


def shards(tokens, q_weight, k_weight, v_weight, o_weight, rand_blocks, global_pos):
    tok_rows = tokens.shape[0]
    far_count, heads, parts = (lax.axis_size(axis) for axis in ("far", "near", "head"))
    near, far, here = (
        lax.axis_index(axis).astype(jnp.int32).reshape(1) for axis in ("near", "far", "head")
    )
    picks = rand_blocks.shape[1]

    blocks = far_count * heads * tok_rows // BLOCK
    *ready, listed = project(
        near, blocks, global_pos, rand_blocks, tokens, q_weight, k_weight, v_weight
    )
    leaving, sent = ready[:heads], ready[heads:]
    messages = [sent[0]] + [swapped(sent[d], "near", d) for d in range(1, heads)]

    if far_count == 2:
        apart = [swapped(leaving[d], ("far", "near"), heads + d) for d in range(heads)]
        peaks, sums, *queries = open_attend(near, far, picks, listed, messages, tok_rows)
        columns = [(heads + d) * tok_rows for d in range(heads)]
        pieces = more_attend(near, heads, queries, [peaks, sums], apart, columns, parts)
    else:
        kvs = lax.all_gather(pack(tok_rows, messages), "far", tiled=True)
        pieces = whole_attend(near, far, picks, listed, messages, kvs, tok_rows, parts)

    distance = parts // 2
    o_blocks = [o_weight, swapped(o_weight, "head", distance)]
    order = [0, distance]
    while distance > 1:
        distance //= 2
        o_blocks.append(swapped(gather(o_blocks, [pieces]), "head", distance))
        order = order + [d ^ distance for d in order]
    got = lax.all_to_all(pieces, ("near", "head"), 0, 0, tiled=True)
    return mix(here, got, o_blocks, order)


def solution(mesh):
    count, columns = mesh.devices.shape
    tm = ("far", "near")
    placed = (
        P(tm, None),
        P(None, "head"),
        P(None, "head"),
        P(None, "head"),
        P("head", None),
        P(tm, None),
        P(),
    )

    def run(tokens, q_weight, *rest):
        heads = q_weight.shape[1] // HEAD_DIM // columns
        split = Mesh(mesh.devices.reshape(count // heads, heads, columns), (*tm, "head"))
        body = jax.shard_map(
            shards, mesh=split, in_specs=placed, out_specs=P((*tm, "head"), None), check_vma=False
        )
        return body(tokens, q_weight, *rest)

    return run
```

```python
import functools
import math

import jax
import jax.numpy as jnp
from jax import lax
from jax.experimental import pallas as pl
from jax.experimental.pallas import tpu as pltpu
from jax.sharding import Mesh
from jax.sharding import PartitionSpec as P

HEAD_DIM = 64
BLOCK = 128
LANES = 128
DIGIT_BITS = 7
DIGIT = 1 << DIGIT_BITS
TILE_ROWS = 16
NEVER = -1e30
MIB = 1024 * 1024
VMEM = pl.BlockSpec(memory_space=pltpu.VMEM)
SMEM = pl.BlockSpec(memory_space=pltpu.SMEM)
HBM = pl.BlockSpec(memory_space=pltpu.HBM)
ANY = pl.BlockSpec(memory_space=pl.ANY)


def low_half():
    return lax.broadcasted_iota(jnp.int32, (1, LANES), 1) < HEAD_DIM


def half_turn(block):
    return pltpu.roll(block, HEAD_DIM, 1)


def own_half(near):
    return lax.broadcasted_iota(jnp.int32, (1, LANES), 1) // HEAD_DIM == (near & 1)


def project_kernel(cuts, near_ref, rand_ref, pos_ref, t_hbm, q_hbm, k_hbm, v_hbm, *refs):
    listed_ref, t_ref, q_ref, k_ref, v_ref, all_ref, sems = refs[-7:]
    rows = t_ref.shape[0]
    heads = k_ref.shape[1] // HEAD_DIM
    far_refs, sent_refs = refs[:heads], refs[heads : 2 * heads]
    copies = []
    for i, (source, target) in enumerate(
        ((t_hbm, t_ref), (k_hbm, k_ref), (v_hbm, v_ref), (q_hbm, q_ref))
    ):
        part = source.shape[0] // cuts
        group = []
        for c in range(cuts):
            at = slice(c * part, (c + 1) * part)
            copy = pltpu.make_async_copy(source.at[at, :], target.at[at, :], sems.at[i, c])
            copy.start()
            group.append(copy)
        copies.append(group)

    spots = lax.broadcasted_iota(jnp.int32, listed_ref.shape, 0) * BLOCK
    spots = spots + lax.broadcasted_iota(jnp.int32, listed_ref.shape, 1)
    listed_ref[...] = lax.fori_loop(
        0,
        pos_ref.shape[0],
        lambda i, flags: jnp.where(spots == pos_ref[i], 1.0, flags),
        jnp.zeros(listed_ref.shape, jnp.float32),
        unroll=16,
    )

    def product(i, weight_ref):
        for copy in copies[i]:
            copy.wait()
        return jnp.dot(t_ref[...], weight_ref[...], preferred_element_type=jnp.float32)

    for copy in copies[0]:
        copy.wait()
    low = low_half()
    k = product(1, k_ref)
    v = product(2, v_ref)
    for pair in range(heads // 2):
        at = slice(pair * LANES, (pair + 1) * LANES)
        key, value = k[:, at], half_turn(v[:, at])
        all_ref[2 * pair, :rows, :] = jnp.where(low, key, value).astype(jnp.bfloat16)
        all_ref[2 * pair + 1, :rows, :] = jnp.where(low, value, key).astype(jnp.bfloat16)
    q = product(3, q_ref)
    for pair in range(heads // 2):
        at = slice(pair * LANES, (pair + 1) * LANES)
        top, bottom = q[: rows // 2, at], half_turn(q[rows // 2 :, at])
        all_ref[2 * pair, rows:, :] = jnp.where(low, top, bottom).astype(jnp.bfloat16)
        all_ref[2 * pair + 1, rows:, :] = jnp.where(low, bottom, top).astype(jnp.bfloat16)
    near = near_ref[0]
    digit_rows = sent_refs[0].shape[0] - rows - rows // 2
    row = lax.broadcasted_iota(jnp.int32, (digit_rows, LANES), 0)
    digits = jnp.zeros((digit_rows, LANES), jnp.float32)
    picks = rand_ref.shape[1]
    for j in range(rand_ref.shape[0]):
        for r in range(picks):
            at = 2 * (j * picks + r)
            value = rand_ref[j, r]
            digits = jnp.where(row == at, (value >> DIGIT_BITS).astype(jnp.float32), digits)
            digits = jnp.where(row == at + 1, (value & (DIGIT - 1)).astype(jnp.float32), digits)
    digits = digits.astype(jnp.bfloat16)
    for d in range(heads):
        far_refs[d][...] = all_ref[near ^ d, :rows, :]
        sent_refs[d][: rows + rows // 2, :] = all_ref[near ^ d]
        sent_refs[d][rows + rows // 2 :, :] = digits


def project(near, blocks, global_pos, rand_blocks, tokens, q_weight, k_weight, v_weight):
    rows, depth = tokens.shape
    feats = k_weight.shape[1]
    heads = feats // HEAD_DIM
    cuts = 2
    message = rows + rows // 2
    digit_rows = -(-2 * rand_blocks.size // TILE_ROWS) * TILE_ROWS
    pinned = [
        pltpu.with_memory_space_constraint(array, pltpu.HBM)
        for array in (rand_blocks, global_pos, tokens, q_weight, k_weight, v_weight)
    ]
    return pl.pallas_call(
        functools.partial(project_kernel, cuts),
        in_specs=[SMEM, SMEM, SMEM, HBM, HBM, HBM, HBM],
        out_specs=[VMEM] * (2 * heads + 1),
        out_shape=[jax.ShapeDtypeStruct((rows, LANES), jnp.bfloat16)] * heads
        + [jax.ShapeDtypeStruct((message + digit_rows, LANES), jnp.bfloat16)] * heads
        + [jax.ShapeDtypeStruct((blocks, LANES), jnp.float32)],
        scratch_shapes=[
            pltpu.VMEM((rows, depth), jnp.bfloat16),
            pltpu.VMEM((depth, feats), jnp.bfloat16),
            pltpu.VMEM((depth, feats), jnp.bfloat16),
            pltpu.VMEM((depth, feats), jnp.bfloat16),
            pltpu.VMEM((heads, message, LANES), jnp.bfloat16),
            pltpu.SemaphoreType.DMA((4, cuts)),
        ],
        compiler_params=pltpu.CompilerParams(vmem_limit_bytes=24 * MIB),
        cost_estimate=pl.CostEstimate(
            flops=6 * rows * depth * feats, bytes_accessed=2 * depth * (rows + 3 * feats), transcendentals=0
        ),
    )(near, *pinned)


def pack_kernel(*refs):
    out_ref = refs[-1]
    rows = out_ref.shape[0] // (len(refs) - 1)
    for i, ref in enumerate(refs[:-1]):
        out_ref[i * rows : (i + 1) * rows, :] = ref[:rows, :]


def pack(rows, messages):
    return pl.pallas_call(
        pack_kernel,
        in_specs=[VMEM] * len(messages),
        out_specs=VMEM,
        out_shape=jax.ShapeDtypeStruct((rows * len(messages), LANES), jnp.bfloat16),
        compiler_params=pltpu.CompilerParams(vmem_limit_bytes=32 * MIB),
    )(*messages)


def gather_kernel(count, *refs):
    out_ref, sems = refs[-2:]
    first, copies = 0, []
    for i, ref in enumerate(refs[:count]):
        at = slice(first, first + ref.shape[0])
        copies.append(pltpu.make_async_copy(ref, out_ref.at[at, :], sems.at[i]))
        first += ref.shape[0]
    for copy in copies:
        copy.start()
    for copy in copies:
        copy.wait()


def gather(blocks, after):
    rows = sum(block.shape[0] for block in blocks)
    return pl.pallas_call(
        functools.partial(gather_kernel, len(blocks)),
        in_specs=[ANY] * (len(blocks) + len(after)),
        out_specs=VMEM,
        out_shape=jax.ShapeDtypeStruct((rows, blocks[0].shape[1]), blocks[0].dtype),
        scratch_shapes=[pltpu.SemaphoreType.DMA((len(blocks),))],
        compiler_params=pltpu.CompilerParams(vmem_limit_bytes=24 * MIB),
    )(*blocks, *after)


def prepare(heads, picks, near, far, span, messages, listed_ref, q_ref, free_ref, block_ref, pick_ref):
    per_shard = span // BLOCK
    mine = own_half(near)
    for d in range(heads):
        packed = messages[d][span : span + span // 2, :].astype(jnp.float32)
        top = jnp.where(mine, packed, 0.0)
        bottom = jnp.where(mine, half_turn(packed), 0.0)
        q_ref[d * span : d * span + span // 2, :] = top.astype(q_ref.dtype)
        q_ref[d * span + span // 2 : (d + 1) * span, :] = bottom.astype(q_ref.dtype)
        rand = messages[d][span + span // 2 :, :].astype(jnp.float32)
        for j in range(per_shard):
            row = slice(d * per_shard + j, d * per_shard + j + 1)
            block = (far * heads + (near ^ d)) * per_shard + j
            block_ref[row, :] = jnp.full((1, LANES), block, jnp.int32)
            flags = jnp.broadcast_to(listed_ref[pl.ds(block, 1), :], (BLOCK, BLOCK))
            at = (d * per_shard + j) * BLOCK
            free_ref[at : at + BLOCK, :] = 1.0 - jnp.transpose(flags)
            for r in range(picks):
                at = 2 * (j * picks + r)
                pick = rand[at : at + 1, :] * DIGIT + rand[at + 1 : at + 2, :]
                pick_ref[r, row, :] = pick.astype(jnp.int32)


def fill_bias(heads, groups, near, listed_ref, block_ref, pick_ref, bias_ref):
    per_shard = block_ref.shape[0] // heads
    blocks = block_ref[...]
    picks = [pick_ref[r] for r in range(pick_ref.shape[0])]
    for g, there in enumerate(groups):
        for d in range(heads):
            for b in range(per_shard):
                key_block = (there * heads + (near ^ d)) * per_shard + b
                away = key_block - blocks
                times = listed_ref[pl.ds(key_block, 1), :] + jnp.where((away >= -2) & (away <= 1), 1.0, 0.0)
                for pick in picks:
                    times = times + jnp.where(pick == key_block, 1.0, 0.0)
                at = ((g * heads + d) * per_shard + b) * BLOCK
                bias_ref[:, at : at + BLOCK] = jnp.where(
                    times > 0, jnp.log2(jnp.maximum(times, 1.0)), NEVER
                )


def attend_rows(near, tile, span, q_ref, free_ref, bias_ref, keys, peak, total):
    per_shard = span // BLOCK
    scale = HEAD_DIM ** (-0.5) * math.log2(math.e)
    mine = own_half(near)
    q = q_ref[tile * span : (tile + 1) * span, :]
    scores = [[] for _ in range(per_shard)]
    for key_ref, first, column in keys:
        s = lax.dot_general(
            q,
            key_ref[first : first + span, :],
            (((1,), (1,)), ((), ())),
            preferred_element_type=jnp.float32,
        )
        for j in range(per_shard):
            block = tile * per_shard + j
            free = free_ref[block * BLOCK : (block + 1) * BLOCK, :]
            for b in range(per_shard):
                bias = bias_ref[block : block + 1, column + b * BLOCK : column + (b + 1) * BLOCK]
                part = s[j * BLOCK : (j + 1) * BLOCK, b * BLOCK : (b + 1) * BLOCK]
                scores[j].append(part * scale + free * bias)
    peaks, weights = [], []
    for j in range(per_shard):
        best = jnp.max(functools.reduce(jnp.maximum, scores[j]), axis=1, keepdims=True)
        best = jnp.broadcast_to(best, (BLOCK, LANES))
        if peak is not None:
            best = jnp.maximum(peak[j * BLOCK : (j + 1) * BLOCK, :], best)
        peaks.append(best)
        weights.append([jnp.exp2(part - best).astype(jnp.bfloat16) for part in scores[j]])
    new = jnp.concatenate(peaks, axis=0)
    if total is not None:
        total = total * jnp.exp2(peak - new)
    for i, (key_ref, first, _) in enumerate(keys):
        e = jnp.concatenate(
            [
                jnp.concatenate(weights[j][i * per_shard : (i + 1) * per_shard], axis=1)
                for j in range(per_shard)
            ],
            axis=0,
        )
        v = jnp.where(mine, jnp.ones((), jnp.bfloat16), key_ref[first : first + span, :])
        term = jnp.dot(e, v, preferred_element_type=jnp.float32)
        total = term if total is None else total + term
    return new, total


def finish(heads, parts, near, span, sums, out_ref):
    mine = own_half(near)
    piece = span // parts
    for d in range(heads):
        for part in range(parts):
            first = d * span + part * piece
            top = sums[first : first + piece // 2, :]
            bottom = sums[first + piece // 2 : first + piece, :]
            values = jnp.where(mine, half_turn(top), bottom)
            totals = jnp.where(mine, top, half_turn(bottom))
            out_ref[(near ^ d) * parts + part] = (values / totals).astype(out_ref.dtype)


def open_kernel(heads, picks, near_ref, far_ref, listed_ref, *refs):
    messages, early, refs = refs[:heads], refs[heads:-7], refs[-7:]
    peaks, sums, q_ref, free_ref, bias_ref, block_ref, pick_ref = refs
    span = q_ref.shape[0] // heads
    near, far = near_ref[0], far_ref[0]
    prepare(heads, picks, near, far, span, messages, listed_ref, q_ref, free_ref, block_ref, pick_ref)
    fill_bias(heads, [far, far ^ 1], near, listed_ref, block_ref, pick_ref, bias_ref)
    keys = [(ref, 0, i * span) for i, ref in enumerate((*messages, *early))]
    for tile in range(heads):
        rows = slice(tile * span, (tile + 1) * span)
        peaks[rows, :], sums[rows, :] = attend_rows(
            near, tile, span, q_ref, free_ref, bias_ref, keys, None, None
        )


def more_kernel(heads, columns, parts, near_ref, q_ref, free_ref, bias_ref, peak_in, sum_in, *refs):
    kv_refs, (out_ref, sums) = refs[: len(columns)], refs[len(columns) :]
    span = q_ref.shape[0] // heads
    near = near_ref[0]
    keys = [(ref, 0, column) for ref, column in zip(kv_refs, columns)]
    for tile in range(heads):
        rows = slice(tile * span, (tile + 1) * span)
        _, sums[rows, :] = attend_rows(
            near, tile, span, q_ref, free_ref, bias_ref, keys, peak_in[rows, :], sum_in[rows, :]
        )
    finish(heads, parts, near, span, sums, out_ref)


def whole_kernel(heads, picks, parts, near_ref, far_ref, listed_ref, kv_ref, *refs):
    messages, refs = refs[:heads], refs[heads:]
    out_ref, peaks, sums, q_ref, free_ref, bias_ref, block_ref, pick_ref = refs
    span = q_ref.shape[0] // heads
    near, far = near_ref[0], far_ref[0]
    step = pl.program_id(0)

    @pl.when(step == 0)
    def _():
        peaks[...] = jnp.full_like(peaks, NEVER)
        sums[...] = jnp.zeros_like(sums)
        prepare(heads, picks, near, far, span, messages, listed_ref, q_ref, free_ref, block_ref, pick_ref)

    fill_bias(heads, [step], near, listed_ref, block_ref, pick_ref, bias_ref)
    keys = [(kv_ref, d * span, d * span) for d in range(heads)]
    for tile in range(heads):
        rows = slice(tile * span, (tile + 1) * span)
        peaks[rows, :], sums[rows, :] = attend_rows(
            near, tile, span, q_ref, free_ref, bias_ref, keys, peaks[rows, :], sums[rows, :]
        )

    @pl.when(step == pl.num_programs(0) - 1)
    def _():
        finish(heads, parts, near, span, sums, out_ref)


def attend_cost(rows, keys):
    return pl.CostEstimate(
        flops=4 * rows * keys * LANES, bytes_accessed=4 * (rows + keys) * LANES, transcendentals=rows * keys
    )


def open_attend(near, far, picks, listed, messages, early, span):
    heads = len(messages)
    rows = heads * span
    blocks = rows // BLOCK
    state = jax.ShapeDtypeStruct((rows, LANES), jnp.float32)
    return pl.pallas_call(
        functools.partial(open_kernel, heads, picks),
        in_specs=[SMEM, SMEM] + [VMEM] * (1 + heads + len(early)),
        out_specs=[VMEM] * 5,
        out_shape=[
            state,
            state,
            jax.ShapeDtypeStruct((rows, LANES), jnp.bfloat16),
            state,
            jax.ShapeDtypeStruct((blocks, 2 * rows), jnp.float32),
        ],
        scratch_shapes=[
            pltpu.VMEM((blocks, LANES), jnp.int32),
            pltpu.VMEM((picks, blocks, LANES), jnp.int32),
        ],
        compiler_params=pltpu.CompilerParams(vmem_limit_bytes=24 * MIB),
        cost_estimate=attend_cost(BLOCK // LANES, rows),
    )(near, far, listed, *messages, *early)


def piece_shape(heads, parts, span):
    return jax.ShapeDtypeStruct((heads * parts, span // parts // 2, LANES), jnp.bfloat16)


def more_attend(near, heads, queries, old, kvs, columns, parts):
    rows = queries[0].shape[0]
    span = rows // heads
    return pl.pallas_call(
        functools.partial(more_kernel, heads, columns, parts),
        in_specs=[SMEM] + [VMEM] * (5 + len(kvs)),
        out_specs=VMEM,
        out_shape=piece_shape(heads, parts, span),
        scratch_shapes=[pltpu.VMEM((rows, LANES), jnp.float32)],
        compiler_params=pltpu.CompilerParams(vmem_limit_bytes=24 * MIB),
        cost_estimate=attend_cost(rows, span * len(kvs)),
    )(near, *queries, *old, *kvs)


def whole_attend(near, far, picks, listed, messages, kvs, span, parts):
    heads = len(messages)
    rows = heads * span
    blocks, steps = rows // BLOCK, kvs.shape[0] // rows
    return pl.pallas_call(
        functools.partial(whole_kernel, heads, picks, parts),
        grid=(steps,),
        in_specs=[SMEM, SMEM, VMEM, pl.BlockSpec((rows, LANES), lambda s: (s, 0))] + [VMEM] * heads,
        out_specs=VMEM,
        out_shape=piece_shape(heads, parts, span),
        scratch_shapes=[
            pltpu.VMEM((rows, LANES), jnp.float32),
            pltpu.VMEM((rows, LANES), jnp.float32),
            pltpu.VMEM((rows, LANES), jnp.bfloat16),
            pltpu.VMEM((rows, LANES), jnp.float32),
            pltpu.VMEM((blocks, rows), jnp.float32),
            pltpu.VMEM((blocks, LANES), jnp.int32),
            pltpu.VMEM((picks, blocks, LANES), jnp.int32),
        ],
        compiler_params=pltpu.CompilerParams(vmem_limit_bytes=24 * MIB),
        cost_estimate=attend_cost(rows, kvs.shape[0]),
    )(near, far, listed, kvs, *messages)


def mix_kernel(near_count, order, here_ref, got_ref, *refs):
    parts = len(order)
    low = low_half()
    depth = refs[0].shape[0]
    blocks = []
    for ref in refs[:-1]:
        blocks += [ref.at[first : first + depth, :] for first in range(0, ref.shape[0], depth)]
    total = None
    for i, d in enumerate(order):
        source = here_ref[0] ^ d
        columns = []
        for near in range(0, near_count, 2):
            even, odd = (got_ref[at * parts + source].astype(jnp.float32) for at in (near, near + 1))
            top = jnp.where(low, even, odd)
            bottom = half_turn(jnp.where(low, odd, even))
            columns.append(jnp.concatenate([top, bottom], axis=0).astype(jnp.bfloat16))
        rows = jnp.concatenate(columns, axis=1)
        term = jnp.dot(rows, blocks[i][...], preferred_element_type=jnp.float32)
        total = term if total is None else total + term
    refs[-1][...] = total.astype(refs[-1].dtype)


def mix(here, got, o_blocks, order):
    parts = len(order)
    return pl.pallas_call(
        functools.partial(mix_kernel, got.shape[0] // parts, order),
        out_shape=jax.ShapeDtypeStruct((2 * got.shape[1], o_blocks[0].shape[1]), jnp.bfloat16),
        in_specs=[SMEM] + [VMEM] * (1 + len(o_blocks)),
        out_specs=VMEM,
        compiler_params=pltpu.CompilerParams(vmem_limit_bytes=24 * MIB),
    )(here, got, *o_blocks)


def swapped(block, axis, distance):
    return lax.ppermute(block, axis, [(i, i ^ distance) for i in range(lax.axis_size(axis))])


def shards(tokens, q_weight, k_weight, v_weight, o_weight, rand_blocks, global_pos):
    tok_rows = tokens.shape[0]
    far_count, heads, parts = (lax.axis_size(axis) for axis in ("far", "near", "head"))
    near, far, here = (
        lax.axis_index(axis).astype(jnp.int32).reshape(1) for axis in ("near", "far", "head")
    )
    picks = rand_blocks.shape[1]

    blocks = far_count * heads * tok_rows // BLOCK
    *ready, listed = project(
        near, blocks, global_pos, rand_blocks, tokens, q_weight, k_weight, v_weight
    )
    leaving, sent = ready[:heads], ready[heads:]
    apart = []
    if far_count == 2:
        apart = [swapped(leaving[d], ("far", "near"), heads + d) for d in range(heads)]
    messages = [sent[0]] + [swapped(sent[d], "near", d) for d in range(1, heads)]

    if far_count == 2:
        early = heads - 1
        peaks, sums, *queries = open_attend(
            near, far, picks, listed, messages, apart[:early], tok_rows
        )
        columns = [(heads + d) * tok_rows for d in range(early, heads)]
        pieces = more_attend(near, heads, queries, [peaks, sums], apart[early:], columns, parts)
    else:
        kvs = lax.all_gather(pack(tok_rows, messages), "far", tiled=True)
        pieces = whole_attend(near, far, picks, listed, messages, kvs, tok_rows, parts)

    distance = parts // 2
    o_blocks = [o_weight, swapped(o_weight, "head", distance)]
    order = [0, distance]
    while distance > 1:
        distance //= 2
        o_blocks.append(swapped(gather(o_blocks, [pieces]), "head", distance))
        order = order + [d ^ distance for d in order]
    got = lax.all_to_all(pieces, ("near", "head"), 0, 0, tiled=True)
    return mix(here, got, o_blocks, order)


def solution(mesh):
    count, columns = mesh.devices.shape
    tm = ("far", "near")
    placed = (
        P(tm, None),
        P(None, "head"),
        P(None, "head"),
        P(None, "head"),
        P("head", None),
        P(tm, None),
        P(),
    )

    def run(tokens, q_weight, *rest):
        heads = q_weight.shape[1] // HEAD_DIM // columns
        split = Mesh(mesh.devices.reshape(count // heads, heads, columns), (*tm, "head"))
        body = jax.shard_map(
            shards, mesh=split, in_specs=placed, out_specs=P((*tm, "head"), None), check_vma=False
        )
        return body(tokens, q_weight, *rest)

    return run
```

```python
import functools
import math

import jax
import jax.numpy as jnp
from jax import lax
from jax.experimental import pallas as pl
from jax.experimental.pallas import tpu as pltpu
from jax.sharding import Mesh
from jax.sharding import PartitionSpec as P

HEAD_DIM = 64
BLOCK = 128
LANES = 128
DIGIT_BITS = 7
DIGIT = 1 << DIGIT_BITS
TILE_ROWS = 16
NEVER = -1e30
MIB = 1024 * 1024
VMEM = pl.BlockSpec(memory_space=pltpu.VMEM)
SMEM = pl.BlockSpec(memory_space=pltpu.SMEM)
HBM = pl.BlockSpec(memory_space=pltpu.HBM)
ANY = pl.BlockSpec(memory_space=pl.ANY)


def low_half():
    return lax.broadcasted_iota(jnp.int32, (1, LANES), 1) < HEAD_DIM


def half_turn(block):
    return pltpu.roll(block, HEAD_DIM, 1)


def own_half(near):
    return lax.broadcasted_iota(jnp.int32, (1, LANES), 1) // HEAD_DIM == (near & 1)


def project_kernel(cuts, near_ref, rand_ref, pos_ref, t_hbm, q_hbm, k_hbm, v_hbm, *refs):
    listed_ref, t_ref, q_ref, k_ref, v_ref, all_ref, sems = refs[-7:]
    rows = t_ref.shape[0]
    heads = k_ref.shape[1] // HEAD_DIM
    far_refs, sent_refs = refs[:heads], refs[heads : 2 * heads]
    copies = []
    for i, (source, target) in enumerate(
        ((t_hbm, t_ref), (k_hbm, k_ref), (v_hbm, v_ref), (q_hbm, q_ref))
    ):
        part = source.shape[0] // cuts
        group = []
        for c in range(cuts):
            at = slice(c * part, (c + 1) * part)
            copy = pltpu.make_async_copy(source.at[at, :], target.at[at, :], sems.at[i, c])
            copy.start()
            group.append(copy)
        copies.append(group)

    spots = lax.broadcasted_iota(jnp.int32, listed_ref.shape, 0) * BLOCK
    spots = spots + lax.broadcasted_iota(jnp.int32, listed_ref.shape, 1)
    listed_ref[...] = lax.fori_loop(
        0,
        pos_ref.shape[0],
        lambda i, flags: jnp.where(spots == pos_ref[i], 1.0, flags),
        jnp.zeros(listed_ref.shape, jnp.float32),
        unroll=16,
    )

    def product(i, weight_ref):
        for copy in copies[i]:
            copy.wait()
        return jnp.dot(t_ref[...], weight_ref[...], preferred_element_type=jnp.float32)

    for copy in copies[0]:
        copy.wait()
    low = low_half()
    k = product(1, k_ref)
    v = product(2, v_ref)
    for pair in range(heads // 2):
        at = slice(pair * LANES, (pair + 1) * LANES)
        key, value = k[:, at], half_turn(v[:, at])
        all_ref[2 * pair, :rows, :] = jnp.where(low, key, value).astype(jnp.bfloat16)
        all_ref[2 * pair + 1, :rows, :] = jnp.where(low, value, key).astype(jnp.bfloat16)
    q = product(3, q_ref)
    for pair in range(heads // 2):
        at = slice(pair * LANES, (pair + 1) * LANES)
        top, bottom = q[: rows // 2, at], half_turn(q[rows // 2 :, at])
        all_ref[2 * pair, rows:, :] = jnp.where(low, top, bottom).astype(jnp.bfloat16)
        all_ref[2 * pair + 1, rows:, :] = jnp.where(low, bottom, top).astype(jnp.bfloat16)
    near = near_ref[0]
    digit_rows = sent_refs[0].shape[0] - rows - rows // 2
    row = lax.broadcasted_iota(jnp.int32, (digit_rows, LANES), 0)
    digits = jnp.zeros((digit_rows, LANES), jnp.float32)
    picks = rand_ref.shape[1]
    for j in range(rand_ref.shape[0]):
        for r in range(picks):
            at = 2 * (j * picks + r)
            value = rand_ref[j, r]
            digits = jnp.where(row == at, (value >> DIGIT_BITS).astype(jnp.float32), digits)
            digits = jnp.where(row == at + 1, (value & (DIGIT - 1)).astype(jnp.float32), digits)
    digits = digits.astype(jnp.bfloat16)
    for d in range(heads):
        far_refs[d][...] = all_ref[near ^ d, :rows, :]
        sent_refs[d][: rows + rows // 2, :] = all_ref[near ^ d]
        sent_refs[d][rows + rows // 2 :, :] = digits


def project(near, blocks, global_pos, rand_blocks, tokens, q_weight, k_weight, v_weight):
    rows, depth = tokens.shape
    feats = k_weight.shape[1]
    heads = feats // HEAD_DIM
    cuts = 2
    message = rows + rows // 2
    digit_rows = -(-2 * rand_blocks.size // TILE_ROWS) * TILE_ROWS
    pinned = [
        pltpu.with_memory_space_constraint(array, pltpu.HBM)
        for array in (rand_blocks, global_pos, q_weight, k_weight, v_weight)
    ]
    return pl.pallas_call(
        functools.partial(project_kernel, cuts),
        in_specs=[SMEM, SMEM, SMEM, HBM, HBM, HBM, HBM],
        out_specs=[VMEM] * (2 * heads + 1),
        out_shape=[jax.ShapeDtypeStruct((rows, LANES), jnp.bfloat16)] * heads
        + [jax.ShapeDtypeStruct((message + digit_rows, LANES), jnp.bfloat16)] * heads
        + [jax.ShapeDtypeStruct((blocks, LANES), jnp.float32)],
        scratch_shapes=[
            pltpu.VMEM((rows, depth), jnp.bfloat16),
            pltpu.VMEM((depth, feats), jnp.bfloat16),
            pltpu.VMEM((depth, feats), jnp.bfloat16),
            pltpu.VMEM((depth, feats), jnp.bfloat16),
            pltpu.VMEM((heads, message, LANES), jnp.bfloat16),
            pltpu.SemaphoreType.DMA((4, cuts)),
        ],
        compiler_params=pltpu.CompilerParams(vmem_limit_bytes=24 * MIB),
        cost_estimate=pl.CostEstimate(
            flops=6 * rows * depth * feats, bytes_accessed=2 * depth * (rows + 3 * feats), transcendentals=0
        ),
    )(near, *pinned[:2], tokens, *pinned[2:])


def pack_kernel(*refs):
    out_ref = refs[-1]
    rows = out_ref.shape[0] // (len(refs) - 1)
    for i, ref in enumerate(refs[:-1]):
        out_ref[i * rows : (i + 1) * rows, :] = ref[:rows, :]


def pack(rows, messages):
    return pl.pallas_call(
        pack_kernel,
        in_specs=[VMEM] * len(messages),
        out_specs=VMEM,
        out_shape=jax.ShapeDtypeStruct((rows * len(messages), LANES), jnp.bfloat16),
        compiler_params=pltpu.CompilerParams(vmem_limit_bytes=32 * MIB),
    )(*messages)


def gather_kernel(count, *refs):
    out_ref, sems = refs[-2:]
    first, copies = 0, []
    for i, ref in enumerate(refs[:count]):
        at = slice(first, first + ref.shape[0])
        copies.append(pltpu.make_async_copy(ref, out_ref.at[at, :], sems.at[i]))
        first += ref.shape[0]
    for copy in copies:
        copy.start()
    for copy in copies:
        copy.wait()


def gather(blocks, after):
    rows = sum(block.shape[0] for block in blocks)
    return pl.pallas_call(
        functools.partial(gather_kernel, len(blocks)),
        in_specs=[ANY] * (len(blocks) + len(after)),
        out_specs=VMEM,
        out_shape=jax.ShapeDtypeStruct((rows, blocks[0].shape[1]), blocks[0].dtype),
        scratch_shapes=[pltpu.SemaphoreType.DMA((len(blocks),))],
        compiler_params=pltpu.CompilerParams(vmem_limit_bytes=24 * MIB),
    )(*blocks, *after)


def prepare(heads, picks, near, far, span, messages, listed_ref, q_ref, free_ref, block_ref, pick_ref):
    per_shard = span // BLOCK
    mine = own_half(near)
    for d in range(heads):
        packed = messages[d][span : span + span // 2, :].astype(jnp.float32)
        top = jnp.where(mine, packed, 0.0)
        bottom = jnp.where(mine, half_turn(packed), 0.0)
        q_ref[d * span : d * span + span // 2, :] = top.astype(q_ref.dtype)
        q_ref[d * span + span // 2 : (d + 1) * span, :] = bottom.astype(q_ref.dtype)
        rand = messages[d][span + span // 2 :, :].astype(jnp.float32)
        for j in range(per_shard):
            row = slice(d * per_shard + j, d * per_shard + j + 1)
            block = (far * heads + (near ^ d)) * per_shard + j
            block_ref[row, :] = jnp.full((1, LANES), block, jnp.int32)
            flags = jnp.broadcast_to(listed_ref[pl.ds(block, 1), :], (BLOCK, BLOCK))
            at = (d * per_shard + j) * BLOCK
            free_ref[at : at + BLOCK, :] = 1.0 - jnp.transpose(flags)
            for r in range(picks):
                at = 2 * (j * picks + r)
                pick = rand[at : at + 1, :] * DIGIT + rand[at + 1 : at + 2, :]
                pick_ref[r, row, :] = pick.astype(jnp.int32)


def fill_bias(heads, groups, near, listed_ref, block_ref, pick_ref, bias_ref):
    per_shard = block_ref.shape[0] // heads
    blocks = block_ref[...]
    picks = [pick_ref[r] for r in range(pick_ref.shape[0])]
    for g, there in enumerate(groups):
        for d in range(heads):
            for b in range(per_shard):
                key_block = (there * heads + (near ^ d)) * per_shard + b
                away = key_block - blocks
                times = listed_ref[pl.ds(key_block, 1), :] + jnp.where((away >= -2) & (away <= 1), 1.0, 0.0)
                for pick in picks:
                    times = times + jnp.where(pick == key_block, 1.0, 0.0)
                at = ((g * heads + d) * per_shard + b) * BLOCK
                bias_ref[:, at : at + BLOCK] = jnp.where(
                    times > 0, jnp.log2(jnp.maximum(times, 1.0)), NEVER
                )


def attend_rows(near, tile, span, q_ref, free_ref, bias_ref, keys, peak, total):
    per_shard = span // BLOCK
    scale = HEAD_DIM ** (-0.5) * math.log2(math.e)
    mine = own_half(near)
    q = q_ref[tile * span : (tile + 1) * span, :]
    scores = [[] for _ in range(per_shard)]
    for key_ref, first, column in keys:
        s = lax.dot_general(
            q,
            key_ref[first : first + span, :],
            (((1,), (1,)), ((), ())),
            preferred_element_type=jnp.float32,
        )
        for j in range(per_shard):
            block = tile * per_shard + j
            free = free_ref[block * BLOCK : (block + 1) * BLOCK, :]
            for b in range(per_shard):
                bias = bias_ref[block : block + 1, column + b * BLOCK : column + (b + 1) * BLOCK]
                part = s[j * BLOCK : (j + 1) * BLOCK, b * BLOCK : (b + 1) * BLOCK]
                scores[j].append(part * scale + free * bias)
    peaks, weights = [], []
    for j in range(per_shard):
        best = jnp.max(functools.reduce(jnp.maximum, scores[j]), axis=1, keepdims=True)
        best = jnp.broadcast_to(best, (BLOCK, LANES))
        if peak is not None:
            best = jnp.maximum(peak[j * BLOCK : (j + 1) * BLOCK, :], best)
        peaks.append(best)
        weights.append([jnp.exp2(part - best).astype(jnp.bfloat16) for part in scores[j]])
    new = jnp.concatenate(peaks, axis=0)
    if total is not None:
        total = total * jnp.exp2(peak - new)
    for i, (key_ref, first, _) in enumerate(keys):
        e = jnp.concatenate(
            [
                jnp.concatenate(weights[j][i * per_shard : (i + 1) * per_shard], axis=1)
                for j in range(per_shard)
            ],
            axis=0,
        )
        v = jnp.where(mine, jnp.ones((), jnp.bfloat16), key_ref[first : first + span, :])
        term = jnp.dot(e, v, preferred_element_type=jnp.float32)
        total = term if total is None else total + term
    return new, total


def finish(heads, parts, near, span, sums, out_ref):
    mine = own_half(near)
    piece = span // parts
    for d in range(heads):
        for part in range(parts):
            first = d * span + part * piece
            top = sums[first : first + piece // 2, :]
            bottom = sums[first + piece // 2 : first + piece, :]
            values = jnp.where(mine, half_turn(top), bottom)
            totals = jnp.where(mine, top, half_turn(bottom))
            out_ref[(near ^ d) * parts + part] = (values / totals).astype(out_ref.dtype)


def open_kernel(heads, picks, near_ref, far_ref, listed_ref, *refs):
    messages, refs = refs[:heads], refs[heads:]
    peaks, sums, q_ref, free_ref, bias_ref, block_ref, pick_ref = refs
    span = q_ref.shape[0] // heads
    near, far = near_ref[0], far_ref[0]
    prepare(heads, picks, near, far, span, messages, listed_ref, q_ref, free_ref, block_ref, pick_ref)
    fill_bias(heads, [far, far ^ 1], near, listed_ref, block_ref, pick_ref, bias_ref)
    keys = [(messages[d], 0, d * span) for d in range(heads)]
    for tile in range(heads):
        rows = slice(tile * span, (tile + 1) * span)
        peaks[rows, :], sums[rows, :] = attend_rows(
            near, tile, span, q_ref, free_ref, bias_ref, keys, None, None
        )


def more_kernel(heads, columns, parts, near_ref, q_ref, free_ref, bias_ref, peak_in, sum_in, *refs):
    kv_refs, refs = refs[: len(columns)], refs[len(columns) :]
    if parts:
        out_ref, sums = refs
        peaks = None
    else:
        peaks, sums = refs
    span = q_ref.shape[0] // heads
    near = near_ref[0]
    keys = [(ref, 0, column) for ref, column in zip(kv_refs, columns)]
    for tile in range(heads):
        rows = slice(tile * span, (tile + 1) * span)
        new, sums[rows, :] = attend_rows(
            near, tile, span, q_ref, free_ref, bias_ref, keys, peak_in[rows, :], sum_in[rows, :]
        )
        if peaks is not None:
            peaks[rows, :] = new
    if parts:
        finish(heads, parts, near, span, sums, out_ref)


def whole_kernel(heads, picks, parts, near_ref, far_ref, listed_ref, kv_ref, *refs):
    messages, refs = refs[:heads], refs[heads:]
    out_ref, peaks, sums, q_ref, free_ref, bias_ref, block_ref, pick_ref = refs
    span = q_ref.shape[0] // heads
    near, far = near_ref[0], far_ref[0]
    step = pl.program_id(0)

    @pl.when(step == 0)
    def _():
        peaks[...] = jnp.full_like(peaks, NEVER)
        sums[...] = jnp.zeros_like(sums)
        prepare(heads, picks, near, far, span, messages, listed_ref, q_ref, free_ref, block_ref, pick_ref)

    fill_bias(heads, [step], near, listed_ref, block_ref, pick_ref, bias_ref)
    keys = [(kv_ref, d * span, d * span) for d in range(heads)]
    for tile in range(heads):
        rows = slice(tile * span, (tile + 1) * span)
        peaks[rows, :], sums[rows, :] = attend_rows(
            near, tile, span, q_ref, free_ref, bias_ref, keys, peaks[rows, :], sums[rows, :]
        )

    @pl.when(step == pl.num_programs(0) - 1)
    def _():
        finish(heads, parts, near, span, sums, out_ref)


def attend_cost(rows, keys):
    return pl.CostEstimate(
        flops=4 * rows * keys * LANES, bytes_accessed=4 * (rows + keys) * LANES, transcendentals=rows * keys
    )


def open_attend(near, far, picks, listed, messages, span):
    heads = len(messages)
    rows = heads * span
    blocks = rows // BLOCK
    state = jax.ShapeDtypeStruct((rows, LANES), jnp.float32)
    return pl.pallas_call(
        functools.partial(open_kernel, heads, picks),
        in_specs=[SMEM, SMEM] + [VMEM] * (1 + heads),
        out_specs=[VMEM] * 5,
        out_shape=[
            state,
            state,
            jax.ShapeDtypeStruct((rows, LANES), jnp.bfloat16),
            state,
            jax.ShapeDtypeStruct((blocks, 2 * rows), jnp.float32),
        ],
        scratch_shapes=[
            pltpu.VMEM((blocks, LANES), jnp.int32),
            pltpu.VMEM((picks, blocks, LANES), jnp.int32),
        ],
        compiler_params=pltpu.CompilerParams(vmem_limit_bytes=24 * MIB),
        cost_estimate=attend_cost(rows, rows),
    )(near, far, listed, *messages)


def piece_shape(heads, parts, span):
    return jax.ShapeDtypeStruct((heads * parts, span // parts // 2, LANES), jnp.bfloat16)


def more_attend(near, heads, queries, old, kvs, columns, parts):
    rows = queries[0].shape[0]
    span = rows // heads
    state = jax.ShapeDtypeStruct((rows, LANES), jnp.float32)
    if parts:
        out_shape, out_specs = piece_shape(heads, parts, span), VMEM
        scratch = [pltpu.VMEM(state.shape, state.dtype)]
    else:
        out_shape, out_specs, scratch = [state] * 2, [VMEM] * 2, []
    return pl.pallas_call(
        functools.partial(more_kernel, heads, columns, parts),
        in_specs=[SMEM] + [VMEM] * (5 + len(kvs)),
        out_specs=out_specs,
        out_shape=out_shape,
        scratch_shapes=scratch,
        compiler_params=pltpu.CompilerParams(vmem_limit_bytes=24 * MIB),
        cost_estimate=attend_cost(rows, span * len(kvs)),
    )(near, *queries, *old, *kvs)


def whole_attend(near, far, picks, listed, messages, kvs, span, parts):
    heads = len(messages)
    rows = heads * span
    blocks, steps = rows // BLOCK, kvs.shape[0] // rows
    return pl.pallas_call(
        functools.partial(whole_kernel, heads, picks, parts),
        grid=(steps,),
        in_specs=[SMEM, SMEM, VMEM, pl.BlockSpec((rows, LANES), lambda s: (s, 0))] + [VMEM] * heads,
        out_specs=VMEM,
        out_shape=piece_shape(heads, parts, span),
        scratch_shapes=[
            pltpu.VMEM((rows, LANES), jnp.float32),
            pltpu.VMEM((rows, LANES), jnp.float32),
            pltpu.VMEM((rows, LANES), jnp.bfloat16),
            pltpu.VMEM((rows, LANES), jnp.float32),
            pltpu.VMEM((blocks, rows), jnp.float32),
            pltpu.VMEM((blocks, LANES), jnp.int32),
            pltpu.VMEM((picks, blocks, LANES), jnp.int32),
        ],
        compiler_params=pltpu.CompilerParams(vmem_limit_bytes=24 * MIB),
        cost_estimate=attend_cost(rows, kvs.shape[0]),
    )(near, far, listed, kvs, *messages)


def mix_kernel(near_count, order, here_ref, got_ref, *refs):
    parts = len(order)
    low = low_half()
    depth = refs[0].shape[0]
    blocks = []
    for ref in refs[:-1]:
        blocks += [ref.at[first : first + depth, :] for first in range(0, ref.shape[0], depth)]
    total = None
    for i, d in enumerate(order):
        source = here_ref[0] ^ d
        columns = []
        for near in range(0, near_count, 2):
            even, odd = (got_ref[at * parts + source].astype(jnp.float32) for at in (near, near + 1))
            top = jnp.where(low, even, odd)
            bottom = half_turn(jnp.where(low, odd, even))
            columns.append(jnp.concatenate([top, bottom], axis=0).astype(jnp.bfloat16))
        rows = jnp.concatenate(columns, axis=1)
        term = jnp.dot(rows, blocks[i][...], preferred_element_type=jnp.float32)
        total = term if total is None else total + term
    refs[-1][...] = total.astype(refs[-1].dtype)


def mix(here, got, o_blocks, order):
    parts = len(order)
    return pl.pallas_call(
        functools.partial(mix_kernel, got.shape[0] // parts, order),
        out_shape=jax.ShapeDtypeStruct((2 * got.shape[1], o_blocks[0].shape[1]), jnp.bfloat16),
        in_specs=[SMEM] + [VMEM] * (1 + len(o_blocks)),
        out_specs=VMEM,
        compiler_params=pltpu.CompilerParams(vmem_limit_bytes=24 * MIB),
    )(here, got, *o_blocks)


def swapped(block, axis, distance):
    return lax.ppermute(block, axis, [(i, i ^ distance) for i in range(lax.axis_size(axis))])


def shards(tokens, q_weight, k_weight, v_weight, o_weight, rand_blocks, global_pos):
    tok_rows = tokens.shape[0]
    far_count, heads, parts = (lax.axis_size(axis) for axis in ("far", "near", "head"))
    near, far, here = (
        lax.axis_index(axis).astype(jnp.int32).reshape(1) for axis in ("near", "far", "head")
    )
    picks = rand_blocks.shape[1]

    blocks = far_count * heads * tok_rows // BLOCK
    *ready, listed = project(
        near, blocks, global_pos, rand_blocks, tokens, q_weight, k_weight, v_weight
    )
    leaving, sent = ready[:heads], ready[heads:]
    messages = [sent[0]] + [swapped(sent[d], "near", d) for d in range(1, heads)]

    if far_count == 2:
        apart = [swapped(leaving[d], ("far", "near"), heads + d) for d in range(heads)]
        peaks, sums, *queries = open_attend(near, far, picks, listed, messages, tok_rows)
        columns = [(heads + d) * tok_rows for d in range(heads)]
        more = functools.partial(more_attend, near, heads, queries)
        old = more([peaks, sums], apart[:-1], columns[:-1], 0)
        pieces = more(old, apart[-1:], columns[-1:], parts)
    else:
        kvs = lax.all_gather(pack(tok_rows, messages), "far", tiled=True)
        pieces = whole_attend(near, far, picks, listed, messages, kvs, tok_rows, parts)

    distance = parts // 2
    o_blocks = [o_weight, swapped(o_weight, "head", distance)]
    order = [0, distance]
    while distance > 1:
        distance //= 2
        o_blocks.append(swapped(gather(o_blocks, [pieces]), "head", distance))
        order = order + [d ^ distance for d in order]
    got = lax.all_to_all(pieces, ("near", "head"), 0, 0, tiled=True)
    return mix(here, got, o_blocks, order)


def solution(mesh):
    count, columns = mesh.devices.shape
    tm = ("far", "near")
    placed = (
        P(tm, None),
        P(None, "head"),
        P(None, "head"),
        P(None, "head"),
        P("head", None),
        P(tm, None),
        P(),
    )

    def run(tokens, q_weight, *rest):
        heads = q_weight.shape[1] // HEAD_DIM // columns
        split = Mesh(mesh.devices.reshape(count // heads, heads, columns), (*tm, "head"))
        body = jax.shard_map(
            shards, mesh=split, in_specs=placed, out_specs=P((*tm, "head"), None), check_vma=False
        )
        return body(tokens, q_weight, *rest)

    return run
```

```python
import functools
import math

import jax
import jax.numpy as jnp
from jax import lax
from jax.experimental import pallas as pl
from jax.experimental.pallas import tpu as pltpu
from jax.sharding import Mesh
from jax.sharding import PartitionSpec as P

HEAD_DIM = 64
BLOCK = 128
LANES = 128
DIGIT_BITS = 7
DIGIT = 1 << DIGIT_BITS
TILE_ROWS = 16
NEVER = -1e30
MIB = 1024 * 1024
VMEM = pl.BlockSpec(memory_space=pltpu.VMEM)
SMEM = pl.BlockSpec(memory_space=pltpu.SMEM)
HBM = pl.BlockSpec(memory_space=pltpu.HBM)
ANY = pl.BlockSpec(memory_space=pl.ANY)


def low_half():
    return lax.broadcasted_iota(jnp.int32, (1, LANES), 1) < HEAD_DIM


def half_turn(block):
    return pltpu.roll(block, HEAD_DIM, 1)


def own_half(near):
    return lax.broadcasted_iota(jnp.int32, (1, LANES), 1) // HEAD_DIM == (near & 1)


def project_kernel(cuts, near_ref, rand_hbm, pos_hbm, t_hbm, q_hbm, k_hbm, v_hbm, *refs):
    listed_ref, t_ref, q_ref, k_ref, v_ref, all_ref, rand_ref, pos_ref, sems, few_sems = refs[-10:]
    rows = t_ref.shape[0]
    heads = k_ref.shape[1] // HEAD_DIM
    far_refs, sent_refs = refs[:heads], refs[heads : 2 * heads]
    few = [
        pltpu.make_async_copy(pos_hbm, pos_ref, few_sems.at[0]),
        pltpu.make_async_copy(rand_hbm, rand_ref, few_sems.at[1]),
    ]
    for copy in few:
        copy.start()
    copies = []
    for i, (source, target) in enumerate(
        ((t_hbm, t_ref), (k_hbm, k_ref), (v_hbm, v_ref), (q_hbm, q_ref))
    ):
        part = source.shape[0] // cuts
        group = []
        for c in range(cuts):
            at = slice(c * part, (c + 1) * part)
            copy = pltpu.make_async_copy(source.at[at, :], target.at[at, :], sems.at[i, c])
            copy.start()
            group.append(copy)
        copies.append(group)

    for copy in few:
        copy.wait()
    spots = lax.broadcasted_iota(jnp.int32, listed_ref.shape, 0) * BLOCK
    spots = spots + lax.broadcasted_iota(jnp.int32, listed_ref.shape, 1)
    listed_ref[...] = lax.fori_loop(
        0,
        pos_ref.shape[0],
        lambda i, flags: jnp.where(spots == pos_ref[i], 1.0, flags),
        jnp.zeros(listed_ref.shape, jnp.float32),
        unroll=16,
    )

    def product(i, weight_ref):
        for copy in copies[i]:
            copy.wait()
        return jnp.dot(t_ref[...], weight_ref[...], preferred_element_type=jnp.float32)

    for copy in copies[0]:
        copy.wait()
    low = low_half()
    k = product(1, k_ref)
    v = product(2, v_ref)
    for pair in range(heads // 2):
        at = slice(pair * LANES, (pair + 1) * LANES)
        key, value = k[:, at], half_turn(v[:, at])
        all_ref[2 * pair, :rows, :] = jnp.where(low, key, value).astype(jnp.bfloat16)
        all_ref[2 * pair + 1, :rows, :] = jnp.where(low, value, key).astype(jnp.bfloat16)
    q = product(3, q_ref)
    for pair in range(heads // 2):
        at = slice(pair * LANES, (pair + 1) * LANES)
        top, bottom = q[: rows // 2, at], half_turn(q[rows // 2 :, at])
        all_ref[2 * pair, rows:, :] = jnp.where(low, top, bottom).astype(jnp.bfloat16)
        all_ref[2 * pair + 1, rows:, :] = jnp.where(low, bottom, top).astype(jnp.bfloat16)
    near = near_ref[0]
    digit_rows = sent_refs[0].shape[0] - rows - rows // 2
    row = lax.broadcasted_iota(jnp.int32, (digit_rows, LANES), 0)
    digits = jnp.zeros((digit_rows, LANES), jnp.float32)
    picks = rand_ref.shape[1]
    for j in range(rand_ref.shape[0]):
        for r in range(picks):
            at = 2 * (j * picks + r)
            value = rand_ref[j, r]
            digits = jnp.where(row == at, (value >> DIGIT_BITS).astype(jnp.float32), digits)
            digits = jnp.where(row == at + 1, (value & (DIGIT - 1)).astype(jnp.float32), digits)
    digits = digits.astype(jnp.bfloat16)
    for d in range(heads):
        far_refs[d][...] = all_ref[near ^ d, :rows, :]
        sent_refs[d][: rows + rows // 2, :] = all_ref[near ^ d]
        sent_refs[d][rows + rows // 2 :, :] = digits


def project(near, blocks, global_pos, rand_blocks, tokens, q_weight, k_weight, v_weight):
    rows, depth = tokens.shape
    feats = k_weight.shape[1]
    heads = feats // HEAD_DIM
    cuts = 2
    message = rows + rows // 2
    digit_rows = -(-2 * rand_blocks.size // TILE_ROWS) * TILE_ROWS
    pinned = [
        pltpu.with_memory_space_constraint(array, pltpu.HBM)
        for array in (rand_blocks, global_pos, tokens, q_weight, k_weight, v_weight)
    ]
    return pl.pallas_call(
        functools.partial(project_kernel, cuts),
        in_specs=[SMEM] + [HBM] * 6,
        out_specs=[VMEM] * (2 * heads + 1),
        out_shape=[jax.ShapeDtypeStruct((rows, LANES), jnp.bfloat16)] * heads
        + [jax.ShapeDtypeStruct((message + digit_rows, LANES), jnp.bfloat16)] * heads
        + [jax.ShapeDtypeStruct((blocks, LANES), jnp.float32)],
        scratch_shapes=[
            pltpu.VMEM((rows, depth), jnp.bfloat16),
            pltpu.VMEM((depth, feats), jnp.bfloat16),
            pltpu.VMEM((depth, feats), jnp.bfloat16),
            pltpu.VMEM((depth, feats), jnp.bfloat16),
            pltpu.VMEM((heads, message, LANES), jnp.bfloat16),
            pltpu.SMEM(rand_blocks.shape, jnp.int32),
            pltpu.SMEM(global_pos.shape, jnp.int32),
            pltpu.SemaphoreType.DMA((4, cuts)),
            pltpu.SemaphoreType.DMA((2,)),
        ],
        compiler_params=pltpu.CompilerParams(vmem_limit_bytes=24 * MIB),
        cost_estimate=pl.CostEstimate(
            flops=6 * rows * depth * feats, bytes_accessed=2 * depth * (rows + 3 * feats), transcendentals=0
        ),
    )(near, *pinned)


def pack_kernel(*refs):
    out_ref = refs[-1]
    rows = out_ref.shape[0] // (len(refs) - 1)
    for i, ref in enumerate(refs[:-1]):
        out_ref[i * rows : (i + 1) * rows, :] = ref[:rows, :]


def pack(rows, messages):
    return pl.pallas_call(
        pack_kernel,
        in_specs=[VMEM] * len(messages),
        out_specs=VMEM,
        out_shape=jax.ShapeDtypeStruct((rows * len(messages), LANES), jnp.bfloat16),
        compiler_params=pltpu.CompilerParams(vmem_limit_bytes=32 * MIB),
    )(*messages)


def gather_kernel(count, *refs):
    out_ref, sems = refs[-2:]
    first, copies = 0, []
    for i, ref in enumerate(refs[:count]):
        at = slice(first, first + ref.shape[0])
        copies.append(pltpu.make_async_copy(ref, out_ref.at[at, :], sems.at[i]))
        first += ref.shape[0]
    for copy in copies:
        copy.start()
    for copy in copies:
        copy.wait()


def gather(blocks, after):
    rows = sum(block.shape[0] for block in blocks)
    return pl.pallas_call(
        functools.partial(gather_kernel, len(blocks)),
        in_specs=[ANY] * (len(blocks) + len(after)),
        out_specs=VMEM,
        out_shape=jax.ShapeDtypeStruct((rows, blocks[0].shape[1]), blocks[0].dtype),
        scratch_shapes=[pltpu.SemaphoreType.DMA((len(blocks),))],
        compiler_params=pltpu.CompilerParams(vmem_limit_bytes=24 * MIB),
    )(*blocks, *after)


def prepare(heads, picks, near, far, span, messages, listed_ref, q_ref, free_ref, block_ref, pick_ref):
    per_shard = span // BLOCK
    mine = own_half(near)
    for d in range(heads):
        packed = messages[d][span : span + span // 2, :].astype(jnp.float32)
        top = jnp.where(mine, packed, 0.0)
        bottom = jnp.where(mine, half_turn(packed), 0.0)
        q_ref[d * span : d * span + span // 2, :] = top.astype(q_ref.dtype)
        q_ref[d * span + span // 2 : (d + 1) * span, :] = bottom.astype(q_ref.dtype)
        rand = messages[d][span + span // 2 :, :].astype(jnp.float32)
        for j in range(per_shard):
            row = slice(d * per_shard + j, d * per_shard + j + 1)
            block = (far * heads + (near ^ d)) * per_shard + j
            block_ref[row, :] = jnp.full((1, LANES), block, jnp.int32)
            flags = jnp.broadcast_to(listed_ref[pl.ds(block, 1), :], (BLOCK, BLOCK))
            at = (d * per_shard + j) * BLOCK
            free_ref[at : at + BLOCK, :] = 1.0 - jnp.transpose(flags)
            for r in range(picks):
                at = 2 * (j * picks + r)
                pick = rand[at : at + 1, :] * DIGIT + rand[at + 1 : at + 2, :]
                pick_ref[r, row, :] = pick.astype(jnp.int32)


def fill_bias(heads, groups, near, listed_ref, block_ref, pick_ref, bias_ref):
    per_shard = block_ref.shape[0] // heads
    blocks = block_ref[...]
    picks = [pick_ref[r] for r in range(pick_ref.shape[0])]
    for g, there in enumerate(groups):
        for d in range(heads):
            for b in range(per_shard):
                key_block = (there * heads + (near ^ d)) * per_shard + b
                away = key_block - blocks
                times = listed_ref[pl.ds(key_block, 1), :] + jnp.where((away >= -2) & (away <= 1), 1.0, 0.0)
                for pick in picks:
                    times = times + jnp.where(pick == key_block, 1.0, 0.0)
                at = ((g * heads + d) * per_shard + b) * BLOCK
                bias_ref[:, at : at + BLOCK] = jnp.where(
                    times > 0, jnp.log2(jnp.maximum(times, 1.0)), NEVER
                )


def attend_rows(near, tile, span, q_ref, free_ref, bias_ref, keys, peak, total):
    per_shard = span // BLOCK
    scale = HEAD_DIM ** (-0.5) * math.log2(math.e)
    mine = own_half(near)
    q = q_ref[tile * span : (tile + 1) * span, :]
    scores = [[] for _ in range(per_shard)]
    for key_ref, first, column in keys:
        s = lax.dot_general(
            q,
            key_ref[first : first + span, :],
            (((1,), (1,)), ((), ())),
            preferred_element_type=jnp.float32,
        )
        for j in range(per_shard):
            block = tile * per_shard + j
            free = free_ref[block * BLOCK : (block + 1) * BLOCK, :]
            for b in range(per_shard):
                bias = bias_ref[block : block + 1, column + b * BLOCK : column + (b + 1) * BLOCK]
                part = s[j * BLOCK : (j + 1) * BLOCK, b * BLOCK : (b + 1) * BLOCK]
                scores[j].append(part * scale + free * bias)
    peaks, weights = [], []
    for j in range(per_shard):
        best = jnp.max(functools.reduce(jnp.maximum, scores[j]), axis=1, keepdims=True)
        best = jnp.broadcast_to(best, (BLOCK, LANES))
        if peak is not None:
            best = jnp.maximum(peak[j * BLOCK : (j + 1) * BLOCK, :], best)
        peaks.append(best)
        weights.append([jnp.exp2(part - best).astype(jnp.bfloat16) for part in scores[j]])
    new = jnp.concatenate(peaks, axis=0)
    if total is not None:
        total = total * jnp.exp2(peak - new)
    for i, (key_ref, first, _) in enumerate(keys):
        e = jnp.concatenate(
            [
                jnp.concatenate(weights[j][i * per_shard : (i + 1) * per_shard], axis=1)
                for j in range(per_shard)
            ],
            axis=0,
        )
        v = jnp.where(mine, jnp.ones((), jnp.bfloat16), key_ref[first : first + span, :])
        term = jnp.dot(e, v, preferred_element_type=jnp.float32)
        total = term if total is None else total + term
    return new, total


def finish(heads, parts, near, span, sums, out_ref):
    mine = own_half(near)
    piece = span // parts
    for d in range(heads):
        for part in range(parts):
            first = d * span + part * piece
            top = sums[first : first + piece // 2, :]
            bottom = sums[first + piece // 2 : first + piece, :]
            values = jnp.where(mine, half_turn(top), bottom)
            totals = jnp.where(mine, top, half_turn(bottom))
            out_ref[(near ^ d) * parts + part] = (values / totals).astype(out_ref.dtype)


def open_kernel(heads, picks, near_ref, far_ref, listed_ref, *refs):
    messages, refs = refs[:heads], refs[heads:]
    peaks, sums, q_ref, free_ref, bias_ref, block_ref, pick_ref = refs
    span = q_ref.shape[0] // heads
    near, far = near_ref[0], far_ref[0]
    prepare(heads, picks, near, far, span, messages, listed_ref, q_ref, free_ref, block_ref, pick_ref)
    fill_bias(heads, [far, far ^ 1], near, listed_ref, block_ref, pick_ref, bias_ref)
    keys = [(messages[d], 0, d * span) for d in range(heads)]
    for tile in range(heads):
        rows = slice(tile * span, (tile + 1) * span)
        peaks[rows, :], sums[rows, :] = attend_rows(
            near, tile, span, q_ref, free_ref, bias_ref, keys, None, None
        )


def more_kernel(heads, columns, parts, near_ref, q_ref, free_ref, bias_ref, peak_in, sum_in, *refs):
    kv_refs, refs = refs[: len(columns)], refs[len(columns) :]
    if parts:
        out_ref, sums = refs
        peaks = None
    else:
        peaks, sums = refs
    span = q_ref.shape[0] // heads
    near = near_ref[0]
    keys = [(ref, 0, column) for ref, column in zip(kv_refs, columns)]
    for tile in range(heads):
        rows = slice(tile * span, (tile + 1) * span)
        new, sums[rows, :] = attend_rows(
            near, tile, span, q_ref, free_ref, bias_ref, keys, peak_in[rows, :], sum_in[rows, :]
        )
        if peaks is not None:
            peaks[rows, :] = new
    if parts:
        finish(heads, parts, near, span, sums, out_ref)


def whole_kernel(heads, picks, parts, near_ref, far_ref, listed_ref, kv_ref, *refs):
    messages, refs = refs[:heads], refs[heads:]
    out_ref, peaks, sums, q_ref, free_ref, bias_ref, block_ref, pick_ref = refs
    span = q_ref.shape[0] // heads
    near, far = near_ref[0], far_ref[0]
    step = pl.program_id(0)

    @pl.when(step == 0)
    def _():
        peaks[...] = jnp.full_like(peaks, NEVER)
        sums[...] = jnp.zeros_like(sums)
        prepare(heads, picks, near, far, span, messages, listed_ref, q_ref, free_ref, block_ref, pick_ref)

    fill_bias(heads, [step], near, listed_ref, block_ref, pick_ref, bias_ref)
    keys = [(kv_ref, d * span, d * span) for d in range(heads)]
    for tile in range(heads):
        rows = slice(tile * span, (tile + 1) * span)
        peaks[rows, :], sums[rows, :] = attend_rows(
            near, tile, span, q_ref, free_ref, bias_ref, keys, peaks[rows, :], sums[rows, :]
        )

    @pl.when(step == pl.num_programs(0) - 1)
    def _():
        finish(heads, parts, near, span, sums, out_ref)


def attend_cost(rows, keys):
    return pl.CostEstimate(
        flops=4 * rows * keys * LANES, bytes_accessed=4 * (rows + keys) * LANES, transcendentals=rows * keys
    )


def open_attend(near, far, picks, listed, messages, span):
    heads = len(messages)
    rows = heads * span
    blocks = rows // BLOCK
    state = jax.ShapeDtypeStruct((rows, LANES), jnp.float32)
    return pl.pallas_call(
        functools.partial(open_kernel, heads, picks),
        in_specs=[SMEM, SMEM] + [VMEM] * (1 + heads),
        out_specs=[VMEM] * 5,
        out_shape=[
            state,
            state,
            jax.ShapeDtypeStruct((rows, LANES), jnp.bfloat16),
            state,
            jax.ShapeDtypeStruct((blocks, 2 * rows), jnp.float32),
        ],
        scratch_shapes=[
            pltpu.VMEM((blocks, LANES), jnp.int32),
            pltpu.VMEM((picks, blocks, LANES), jnp.int32),
        ],
        compiler_params=pltpu.CompilerParams(vmem_limit_bytes=24 * MIB),
        cost_estimate=attend_cost(rows, rows),
    )(near, far, listed, *messages)


def piece_shape(heads, parts, span):
    return jax.ShapeDtypeStruct((heads * parts, span // parts // 2, LANES), jnp.bfloat16)


def more_attend(near, heads, queries, old, kvs, columns, parts):
    rows = queries[0].shape[0]
    span = rows // heads
    state = jax.ShapeDtypeStruct((rows, LANES), jnp.float32)
    if parts:
        out_shape, out_specs = piece_shape(heads, parts, span), VMEM
        scratch = [pltpu.VMEM(state.shape, state.dtype)]
    else:
        out_shape, out_specs, scratch = [state] * 2, [VMEM] * 2, []
    return pl.pallas_call(
        functools.partial(more_kernel, heads, columns, parts),
        in_specs=[SMEM] + [VMEM] * (5 + len(kvs)),
        out_specs=out_specs,
        out_shape=out_shape,
        scratch_shapes=scratch,
        compiler_params=pltpu.CompilerParams(vmem_limit_bytes=24 * MIB),
        cost_estimate=attend_cost(rows, span * len(kvs)),
    )(near, *queries, *old, *kvs)


def whole_attend(near, far, picks, listed, messages, kvs, span, parts):
    heads = len(messages)
    rows = heads * span
    blocks, steps = rows // BLOCK, kvs.shape[0] // rows
    return pl.pallas_call(
        functools.partial(whole_kernel, heads, picks, parts),
        grid=(steps,),
        in_specs=[SMEM, SMEM, VMEM, pl.BlockSpec((rows, LANES), lambda s: (s, 0))] + [VMEM] * heads,
        out_specs=VMEM,
        out_shape=piece_shape(heads, parts, span),
        scratch_shapes=[
            pltpu.VMEM((rows, LANES), jnp.float32),
            pltpu.VMEM((rows, LANES), jnp.float32),
            pltpu.VMEM((rows, LANES), jnp.bfloat16),
            pltpu.VMEM((rows, LANES), jnp.float32),
            pltpu.VMEM((blocks, rows), jnp.float32),
            pltpu.VMEM((blocks, LANES), jnp.int32),
            pltpu.VMEM((picks, blocks, LANES), jnp.int32),
        ],
        compiler_params=pltpu.CompilerParams(vmem_limit_bytes=24 * MIB),
        cost_estimate=attend_cost(rows, kvs.shape[0]),
    )(near, far, listed, kvs, *messages)


def mix_kernel(near_count, order, here_ref, got_ref, *refs):
    parts = len(order)
    low = low_half()
    depth = refs[0].shape[0]
    blocks = []
    for ref in refs[:-1]:
        blocks += [ref.at[first : first + depth, :] for first in range(0, ref.shape[0], depth)]
    total = None
    for i, d in enumerate(order):
        source = here_ref[0] ^ d
        columns = []
        for near in range(0, near_count, 2):
            even, odd = (got_ref[at * parts + source].astype(jnp.float32) for at in (near, near + 1))
            top = jnp.where(low, even, odd)
            bottom = half_turn(jnp.where(low, odd, even))
            columns.append(jnp.concatenate([top, bottom], axis=0).astype(jnp.bfloat16))
        rows = jnp.concatenate(columns, axis=1)
        term = jnp.dot(rows, blocks[i][...], preferred_element_type=jnp.float32)
        total = term if total is None else total + term
    refs[-1][...] = total.astype(refs[-1].dtype)


def mix(here, got, o_blocks, order):
    parts = len(order)
    return pl.pallas_call(
        functools.partial(mix_kernel, got.shape[0] // parts, order),
        out_shape=jax.ShapeDtypeStruct((2 * got.shape[1], o_blocks[0].shape[1]), jnp.bfloat16),
        in_specs=[SMEM] + [VMEM] * (1 + len(o_blocks)),
        out_specs=VMEM,
        compiler_params=pltpu.CompilerParams(vmem_limit_bytes=24 * MIB),
    )(here, got, *o_blocks)


def swapped(block, axis, distance):
    return lax.ppermute(block, axis, [(i, i ^ distance) for i in range(lax.axis_size(axis))])


def shards(tokens, q_weight, k_weight, v_weight, o_weight, rand_blocks, global_pos):
    tok_rows = tokens.shape[0]
    far_count, heads, parts = (lax.axis_size(axis) for axis in ("far", "near", "head"))
    near, far, here = (
        lax.axis_index(axis).astype(jnp.int32).reshape(1) for axis in ("near", "far", "head")
    )
    picks = rand_blocks.shape[1]

    blocks = far_count * heads * tok_rows // BLOCK
    *ready, listed = project(
        near, blocks, global_pos, rand_blocks, tokens, q_weight, k_weight, v_weight
    )
    leaving, sent = ready[:heads], ready[heads:]
    messages = [sent[0]] + [swapped(sent[d], "near", d) for d in range(1, heads)]

    if far_count == 2:
        apart = [swapped(leaving[d], ("far", "near"), heads + d) for d in range(heads)]
        peaks, sums, *queries = open_attend(near, far, picks, listed, messages, tok_rows)
        columns = [(heads + d) * tok_rows for d in range(heads)]
        more = functools.partial(more_attend, near, heads, queries)
        old = more([peaks, sums], apart[:-1], columns[:-1], 0)
        pieces = more(old, apart[-1:], columns[-1:], parts)
    else:
        kvs = lax.all_gather(pack(tok_rows, messages), "far", tiled=True)
        pieces = whole_attend(near, far, picks, listed, messages, kvs, tok_rows, parts)

    distance = parts // 2
    o_blocks = [o_weight, swapped(o_weight, "head", distance)]
    order = [0, distance]
    while distance > 1:
        distance //= 2
        o_blocks.append(swapped(gather(o_blocks, [pieces]), "head", distance))
        order = order + [d ^ distance for d in order]
    got = lax.all_to_all(pieces, ("near", "head"), 0, 0, tiled=True)
    return mix(here, got, o_blocks, order)


def solution(mesh):
    count, columns = mesh.devices.shape
    tm = ("far", "near")
    placed = (
        P(tm, None),
        P(None, "head"),
        P(None, "head"),
        P(None, "head"),
        P("head", None),
        P(tm, None),
        P(),
    )

    def run(tokens, q_weight, *rest):
        heads = q_weight.shape[1] // HEAD_DIM // columns
        split = Mesh(mesh.devices.reshape(count // heads, heads, columns), (*tm, "head"))
        body = jax.shard_map(
            shards, mesh=split, in_specs=placed, out_specs=P((*tm, "head"), None), check_vma=False
        )
        return body(tokens, q_weight, *rest)

    return run
```

```python
import functools
import math

import jax
import jax.numpy as jnp
from jax import lax
from jax.experimental import pallas as pl
from jax.experimental.pallas import tpu as pltpu
from jax.sharding import Mesh
from jax.sharding import PartitionSpec as P

HEAD_DIM = 64
BLOCK = 128
LANES = 128
DIGIT_BITS = 7
DIGIT = 1 << DIGIT_BITS
TILE_ROWS = 16
NEVER = -1e30
MIB = 1024 * 1024
VMEM = pl.BlockSpec(memory_space=pltpu.VMEM)
SMEM = pl.BlockSpec(memory_space=pltpu.SMEM)
HBM = pl.BlockSpec(memory_space=pltpu.HBM)
ANY = pl.BlockSpec(memory_space=pl.ANY)


def low_half():
    return lax.broadcasted_iota(jnp.int32, (1, LANES), 1) < HEAD_DIM


def half_turn(block):
    return pltpu.roll(block, HEAD_DIM, 1)


def own_half(near):
    return lax.broadcasted_iota(jnp.int32, (1, LANES), 1) // HEAD_DIM == (near & 1)


def project_kernel(cuts, near_ref, rand_hbm, pos_hbm, t_hbm, q_hbm, k_hbm, v_hbm, *refs):
    listed_ref, t_ref, q_ref, k_ref, v_ref, all_ref, rand_ref, pos_ref, sems, few_sems = refs[-10:]
    rows = t_ref.shape[0]
    heads = k_ref.shape[1] // HEAD_DIM
    far_refs, sent_refs = refs[:heads], refs[heads : 2 * heads]
    few = [
        pltpu.make_async_copy(pos_hbm, pos_ref, few_sems.at[0]),
        pltpu.make_async_copy(rand_hbm, rand_ref, few_sems.at[1]),
    ]
    for copy in few:
        copy.start()
    copies = []
    for i, (source, target) in enumerate(
        ((t_hbm, t_ref), (k_hbm, k_ref), (v_hbm, v_ref), (q_hbm, q_ref))
    ):
        part = source.shape[0] // cuts
        group = []
        for c in range(cuts):
            at = slice(c * part, (c + 1) * part)
            copy = pltpu.make_async_copy(source.at[at, :], target.at[at, :], sems.at[i, c])
            copy.start()
            group.append(copy)
        copies.append(group)

    for copy in few:
        copy.wait()
    spots = lax.broadcasted_iota(jnp.int32, listed_ref.shape, 0) * BLOCK
    spots = spots + lax.broadcasted_iota(jnp.int32, listed_ref.shape, 1)
    listed_ref[...] = lax.fori_loop(
        0,
        pos_ref.shape[0],
        lambda i, flags: jnp.where(spots == pos_ref[i], 1.0, flags),
        jnp.zeros(listed_ref.shape, jnp.float32),
        unroll=16,
    )

    def product(i, weight_ref):
        for copy in copies[i]:
            copy.wait()
        return jnp.dot(t_ref[...], weight_ref[...], preferred_element_type=jnp.float32)

    for copy in copies[0]:
        copy.wait()
    low = low_half()
    k = product(1, k_ref)
    v = product(2, v_ref)
    for pair in range(heads // 2):
        at = slice(pair * LANES, (pair + 1) * LANES)
        key, value = k[:, at], half_turn(v[:, at])
        all_ref[2 * pair, :rows, :] = jnp.where(low, key, value).astype(jnp.bfloat16)
        all_ref[2 * pair + 1, :rows, :] = jnp.where(low, value, key).astype(jnp.bfloat16)
    q = product(3, q_ref)
    for pair in range(heads // 2):
        at = slice(pair * LANES, (pair + 1) * LANES)
        top, bottom = q[: rows // 2, at], half_turn(q[rows // 2 :, at])
        all_ref[2 * pair, rows:, :] = jnp.where(low, top, bottom).astype(jnp.bfloat16)
        all_ref[2 * pair + 1, rows:, :] = jnp.where(low, bottom, top).astype(jnp.bfloat16)
    near = near_ref[0]
    digit_rows = sent_refs[0].shape[0] - rows - rows // 2
    row = lax.broadcasted_iota(jnp.int32, (digit_rows, LANES), 0)
    digits = jnp.zeros((digit_rows, LANES), jnp.float32)
    picks = rand_ref.shape[1]
    for j in range(rand_ref.shape[0]):
        for r in range(picks):
            at = 2 * (j * picks + r)
            value = rand_ref[j, r]
            digits = jnp.where(row == at, (value >> DIGIT_BITS).astype(jnp.float32), digits)
            digits = jnp.where(row == at + 1, (value & (DIGIT - 1)).astype(jnp.float32), digits)
    digits = digits.astype(jnp.bfloat16)
    for d in range(heads):
        far_refs[d][...] = all_ref[near ^ d, :rows, :]
        sent_refs[d][: rows + rows // 2, :] = all_ref[near ^ d]
        sent_refs[d][rows + rows // 2 :, :] = digits


def project(near, blocks, global_pos, rand_blocks, tokens, q_weight, k_weight, v_weight):
    rows, depth = tokens.shape
    feats = k_weight.shape[1]
    heads = feats // HEAD_DIM
    cuts = 2
    message = rows + rows // 2
    digit_rows = -(-2 * rand_blocks.size // TILE_ROWS) * TILE_ROWS
    pinned = [
        pltpu.with_memory_space_constraint(array, pltpu.HBM)
        for array in (rand_blocks, global_pos, tokens, q_weight, k_weight, v_weight)
    ]
    return pl.pallas_call(
        functools.partial(project_kernel, cuts),
        in_specs=[SMEM] + [HBM] * 6,
        out_specs=[VMEM] * (2 * heads + 1),
        out_shape=[jax.ShapeDtypeStruct((rows, LANES), jnp.bfloat16)] * heads
        + [jax.ShapeDtypeStruct((message + digit_rows, LANES), jnp.bfloat16)] * heads
        + [jax.ShapeDtypeStruct((blocks, LANES), jnp.float32)],
        scratch_shapes=[
            pltpu.VMEM((rows, depth), jnp.bfloat16),
            pltpu.VMEM((depth, feats), jnp.bfloat16),
            pltpu.VMEM((depth, feats), jnp.bfloat16),
            pltpu.VMEM((depth, feats), jnp.bfloat16),
            pltpu.VMEM((heads, message, LANES), jnp.bfloat16),
            pltpu.SMEM(rand_blocks.shape, jnp.int32),
            pltpu.SMEM(global_pos.shape, jnp.int32),
            pltpu.SemaphoreType.DMA((4, cuts)),
            pltpu.SemaphoreType.DMA((2,)),
        ],
        compiler_params=pltpu.CompilerParams(vmem_limit_bytes=24 * MIB),
        cost_estimate=pl.CostEstimate(
            flops=6 * rows * depth * feats, bytes_accessed=2 * depth * (rows + 3 * feats), transcendentals=0
        ),
    )(near, *pinned)


def pack_kernel(*refs):
    out_ref = refs[-1]
    rows = out_ref.shape[0] // (len(refs) - 1)
    for i, ref in enumerate(refs[:-1]):
        out_ref[i * rows : (i + 1) * rows, :] = ref[:rows, :]


def pack(rows, messages):
    return pl.pallas_call(
        pack_kernel,
        in_specs=[VMEM] * len(messages),
        out_specs=VMEM,
        out_shape=jax.ShapeDtypeStruct((rows * len(messages), LANES), jnp.bfloat16),
        compiler_params=pltpu.CompilerParams(vmem_limit_bytes=32 * MIB),
    )(*messages)


def gather_kernel(count, *refs):
    out_ref, sems = refs[-2:]
    first, copies = 0, []
    for i, ref in enumerate(refs[:count]):
        at = slice(first, first + ref.shape[0])
        copies.append(pltpu.make_async_copy(ref, out_ref.at[at, :], sems.at[i]))
        first += ref.shape[0]
    for copy in copies:
        copy.start()
    for copy in copies:
        copy.wait()


def gather(blocks, after):
    rows = sum(block.shape[0] for block in blocks)
    return pl.pallas_call(
        functools.partial(gather_kernel, len(blocks)),
        in_specs=[ANY] * (len(blocks) + len(after)),
        out_specs=VMEM,
        out_shape=jax.ShapeDtypeStruct((rows, blocks[0].shape[1]), blocks[0].dtype),
        scratch_shapes=[pltpu.SemaphoreType.DMA((len(blocks),))],
        compiler_params=pltpu.CompilerParams(vmem_limit_bytes=24 * MIB),
    )(*blocks, *after)


def prepare(heads, picks, near, far, span, messages, listed_ref, q_ref, free_ref, block_ref, pick_ref):
    per_shard = span // BLOCK
    mine = own_half(near)
    for d in range(heads):
        packed = messages[d][span : span + span // 2, :].astype(jnp.float32)
        top = jnp.where(mine, packed, 0.0)
        bottom = jnp.where(mine, half_turn(packed), 0.0)
        q_ref[d * span : d * span + span // 2, :] = top.astype(q_ref.dtype)
        q_ref[d * span + span // 2 : (d + 1) * span, :] = bottom.astype(q_ref.dtype)
        rand = messages[d][span + span // 2 :, :].astype(jnp.float32)
        for j in range(per_shard):
            row = slice(d * per_shard + j, d * per_shard + j + 1)
            block = (far * heads + (near ^ d)) * per_shard + j
            block_ref[row, :] = jnp.full((1, LANES), block, jnp.int32)
            flags = jnp.broadcast_to(listed_ref[pl.ds(block, 1), :], (BLOCK, BLOCK))
            at = (d * per_shard + j) * BLOCK
            free_ref[at : at + BLOCK, :] = 1.0 - jnp.transpose(flags)
            for r in range(picks):
                at = 2 * (j * picks + r)
                pick = rand[at : at + 1, :] * DIGIT + rand[at + 1 : at + 2, :]
                pick_ref[r, row, :] = pick.astype(jnp.int32)


def fill_bias(heads, groups, near, listed_ref, block_ref, pick_ref, bias_ref):
    per_shard = block_ref.shape[0] // heads
    blocks = block_ref[...]
    picks = [pick_ref[r] for r in range(pick_ref.shape[0])]
    for g, there in enumerate(groups):
        for d in range(heads):
            for b in range(per_shard):
                key_block = (there * heads + (near ^ d)) * per_shard + b
                away = key_block - blocks
                times = listed_ref[pl.ds(key_block, 1), :] + jnp.where((away >= -2) & (away <= 1), 1.0, 0.0)
                for pick in picks:
                    times = times + jnp.where(pick == key_block, 1.0, 0.0)
                at = ((g * heads + d) * per_shard + b) * BLOCK
                bias_ref[:, at : at + BLOCK] = jnp.where(
                    times > 0, jnp.log2(jnp.maximum(times, 1.0)), NEVER
                )


def attend_rows(near, tile, span, q_ref, free_ref, bias_ref, keys, peak, total):
    per_shard = span // BLOCK
    scale = HEAD_DIM ** (-0.5) * math.log2(math.e)
    mine = own_half(near)
    q = q_ref[tile * span : (tile + 1) * span, :]
    scores = [[] for _ in range(per_shard)]
    for key_ref, first, column in keys:
        s = lax.dot_general(
            q,
            key_ref[first : first + span, :],
            (((1,), (1,)), ((), ())),
            preferred_element_type=jnp.float32,
        )
        for j in range(per_shard):
            block = tile * per_shard + j
            free = free_ref[block * BLOCK : (block + 1) * BLOCK, :]
            for b in range(per_shard):
                bias = bias_ref[block : block + 1, column + b * BLOCK : column + (b + 1) * BLOCK]
                part = s[j * BLOCK : (j + 1) * BLOCK, b * BLOCK : (b + 1) * BLOCK]
                scores[j].append(part * scale + free * bias)
    peaks, weights = [], []
    for j in range(per_shard):
        best = jnp.max(functools.reduce(jnp.maximum, scores[j]), axis=1, keepdims=True)
        best = jnp.broadcast_to(best, (BLOCK, LANES))
        if peak is not None:
            best = jnp.maximum(peak[j * BLOCK : (j + 1) * BLOCK, :], best)
        peaks.append(best)
        weights.append([jnp.exp2(part - best).astype(jnp.bfloat16) for part in scores[j]])
    new = jnp.concatenate(peaks, axis=0)
    if total is not None:
        total = total * jnp.exp2(peak - new)
    for i, (key_ref, first, _) in enumerate(keys):
        e = jnp.concatenate(
            [
                jnp.concatenate(weights[j][i * per_shard : (i + 1) * per_shard], axis=1)
                for j in range(per_shard)
            ],
            axis=0,
        )
        v = jnp.where(mine, jnp.ones((), jnp.bfloat16), key_ref[first : first + span, :])
        term = jnp.dot(e, v, preferred_element_type=jnp.float32)
        total = term if total is None else total + term
    return new, total


def finish(heads, parts, near, span, sums, out_ref):
    mine = own_half(near)
    piece = span // parts
    for d in range(heads):
        for part in range(parts):
            first = d * span + part * piece
            top = sums[first : first + piece // 2, :]
            bottom = sums[first + piece // 2 : first + piece, :]
            values = jnp.where(mine, half_turn(top), bottom)
            totals = jnp.where(mine, top, half_turn(bottom))
            out_ref[(near ^ d) * parts + part] = (values / totals).astype(out_ref.dtype)


def open_kernel(heads, picks, near_ref, far_ref, listed_ref, *refs):
    messages, refs = refs[:heads], refs[heads:]
    peaks, sums, q_ref, free_ref, bias_ref, block_ref, pick_ref = refs
    span = q_ref.shape[0] // heads
    near, far = near_ref[0], far_ref[0]
    prepare(heads, picks, near, far, span, messages, listed_ref, q_ref, free_ref, block_ref, pick_ref)
    fill_bias(heads, [far, far ^ 1], near, listed_ref, block_ref, pick_ref, bias_ref)
    keys = [(messages[d], 0, d * span) for d in range(heads)]
    for tile in range(heads):
        rows = slice(tile * span, (tile + 1) * span)
        peaks[rows, :], sums[rows, :] = attend_rows(
            near, tile, span, q_ref, free_ref, bias_ref, keys, None, None
        )


def more_kernel(heads, columns, parts, near_ref, q_ref, free_ref, bias_ref, peak_in, sum_in, *refs):
    kv_refs, refs = refs[: len(columns)], refs[len(columns) :]
    if parts:
        out_ref, sums = refs
        peaks = None
    else:
        peaks, sums = refs
    span = q_ref.shape[0] // heads
    near = near_ref[0]
    keys = [(ref, 0, column) for ref, column in zip(kv_refs, columns)]
    for tile in range(heads):
        rows = slice(tile * span, (tile + 1) * span)
        new, sums[rows, :] = attend_rows(
            near, tile, span, q_ref, free_ref, bias_ref, keys, peak_in[rows, :], sum_in[rows, :]
        )
        if peaks is not None:
            peaks[rows, :] = new
    if parts:
        finish(heads, parts, near, span, sums, out_ref)


def whole_kernel(heads, picks, parts, near_ref, far_ref, listed_ref, kv_ref, *refs):
    messages, refs = refs[:heads], refs[heads:]
    out_ref, peaks, sums, q_ref, free_ref, bias_ref, block_ref, pick_ref = refs
    span = q_ref.shape[0] // heads
    near, far = near_ref[0], far_ref[0]
    step = pl.program_id(0)

    @pl.when(step == 0)
    def _():
        peaks[...] = jnp.full_like(peaks, NEVER)
        sums[...] = jnp.zeros_like(sums)
        prepare(heads, picks, near, far, span, messages, listed_ref, q_ref, free_ref, block_ref, pick_ref)

    fill_bias(heads, [step], near, listed_ref, block_ref, pick_ref, bias_ref)
    keys = [(kv_ref, d * span, d * span) for d in range(heads)]
    for tile in range(heads):
        rows = slice(tile * span, (tile + 1) * span)
        peaks[rows, :], sums[rows, :] = attend_rows(
            near, tile, span, q_ref, free_ref, bias_ref, keys, peaks[rows, :], sums[rows, :]
        )

    @pl.when(step == pl.num_programs(0) - 1)
    def _():
        finish(heads, parts, near, span, sums, out_ref)


def attend_cost(rows, keys):
    return pl.CostEstimate(
        flops=4 * rows * keys * LANES, bytes_accessed=4 * (rows + keys) * LANES, transcendentals=rows * keys
    )


def open_attend(near, far, picks, listed, messages, span):
    heads = len(messages)
    rows = heads * span
    blocks = rows // BLOCK
    state = jax.ShapeDtypeStruct((rows, LANES), jnp.float32)
    return pl.pallas_call(
        functools.partial(open_kernel, heads, picks),
        in_specs=[SMEM, SMEM] + [VMEM] * (1 + heads),
        out_specs=[VMEM] * 5,
        out_shape=[
            state,
            state,
            jax.ShapeDtypeStruct((rows, LANES), jnp.bfloat16),
            state,
            jax.ShapeDtypeStruct((blocks, 2 * rows), jnp.float32),
        ],
        scratch_shapes=[
            pltpu.VMEM((blocks, LANES), jnp.int32),
            pltpu.VMEM((picks, blocks, LANES), jnp.int32),
        ],
        compiler_params=pltpu.CompilerParams(vmem_limit_bytes=24 * MIB),
        cost_estimate=attend_cost(rows, rows),
    )(near, far, listed, *messages)


def piece_shape(heads, parts, span):
    return jax.ShapeDtypeStruct((heads * parts, span // parts // 2, LANES), jnp.bfloat16)


def more_attend(near, heads, queries, old, kvs, columns, parts):
    rows = queries[0].shape[0]
    span = rows // heads
    state = jax.ShapeDtypeStruct((rows, LANES), jnp.float32)
    if parts:
        out_shape, out_specs = piece_shape(heads, parts, span), VMEM
        scratch = [pltpu.VMEM(state.shape, state.dtype)]
    else:
        out_shape, out_specs, scratch = [state] * 2, [VMEM] * 2, []
    return pl.pallas_call(
        functools.partial(more_kernel, heads, columns, parts),
        in_specs=[SMEM] + [VMEM] * (5 + len(kvs)),
        out_specs=out_specs,
        out_shape=out_shape,
        scratch_shapes=scratch,
        compiler_params=pltpu.CompilerParams(vmem_limit_bytes=24 * MIB),
        cost_estimate=attend_cost(20 * rows, span * len(kvs)),
    )(near, *queries, *old, *kvs)


def whole_attend(near, far, picks, listed, messages, kvs, span, parts):
    heads = len(messages)
    rows = heads * span
    blocks, steps = rows // BLOCK, kvs.shape[0] // rows
    return pl.pallas_call(
        functools.partial(whole_kernel, heads, picks, parts),
        grid=(steps,),
        in_specs=[SMEM, SMEM, VMEM, pl.BlockSpec((rows, LANES), lambda s: (s, 0))] + [VMEM] * heads,
        out_specs=VMEM,
        out_shape=piece_shape(heads, parts, span),
        scratch_shapes=[
            pltpu.VMEM((rows, LANES), jnp.float32),
            pltpu.VMEM((rows, LANES), jnp.float32),
            pltpu.VMEM((rows, LANES), jnp.bfloat16),
            pltpu.VMEM((rows, LANES), jnp.float32),
            pltpu.VMEM((blocks, rows), jnp.float32),
            pltpu.VMEM((blocks, LANES), jnp.int32),
            pltpu.VMEM((picks, blocks, LANES), jnp.int32),
        ],
        compiler_params=pltpu.CompilerParams(vmem_limit_bytes=24 * MIB),
        cost_estimate=attend_cost(rows, kvs.shape[0]),
    )(near, far, listed, kvs, *messages)


def mix_kernel(near_count, order, here_ref, got_ref, *refs):
    parts = len(order)
    low = low_half()
    depth = refs[0].shape[0]
    blocks = []
    for ref in refs[:-1]:
        blocks += [ref.at[first : first + depth, :] for first in range(0, ref.shape[0], depth)]
    total = None
    for i, d in enumerate(order):
        source = here_ref[0] ^ d
        columns = []
        for near in range(0, near_count, 2):
            even, odd = (got_ref[at * parts + source].astype(jnp.float32) for at in (near, near + 1))
            top = jnp.where(low, even, odd)
            bottom = half_turn(jnp.where(low, odd, even))
            columns.append(jnp.concatenate([top, bottom], axis=0).astype(jnp.bfloat16))
        rows = jnp.concatenate(columns, axis=1)
        term = jnp.dot(rows, blocks[i][...], preferred_element_type=jnp.float32)
        total = term if total is None else total + term
    refs[-1][...] = total.astype(refs[-1].dtype)


def mix(here, got, o_blocks, order):
    parts = len(order)
    return pl.pallas_call(
        functools.partial(mix_kernel, got.shape[0] // parts, order),
        out_shape=jax.ShapeDtypeStruct((2 * got.shape[1], o_blocks[0].shape[1]), jnp.bfloat16),
        in_specs=[SMEM] + [VMEM] * (1 + len(o_blocks)),
        out_specs=VMEM,
        compiler_params=pltpu.CompilerParams(vmem_limit_bytes=24 * MIB),
    )(here, got, *o_blocks)


def swapped(block, axis, distance):
    return lax.ppermute(block, axis, [(i, i ^ distance) for i in range(lax.axis_size(axis))])


def shards(tokens, q_weight, k_weight, v_weight, o_weight, rand_blocks, global_pos):
    tok_rows = tokens.shape[0]
    far_count, heads, parts = (lax.axis_size(axis) for axis in ("far", "near", "head"))
    near, far, here = (
        lax.axis_index(axis).astype(jnp.int32).reshape(1) for axis in ("near", "far", "head")
    )
    picks = rand_blocks.shape[1]

    blocks = far_count * heads * tok_rows // BLOCK
    *ready, listed = project(
        near, blocks, global_pos, rand_blocks, tokens, q_weight, k_weight, v_weight
    )
    leaving, sent = ready[:heads], ready[heads:]
    messages = [sent[0]] + [swapped(sent[d], "near", d) for d in range(1, heads)]

    if far_count == 2:
        apart = [swapped(leaving[d], ("far", "near"), heads + d) for d in range(heads)]
        peaks, sums, *queries = open_attend(near, far, picks, listed, messages, tok_rows)
        ready_at = queries[-1:]
        columns = [(heads + d) * tok_rows for d in range(heads)]
        more = functools.partial(more_attend, near, heads, queries)
        old = more([peaks, sums], apart[:-1], columns[:-1], 0)
        pieces = more(old, apart[-1:], columns[-1:], parts)
    else:
        kvs = lax.all_gather(pack(tok_rows, messages), "far", tiled=True)
        ready_at = messages[1:]
        pieces = whole_attend(near, far, picks, listed, messages, kvs, tok_rows, parts)

    distance = parts // 2
    o_blocks = [o_weight, swapped(o_weight, "head", distance)]
    order = [0, distance]
    while distance > 1:
        distance //= 2
        o_blocks.append(swapped(gather(o_blocks, ready_at), "head", distance))
        order = order + [d ^ distance for d in order]
    got = lax.all_to_all(pieces, ("near", "head"), 0, 0, tiled=True)
    return mix(here, got, o_blocks, order)


def solution(mesh):
    count, columns = mesh.devices.shape
    tm = ("far", "near")
    placed = (
        P(tm, None),
        P(None, "head"),
        P(None, "head"),
        P(None, "head"),
        P("head", None),
        P(tm, None),
        P(),
    )

    def run(tokens, q_weight, *rest):
        heads = q_weight.shape[1] // HEAD_DIM // columns
        split = Mesh(mesh.devices.reshape(count // heads, heads, columns), (*tm, "head"))
        body = jax.shard_map(
            shards, mesh=split, in_specs=placed, out_specs=P((*tm, "head"), None), check_vma=False
        )
        return body(tokens, q_weight, *rest)

    return run
```

```python
import functools
import math

import jax
import jax.numpy as jnp
from jax import lax
from jax.experimental import pallas as pl
from jax.experimental.pallas import tpu as pltpu
from jax.sharding import Mesh
from jax.sharding import PartitionSpec as P

HEAD_DIM = 64
BLOCK = 128
LANES = 128
DIGIT_BITS = 7
DIGIT = 1 << DIGIT_BITS
TILE_ROWS = 16
NEVER = -1e30
MIB = 1024 * 1024
VMEM = pl.BlockSpec(memory_space=pltpu.VMEM)
SMEM = pl.BlockSpec(memory_space=pltpu.SMEM)
HBM = pl.BlockSpec(memory_space=pltpu.HBM)
ANY = pl.BlockSpec(memory_space=pl.ANY)


def low_half():
    return lax.broadcasted_iota(jnp.int32, (1, LANES), 1) < HEAD_DIM


def half_turn(block):
    return pltpu.roll(block, HEAD_DIM, 1)


def own_half(near):
    return lax.broadcasted_iota(jnp.int32, (1, LANES), 1) // HEAD_DIM == (near & 1)


def project_kernel(cuts, near_ref, rand_hbm, pos_hbm, t_hbm, q_hbm, k_hbm, v_hbm, *refs):
    listed_ref, t_ref, q_ref, k_ref, v_ref, all_ref, rand_ref, pos_ref, sems, few_sems = refs[-10:]
    rows = t_ref.shape[0]
    heads = k_ref.shape[1] // HEAD_DIM
    far_refs, sent_refs = refs[:heads], refs[heads : 2 * heads]
    few = [
        pltpu.make_async_copy(pos_hbm, pos_ref, few_sems.at[0]),
        pltpu.make_async_copy(rand_hbm, rand_ref, few_sems.at[1]),
    ]
    for copy in few:
        copy.start()
    copies = []
    for i, (source, target) in enumerate(
        ((t_hbm, t_ref), (k_hbm, k_ref), (v_hbm, v_ref), (q_hbm, q_ref))
    ):
        part = source.shape[0] // cuts
        group = []
        for c in range(cuts):
            at = slice(c * part, (c + 1) * part)
            copy = pltpu.make_async_copy(source.at[at, :], target.at[at, :], sems.at[i, c])
            copy.start()
            group.append(copy)
        copies.append(group)

    for copy in few:
        copy.wait()
    spots = lax.broadcasted_iota(jnp.int32, listed_ref.shape, 0) * BLOCK
    spots = spots + lax.broadcasted_iota(jnp.int32, listed_ref.shape, 1)
    listed_ref[...] = lax.fori_loop(
        0,
        pos_ref.shape[0],
        lambda i, flags: jnp.where(spots == pos_ref[i], 1.0, flags),
        jnp.zeros(listed_ref.shape, jnp.float32),
        unroll=16,
    )

    def product(i, weight_ref):
        for copy in copies[i]:
            copy.wait()
        return jnp.dot(t_ref[...], weight_ref[...], preferred_element_type=jnp.float32)

    for copy in copies[0]:
        copy.wait()
    low = low_half()
    k = product(1, k_ref)
    v = product(2, v_ref)
    for pair in range(heads // 2):
        at = slice(pair * LANES, (pair + 1) * LANES)
        key, value = k[:, at], half_turn(v[:, at])
        all_ref[2 * pair, :rows, :] = jnp.where(low, key, value).astype(jnp.bfloat16)
        all_ref[2 * pair + 1, :rows, :] = jnp.where(low, value, key).astype(jnp.bfloat16)
    q = product(3, q_ref)
    for pair in range(heads // 2):
        at = slice(pair * LANES, (pair + 1) * LANES)
        top, bottom = q[: rows // 2, at], half_turn(q[rows // 2 :, at])
        all_ref[2 * pair, rows:, :] = jnp.where(low, top, bottom).astype(jnp.bfloat16)
        all_ref[2 * pair + 1, rows:, :] = jnp.where(low, bottom, top).astype(jnp.bfloat16)
    near = near_ref[0]
    digit_rows = sent_refs[0].shape[0] - rows - rows // 2
    row = lax.broadcasted_iota(jnp.int32, (digit_rows, LANES), 0)
    digits = jnp.zeros((digit_rows, LANES), jnp.float32)
    picks = rand_ref.shape[1]
    for j in range(rand_ref.shape[0]):
        for r in range(picks):
            at = 2 * (j * picks + r)
            value = rand_ref[j, r]
            digits = jnp.where(row == at, (value >> DIGIT_BITS).astype(jnp.float32), digits)
            digits = jnp.where(row == at + 1, (value & (DIGIT - 1)).astype(jnp.float32), digits)
    digits = digits.astype(jnp.bfloat16)
    for d in range(heads):
        far_refs[d][...] = all_ref[near ^ d, :rows, :]
        sent_refs[d][: rows + rows // 2, :] = all_ref[near ^ d]
        sent_refs[d][rows + rows // 2 :, :] = digits


def project(near, blocks, global_pos, rand_blocks, tokens, q_weight, k_weight, v_weight):
    rows, depth = tokens.shape
    feats = k_weight.shape[1]
    heads = feats // HEAD_DIM
    cuts = 2
    message = rows + rows // 2
    digit_rows = -(-2 * rand_blocks.size // TILE_ROWS) * TILE_ROWS
    pinned = [
        pltpu.with_memory_space_constraint(array, pltpu.HBM)
        for array in (rand_blocks, global_pos, tokens, q_weight, k_weight, v_weight)
    ]
    return pl.pallas_call(
        functools.partial(project_kernel, cuts),
        in_specs=[SMEM] + [HBM] * 6,
        out_specs=[VMEM] * (2 * heads + 1),
        out_shape=[jax.ShapeDtypeStruct((rows, LANES), jnp.bfloat16)] * heads
        + [jax.ShapeDtypeStruct((message + digit_rows, LANES), jnp.bfloat16)] * heads
        + [jax.ShapeDtypeStruct((blocks, LANES), jnp.float32)],
        scratch_shapes=[
            pltpu.VMEM((rows, depth), jnp.bfloat16),
            pltpu.VMEM((depth, feats), jnp.bfloat16),
            pltpu.VMEM((depth, feats), jnp.bfloat16),
            pltpu.VMEM((depth, feats), jnp.bfloat16),
            pltpu.VMEM((heads, message, LANES), jnp.bfloat16),
            pltpu.SMEM(rand_blocks.shape, jnp.int32),
            pltpu.SMEM(global_pos.shape, jnp.int32),
            pltpu.SemaphoreType.DMA((4, cuts)),
            pltpu.SemaphoreType.DMA((2,)),
        ],
        compiler_params=pltpu.CompilerParams(vmem_limit_bytes=24 * MIB),
        cost_estimate=pl.CostEstimate(
            flops=6 * rows * depth * feats, bytes_accessed=2 * depth * (rows + 3 * feats), transcendentals=0
        ),
    )(near, *pinned)


def pack_kernel(*refs):
    out_ref = refs[-1]
    rows = out_ref.shape[0] // (len(refs) - 1)
    for i, ref in enumerate(refs[:-1]):
        out_ref[i * rows : (i + 1) * rows, :] = ref[:rows, :]


def pack(rows, messages):
    return pl.pallas_call(
        pack_kernel,
        in_specs=[VMEM] * len(messages),
        out_specs=VMEM,
        out_shape=jax.ShapeDtypeStruct((rows * len(messages), LANES), jnp.bfloat16),
        compiler_params=pltpu.CompilerParams(vmem_limit_bytes=32 * MIB),
    )(*messages)


def gather_kernel(count, *refs):
    out_ref, sems = refs[-2:]
    first, copies = 0, []
    for i, ref in enumerate(refs[:count]):
        at = slice(first, first + ref.shape[0])
        copies.append(pltpu.make_async_copy(ref, out_ref.at[at, :], sems.at[i]))
        first += ref.shape[0]
    for copy in copies:
        copy.start()
    for copy in copies:
        copy.wait()


def gather(blocks, after):
    rows = sum(block.shape[0] for block in blocks)
    return pl.pallas_call(
        functools.partial(gather_kernel, len(blocks)),
        in_specs=[ANY] * (len(blocks) + len(after)),
        out_specs=VMEM,
        out_shape=jax.ShapeDtypeStruct((rows, blocks[0].shape[1]), blocks[0].dtype),
        scratch_shapes=[pltpu.SemaphoreType.DMA((len(blocks),))],
        compiler_params=pltpu.CompilerParams(vmem_limit_bytes=24 * MIB),
    )(*blocks, *after)


def prepare(heads, picks, near, far, span, messages, listed_ref, q_ref, free_ref, block_ref, pick_ref):
    per_shard = span // BLOCK
    mine = own_half(near)
    for d in range(heads):
        packed = messages[d][span : span + span // 2, :].astype(jnp.float32)
        top = jnp.where(mine, packed, 0.0)
        bottom = jnp.where(mine, half_turn(packed), 0.0)
        q_ref[d * span : d * span + span // 2, :] = top.astype(q_ref.dtype)
        q_ref[d * span + span // 2 : (d + 1) * span, :] = bottom.astype(q_ref.dtype)
        rand = messages[d][span + span // 2 :, :].astype(jnp.float32)
        for j in range(per_shard):
            row = slice(d * per_shard + j, d * per_shard + j + 1)
            block = (far * heads + (near ^ d)) * per_shard + j
            block_ref[row, :] = jnp.full((1, LANES), block, jnp.int32)
            flags = jnp.broadcast_to(listed_ref[pl.ds(block, 1), :], (BLOCK, BLOCK))
            at = (d * per_shard + j) * BLOCK
            free_ref[at : at + BLOCK, :] = 1.0 - jnp.transpose(flags)
            for r in range(picks):
                at = 2 * (j * picks + r)
                pick = rand[at : at + 1, :] * DIGIT + rand[at + 1 : at + 2, :]
                pick_ref[r, row, :] = pick.astype(jnp.int32)


def fill_bias(heads, groups, near, listed_ref, block_ref, pick_ref, bias_ref):
    per_shard = block_ref.shape[0] // heads
    blocks = block_ref[...]
    picks = [pick_ref[r] for r in range(pick_ref.shape[0])]
    for g, there in enumerate(groups):
        for d in range(heads):
            for b in range(per_shard):
                key_block = (there * heads + (near ^ d)) * per_shard + b
                away = key_block - blocks
                times = listed_ref[pl.ds(key_block, 1), :] + jnp.where((away >= -2) & (away <= 1), 1.0, 0.0)
                for pick in picks:
                    times = times + jnp.where(pick == key_block, 1.0, 0.0)
                at = ((g * heads + d) * per_shard + b) * BLOCK
                bias_ref[:, at : at + BLOCK] = jnp.where(
                    times > 0, jnp.log2(jnp.maximum(times, 1.0)), NEVER
                )


def attend_rows(near, tile, span, q_ref, free_ref, bias_ref, keys, peak, total):
    per_shard = span // BLOCK
    scale = HEAD_DIM ** (-0.5) * math.log2(math.e)
    mine = own_half(near)
    q = q_ref[tile * span : (tile + 1) * span, :]
    scores = [[] for _ in range(per_shard)]
    for key_ref, first, column in keys:
        s = lax.dot_general(
            q,
            key_ref[first : first + span, :],
            (((1,), (1,)), ((), ())),
            preferred_element_type=jnp.float32,
        )
        for j in range(per_shard):
            block = tile * per_shard + j
            free = free_ref[block * BLOCK : (block + 1) * BLOCK, :]
            for b in range(per_shard):
                bias = bias_ref[block : block + 1, column + b * BLOCK : column + (b + 1) * BLOCK]
                part = s[j * BLOCK : (j + 1) * BLOCK, b * BLOCK : (b + 1) * BLOCK]
                scores[j].append(part * scale + free * bias)
    peaks, weights = [], []
    for j in range(per_shard):
        best = jnp.max(functools.reduce(jnp.maximum, scores[j]), axis=1, keepdims=True)
        best = jnp.broadcast_to(best, (BLOCK, LANES))
        if peak is not None:
            best = jnp.maximum(peak[j * BLOCK : (j + 1) * BLOCK, :], best)
        peaks.append(best)
        weights.append([jnp.exp2(part - best).astype(jnp.bfloat16) for part in scores[j]])
    new = jnp.concatenate(peaks, axis=0)
    if total is not None:
        total = total * jnp.exp2(peak - new)
    for i, (key_ref, first, _) in enumerate(keys):
        e = jnp.concatenate(
            [
                jnp.concatenate(weights[j][i * per_shard : (i + 1) * per_shard], axis=1)
                for j in range(per_shard)
            ],
            axis=0,
        )
        v = jnp.where(mine, jnp.ones((), jnp.bfloat16), key_ref[first : first + span, :])
        term = jnp.dot(e, v, preferred_element_type=jnp.float32)
        total = term if total is None else total + term
    return new, total


def finish(heads, parts, near, span, sums, out_ref):
    mine = own_half(near)
    piece = span // parts
    for d in range(heads):
        for part in range(parts):
            first = d * span + part * piece
            top = sums[first : first + piece // 2, :]
            bottom = sums[first + piece // 2 : first + piece, :]
            values = jnp.where(mine, half_turn(top), bottom)
            totals = jnp.where(mine, top, half_turn(bottom))
            out_ref[(near ^ d) * parts + part] = (values / totals).astype(out_ref.dtype)


def open_kernel(heads, picks, near_ref, far_ref, listed_ref, *refs):
    messages, refs = refs[:heads], refs[heads:]
    peaks, sums, q_ref, free_ref, bias_ref, block_ref, pick_ref = refs
    span = q_ref.shape[0] // heads
    near, far = near_ref[0], far_ref[0]
    prepare(heads, picks, near, far, span, messages, listed_ref, q_ref, free_ref, block_ref, pick_ref)
    fill_bias(heads, [far, far ^ 1], near, listed_ref, block_ref, pick_ref, bias_ref)
    keys = [(messages[d], 0, d * span) for d in range(heads)]
    for tile in range(heads):
        rows = slice(tile * span, (tile + 1) * span)
        peaks[rows, :], sums[rows, :] = attend_rows(
            near, tile, span, q_ref, free_ref, bias_ref, keys, None, None
        )


def more_kernel(heads, columns, parts, near_ref, q_ref, free_ref, bias_ref, peak_in, sum_in, *refs):
    kv_refs, refs = refs[: len(columns)], refs[len(columns) :]
    if parts:
        out_ref, sums = refs
        peaks = None
    else:
        peaks, sums = refs
    span = q_ref.shape[0] // heads
    near = near_ref[0]
    keys = [(ref, 0, column) for ref, column in zip(kv_refs, columns)]
    for tile in range(heads):
        rows = slice(tile * span, (tile + 1) * span)
        new, sums[rows, :] = attend_rows(
            near, tile, span, q_ref, free_ref, bias_ref, keys, peak_in[rows, :], sum_in[rows, :]
        )
        if peaks is not None:
            peaks[rows, :] = new
    if parts:
        finish(heads, parts, near, span, sums, out_ref)


def whole_kernel(heads, picks, parts, near_ref, far_ref, listed_ref, kv_ref, *refs):
    messages, refs = refs[:heads], refs[heads:]
    out_ref, peaks, sums, q_ref, free_ref, bias_ref, block_ref, pick_ref = refs
    span = q_ref.shape[0] // heads
    near, far = near_ref[0], far_ref[0]
    step = pl.program_id(0)

    @pl.when(step == 0)
    def _():
        peaks[...] = jnp.full_like(peaks, NEVER)
        sums[...] = jnp.zeros_like(sums)
        prepare(heads, picks, near, far, span, messages, listed_ref, q_ref, free_ref, block_ref, pick_ref)

    fill_bias(heads, [step], near, listed_ref, block_ref, pick_ref, bias_ref)
    keys = [(kv_ref, d * span, d * span) for d in range(heads)]
    for tile in range(heads):
        rows = slice(tile * span, (tile + 1) * span)
        peaks[rows, :], sums[rows, :] = attend_rows(
            near, tile, span, q_ref, free_ref, bias_ref, keys, peaks[rows, :], sums[rows, :]
        )

    @pl.when(step == pl.num_programs(0) - 1)
    def _():
        finish(heads, parts, near, span, sums, out_ref)


def attend_cost(rows, keys):
    return pl.CostEstimate(
        flops=4 * rows * keys * LANES, bytes_accessed=4 * (rows + keys) * LANES, transcendentals=rows * keys
    )


def open_attend(near, far, picks, listed, messages, span):
    heads = len(messages)
    rows = heads * span
    blocks = rows // BLOCK
    state = jax.ShapeDtypeStruct((rows, LANES), jnp.float32)
    return pl.pallas_call(
        functools.partial(open_kernel, heads, picks),
        in_specs=[SMEM, SMEM] + [VMEM] * (1 + heads),
        out_specs=[VMEM] * 5,
        out_shape=[
            state,
            state,
            jax.ShapeDtypeStruct((rows, LANES), jnp.bfloat16),
            state,
            jax.ShapeDtypeStruct((blocks, 2 * rows), jnp.float32),
        ],
        scratch_shapes=[
            pltpu.VMEM((blocks, LANES), jnp.int32),
            pltpu.VMEM((picks, blocks, LANES), jnp.int32),
        ],
        compiler_params=pltpu.CompilerParams(vmem_limit_bytes=24 * MIB),
        cost_estimate=attend_cost(rows, rows),
    )(near, far, listed, *messages)


def piece_shape(heads, parts, span):
    return jax.ShapeDtypeStruct((heads * parts, span // parts // 2, LANES), jnp.bfloat16)


def more_attend(near, heads, queries, old, kvs, columns, parts):
    rows = queries[0].shape[0]
    span = rows // heads
    state = jax.ShapeDtypeStruct((rows, LANES), jnp.float32)
    if parts:
        out_shape, out_specs = piece_shape(heads, parts, span), VMEM
        scratch = [pltpu.VMEM(state.shape, state.dtype)]
    else:
        out_shape, out_specs, scratch = [state] * 2, [VMEM] * 2, []
    return pl.pallas_call(
        functools.partial(more_kernel, heads, columns, parts),
        in_specs=[SMEM] + [VMEM] * (5 + len(kvs)),
        out_specs=out_specs,
        out_shape=out_shape,
        scratch_shapes=scratch,
        compiler_params=pltpu.CompilerParams(vmem_limit_bytes=24 * MIB),
        cost_estimate=attend_cost(rows, span * len(kvs)),
    )(near, *queries, *old, *kvs)


def whole_attend(near, far, picks, listed, messages, kvs, span, parts):
    heads = len(messages)
    rows = heads * span
    blocks, steps = rows // BLOCK, kvs.shape[0] // rows
    return pl.pallas_call(
        functools.partial(whole_kernel, heads, picks, parts),
        grid=(steps,),
        in_specs=[SMEM, SMEM, VMEM, pl.BlockSpec((rows, LANES), lambda s: (s, 0))] + [VMEM] * heads,
        out_specs=VMEM,
        out_shape=piece_shape(heads, parts, span),
        scratch_shapes=[
            pltpu.VMEM((rows, LANES), jnp.float32),
            pltpu.VMEM((rows, LANES), jnp.float32),
            pltpu.VMEM((rows, LANES), jnp.bfloat16),
            pltpu.VMEM((rows, LANES), jnp.float32),
            pltpu.VMEM((blocks, rows), jnp.float32),
            pltpu.VMEM((blocks, LANES), jnp.int32),
            pltpu.VMEM((picks, blocks, LANES), jnp.int32),
        ],
        compiler_params=pltpu.CompilerParams(vmem_limit_bytes=24 * MIB),
        cost_estimate=attend_cost(rows, kvs.shape[0]),
    )(near, far, listed, kvs, *messages)


def mix_kernel(near_count, order, here_ref, got_ref, *refs):
    parts = len(order)
    low = low_half()
    depth = refs[0].shape[0]
    blocks = []
    for ref in refs[:-1]:
        blocks += [ref.at[first : first + depth, :] for first in range(0, ref.shape[0], depth)]
    total = None
    for i, d in enumerate(order):
        source = here_ref[0] ^ d
        columns = []
        for near in range(0, near_count, 2):
            even, odd = (got_ref[at * parts + source].astype(jnp.float32) for at in (near, near + 1))
            top = jnp.where(low, even, odd)
            bottom = half_turn(jnp.where(low, odd, even))
            columns.append(jnp.concatenate([top, bottom], axis=0).astype(jnp.bfloat16))
        rows = jnp.concatenate(columns, axis=1)
        term = jnp.dot(rows, blocks[i][...], preferred_element_type=jnp.float32)
        total = term if total is None else total + term
    refs[-1][...] = total.astype(refs[-1].dtype)


def mix(here, got, o_blocks, order):
    parts = len(order)
    return pl.pallas_call(
        functools.partial(mix_kernel, got.shape[0] // parts, order),
        out_shape=jax.ShapeDtypeStruct((2 * got.shape[1], o_blocks[0].shape[1]), jnp.bfloat16),
        in_specs=[SMEM] + [VMEM] * (1 + len(o_blocks)),
        out_specs=VMEM,
        compiler_params=pltpu.CompilerParams(vmem_limit_bytes=24 * MIB),
    )(here, got, *o_blocks)


def swapped(block, axis, distance):
    return lax.ppermute(block, axis, [(i, i ^ distance) for i in range(lax.axis_size(axis))])


def shards(tokens, q_weight, k_weight, v_weight, o_weight, rand_blocks, global_pos):
    tok_rows = tokens.shape[0]
    far_count, heads, parts = (lax.axis_size(axis) for axis in ("far", "near", "head"))
    near, far, here = (
        lax.axis_index(axis).astype(jnp.int32).reshape(1) for axis in ("near", "far", "head")
    )
    picks = rand_blocks.shape[1]

    blocks = far_count * heads * tok_rows // BLOCK
    *ready, listed = project(
        near, blocks, global_pos, rand_blocks, tokens, q_weight, k_weight, v_weight
    )
    leaving, sent = ready[:heads], ready[heads:]
    messages = [sent[0]] + [swapped(sent[d], "near", d) for d in range(1, heads)]

    if far_count == 2:
        apart = [swapped(leaving[d], ("far", "near"), heads + d) for d in range(heads)]
        peaks, sums, *queries = open_attend(near, far, picks, listed, messages, tok_rows)
        columns = [(heads + d) * tok_rows for d in range(heads)]
        more = functools.partial(more_attend, near, heads, queries)
        cut = heads // 2
        old = more([peaks, sums], apart[:cut], columns[:cut], 0)
        pieces = more(old, apart[cut:], columns[cut:], parts)
    else:
        kvs = lax.all_gather(pack(tok_rows, messages), "far", tiled=True)
        pieces = whole_attend(near, far, picks, listed, messages, kvs, tok_rows, parts)

    distance = parts // 2
    o_blocks = [o_weight, swapped(o_weight, "head", distance)]
    order = [0, distance]
    while distance > 1:
        distance //= 2
        o_blocks.append(swapped(gather(o_blocks, [pieces]), "head", distance))
        order = order + [d ^ distance for d in order]
    got = lax.all_to_all(pieces, ("near", "head"), 0, 0, tiled=True)
    return mix(here, got, o_blocks, order)


def solution(mesh):
    count, columns = mesh.devices.shape
    tm = ("far", "near")
    placed = (
        P(tm, None),
        P(None, "head"),
        P(None, "head"),
        P(None, "head"),
        P("head", None),
        P(tm, None),
        P(),
    )

    def run(tokens, q_weight, *rest):
        heads = q_weight.shape[1] // HEAD_DIM // columns
        split = Mesh(mesh.devices.reshape(count // heads, heads, columns), (*tm, "head"))
        body = jax.shard_map(
            shards, mesh=split, in_specs=placed, out_specs=P((*tm, "head"), None), check_vma=False
        )
        return body(tokens, q_weight, *rest)

    return run
```

```python
import functools
import math

import jax
import jax.numpy as jnp
from jax import lax
from jax.experimental import pallas as pl
from jax.experimental.pallas import tpu as pltpu
from jax.sharding import Mesh
from jax.sharding import PartitionSpec as P

HEAD_DIM = 64
BLOCK = 128
LANES = 128
DIGIT_BITS = 7
DIGIT = 1 << DIGIT_BITS
TILE_ROWS = 16
NEVER = -1e30
MIB = 1024 * 1024
VMEM = pl.BlockSpec(memory_space=pltpu.VMEM)
SMEM = pl.BlockSpec(memory_space=pltpu.SMEM)
HBM = pl.BlockSpec(memory_space=pltpu.HBM)
ANY = pl.BlockSpec(memory_space=pl.ANY)


def low_half():
    return lax.broadcasted_iota(jnp.int32, (1, LANES), 1) < HEAD_DIM


def half_turn(block):
    return pltpu.roll(block, HEAD_DIM, 1)


def own_half(near):
    return lax.broadcasted_iota(jnp.int32, (1, LANES), 1) // HEAD_DIM == (near & 1)


def project_kernel(cuts, near_ref, rand_hbm, pos_hbm, t_hbm, q_hbm, k_hbm, v_hbm, *refs):
    listed_ref, t_ref, q_ref, k_ref, v_ref, all_ref, rand_ref, pos_ref, sems, few_sems = refs[-10:]
    rows = t_ref.shape[0]
    heads = k_ref.shape[1] // HEAD_DIM
    far_refs, sent_refs = refs[:heads], refs[heads : 2 * heads]
    few = [
        pltpu.make_async_copy(pos_hbm, pos_ref, few_sems.at[0]),
        pltpu.make_async_copy(rand_hbm, rand_ref, few_sems.at[1]),
    ]
    for copy in few:
        copy.start()
    copies = []
    for i, (source, target) in enumerate(
        ((t_hbm, t_ref), (k_hbm, k_ref), (v_hbm, v_ref), (q_hbm, q_ref))
    ):
        part = source.shape[0] // cuts
        group = []
        for c in range(cuts):
            at = slice(c * part, (c + 1) * part)
            copy = pltpu.make_async_copy(source.at[at, :], target.at[at, :], sems.at[i, c])
            copy.start()
            group.append(copy)
        copies.append(group)

    for copy in few:
        copy.wait()
    spots = lax.broadcasted_iota(jnp.int32, listed_ref.shape, 0) * BLOCK
    spots = spots + lax.broadcasted_iota(jnp.int32, listed_ref.shape, 1)
    listed_ref[...] = lax.fori_loop(
        0,
        pos_ref.shape[0],
        lambda i, flags: jnp.where(spots == pos_ref[i], 1.0, flags),
        jnp.zeros(listed_ref.shape, jnp.float32),
        unroll=16,
    )

    def product(i, weight_ref):
        for copy in copies[i]:
            copy.wait()
        return jnp.dot(t_ref[...], weight_ref[...], preferred_element_type=jnp.float32)

    for copy in copies[0]:
        copy.wait()
    low = low_half()
    k = product(1, k_ref)
    v = product(2, v_ref)
    for pair in range(heads // 2):
        at = slice(pair * LANES, (pair + 1) * LANES)
        key, value = k[:, at], half_turn(v[:, at])
        all_ref[2 * pair, :rows, :] = jnp.where(low, key, value).astype(jnp.bfloat16)
        all_ref[2 * pair + 1, :rows, :] = jnp.where(low, value, key).astype(jnp.bfloat16)
    q = product(3, q_ref)
    for pair in range(heads // 2):
        at = slice(pair * LANES, (pair + 1) * LANES)
        top, bottom = q[: rows // 2, at], half_turn(q[rows // 2 :, at])
        all_ref[2 * pair, rows:, :] = jnp.where(low, top, bottom).astype(jnp.bfloat16)
        all_ref[2 * pair + 1, rows:, :] = jnp.where(low, bottom, top).astype(jnp.bfloat16)
    near = near_ref[0]
    digit_rows = sent_refs[0].shape[0] - rows - rows // 2
    row = lax.broadcasted_iota(jnp.int32, (digit_rows, LANES), 0)
    digits = jnp.zeros((digit_rows, LANES), jnp.float32)
    picks = rand_ref.shape[1]
    for j in range(rand_ref.shape[0]):
        for r in range(picks):
            at = 2 * (j * picks + r)
            value = rand_ref[j, r]
            digits = jnp.where(row == at, (value >> DIGIT_BITS).astype(jnp.float32), digits)
            digits = jnp.where(row == at + 1, (value & (DIGIT - 1)).astype(jnp.float32), digits)
    digits = digits.astype(jnp.bfloat16)
    for d in range(heads):
        far_refs[d][...] = all_ref[near ^ d, :rows, :]
        sent_refs[d][: rows + rows // 2, :] = all_ref[near ^ d]
        sent_refs[d][rows + rows // 2 :, :] = digits


def project(near, blocks, global_pos, rand_blocks, tokens, q_weight, k_weight, v_weight):
    rows, depth = tokens.shape
    feats = k_weight.shape[1]
    heads = feats // HEAD_DIM
    cuts = 2
    message = rows + rows // 2
    digit_rows = -(-2 * rand_blocks.size // TILE_ROWS) * TILE_ROWS
    pinned = [
        pltpu.with_memory_space_constraint(array, pltpu.HBM)
        for array in (rand_blocks, global_pos, tokens, q_weight, k_weight, v_weight)
    ]
    return pl.pallas_call(
        functools.partial(project_kernel, cuts),
        in_specs=[SMEM] + [HBM] * 6,
        out_specs=[VMEM] * (2 * heads + 1),
        out_shape=[jax.ShapeDtypeStruct((rows, LANES), jnp.bfloat16)] * heads
        + [jax.ShapeDtypeStruct((message + digit_rows, LANES), jnp.bfloat16)] * heads
        + [jax.ShapeDtypeStruct((blocks, LANES), jnp.float32)],
        scratch_shapes=[
            pltpu.VMEM((rows, depth), jnp.bfloat16),
            pltpu.VMEM((depth, feats), jnp.bfloat16),
            pltpu.VMEM((depth, feats), jnp.bfloat16),
            pltpu.VMEM((depth, feats), jnp.bfloat16),
            pltpu.VMEM((heads, message, LANES), jnp.bfloat16),
            pltpu.SMEM(rand_blocks.shape, jnp.int32),
            pltpu.SMEM(global_pos.shape, jnp.int32),
            pltpu.SemaphoreType.DMA((4, cuts)),
            pltpu.SemaphoreType.DMA((2,)),
        ],
        compiler_params=pltpu.CompilerParams(vmem_limit_bytes=24 * MIB),
        cost_estimate=pl.CostEstimate(
            flops=6 * rows * depth * feats, bytes_accessed=2 * depth * (rows + 3 * feats), transcendentals=0
        ),
    )(near, *pinned)


def pack_kernel(*refs):
    out_ref = refs[-1]
    rows = out_ref.shape[0] // (len(refs) - 1)
    for i, ref in enumerate(refs[:-1]):
        out_ref[i * rows : (i + 1) * rows, :] = ref[:rows, :]


def pack(rows, messages):
    return pl.pallas_call(
        pack_kernel,
        in_specs=[VMEM] * len(messages),
        out_specs=VMEM,
        out_shape=jax.ShapeDtypeStruct((rows * len(messages), LANES), jnp.bfloat16),
        compiler_params=pltpu.CompilerParams(vmem_limit_bytes=32 * MIB),
    )(*messages)


def gather_kernel(count, *refs):
    out_ref, sems = refs[-2:]
    first, copies = 0, []
    for i, ref in enumerate(refs[:count]):
        at = slice(first, first + ref.shape[0])
        copies.append(pltpu.make_async_copy(ref, out_ref.at[at, :], sems.at[i]))
        first += ref.shape[0]
    for copy in copies:
        copy.start()
    for copy in copies:
        copy.wait()


def gather(blocks, after):
    rows = sum(block.shape[0] for block in blocks)
    return pl.pallas_call(
        functools.partial(gather_kernel, len(blocks)),
        in_specs=[ANY] * (len(blocks) + len(after)),
        out_specs=VMEM,
        out_shape=jax.ShapeDtypeStruct((rows, blocks[0].shape[1]), blocks[0].dtype),
        scratch_shapes=[pltpu.SemaphoreType.DMA((len(blocks),))],
        compiler_params=pltpu.CompilerParams(vmem_limit_bytes=24 * MIB),
    )(*blocks, *after)


def prepare(heads, picks, near, far, span, messages, listed_ref, q_ref, free_ref, block_ref, pick_ref):
    per_shard = span // BLOCK
    mine = own_half(near)
    for d in range(heads):
        packed = messages[d][span : span + span // 2, :].astype(jnp.float32)
        top = jnp.where(mine, packed, 0.0)
        bottom = jnp.where(mine, half_turn(packed), 0.0)
        q_ref[d * span : d * span + span // 2, :] = top.astype(q_ref.dtype)
        q_ref[d * span + span // 2 : (d + 1) * span, :] = bottom.astype(q_ref.dtype)
        rand = messages[d][span + span // 2 :, :].astype(jnp.float32)
        for j in range(per_shard):
            row = slice(d * per_shard + j, d * per_shard + j + 1)
            block = (far * heads + (near ^ d)) * per_shard + j
            block_ref[row, :] = jnp.full((1, LANES), block, jnp.int32)
            flags = jnp.broadcast_to(listed_ref[pl.ds(block, 1), :], (BLOCK, BLOCK))
            at = (d * per_shard + j) * BLOCK
            free_ref[at : at + BLOCK, :] = 1.0 - jnp.transpose(flags)
            for r in range(picks):
                at = 2 * (j * picks + r)
                pick = rand[at : at + 1, :] * DIGIT + rand[at + 1 : at + 2, :]
                pick_ref[r, row, :] = pick.astype(jnp.int32)


def fill_bias(heads, groups, near, listed_ref, block_ref, pick_ref, bias_ref):
    per_shard = block_ref.shape[0] // heads
    blocks = block_ref[...]
    picks = [pick_ref[r] for r in range(pick_ref.shape[0])]
    for g, there in enumerate(groups):
        for d in range(heads):
            for b in range(per_shard):
                key_block = (there * heads + (near ^ d)) * per_shard + b
                away = key_block - blocks
                times = listed_ref[pl.ds(key_block, 1), :] + jnp.where((away >= -2) & (away <= 1), 1.0, 0.0)
                for pick in picks:
                    times = times + jnp.where(pick == key_block, 1.0, 0.0)
                at = ((g * heads + d) * per_shard + b) * BLOCK
                bias_ref[:, at : at + BLOCK] = jnp.where(
                    times > 0, jnp.log2(jnp.maximum(times, 1.0)), NEVER
                )


def attend_rows(near, tile, span, q_ref, free_ref, bias_ref, keys, peak, total):
    per_shard = span // BLOCK
    scale = HEAD_DIM ** (-0.5) * math.log2(math.e)
    mine = own_half(near)
    q = q_ref[tile * span : (tile + 1) * span, :]
    scores = [[] for _ in range(per_shard)]
    for key_ref, first, column in keys:
        s = lax.dot_general(
            q,
            key_ref[first : first + span, :],
            (((1,), (1,)), ((), ())),
            preferred_element_type=jnp.float32,
        )
        for j in range(per_shard):
            block = tile * per_shard + j
            free = free_ref[block * BLOCK : (block + 1) * BLOCK, :]
            for b in range(per_shard):
                bias = bias_ref[block : block + 1, column + b * BLOCK : column + (b + 1) * BLOCK]
                part = s[j * BLOCK : (j + 1) * BLOCK, b * BLOCK : (b + 1) * BLOCK]
                scores[j].append(part * scale + free * bias)
    peaks, weights = [], []
    for j in range(per_shard):
        best = jnp.max(functools.reduce(jnp.maximum, scores[j]), axis=1, keepdims=True)
        best = jnp.broadcast_to(best, (BLOCK, LANES))
        if peak is not None:
            best = jnp.maximum(peak[j * BLOCK : (j + 1) * BLOCK, :], best)
        peaks.append(best)
        weights.append([jnp.exp2(part - best).astype(jnp.bfloat16) for part in scores[j]])
    new = jnp.concatenate(peaks, axis=0)
    if total is not None:
        total = total * jnp.exp2(peak - new)
    for i, (key_ref, first, _) in enumerate(keys):
        e = jnp.concatenate(
            [
                jnp.concatenate(weights[j][i * per_shard : (i + 1) * per_shard], axis=1)
                for j in range(per_shard)
            ],
            axis=0,
        )
        v = jnp.where(mine, jnp.ones((), jnp.bfloat16), key_ref[first : first + span, :])
        term = jnp.dot(e, v, preferred_element_type=jnp.float32)
        total = term if total is None else total + term
    return new, total


def finish(heads, parts, near, span, sums, out_ref):
    mine = own_half(near)
    piece = span // parts
    for d in range(heads):
        for part in range(parts):
            first = d * span + part * piece
            top = sums[first : first + piece // 2, :]
            bottom = sums[first + piece // 2 : first + piece, :]
            values = jnp.where(mine, half_turn(top), bottom)
            totals = jnp.where(mine, top, half_turn(bottom))
            out_ref[(near ^ d) * parts + part] = (values / totals).astype(out_ref.dtype)


def open_kernel(heads, picks, near_ref, far_ref, listed_ref, *refs):
    messages, refs = refs[:heads], refs[heads:]
    peaks, sums, q_ref, free_ref, bias_ref, block_ref, pick_ref = refs
    span = q_ref.shape[0] // heads
    near, far = near_ref[0], far_ref[0]
    prepare(heads, picks, near, far, span, messages, listed_ref, q_ref, free_ref, block_ref, pick_ref)
    fill_bias(heads, [far, far ^ 1], near, listed_ref, block_ref, pick_ref, bias_ref)
    keys = [(messages[d], 0, d * span) for d in range(heads)]
    for tile in range(heads):
        rows = slice(tile * span, (tile + 1) * span)
        peaks[rows, :], sums[rows, :] = attend_rows(
            near, tile, span, q_ref, free_ref, bias_ref, keys, None, None
        )


def more_kernel(heads, columns, parts, near_ref, q_ref, free_ref, bias_ref, peak_in, sum_in, *refs):
    kv_refs, refs = refs[: len(columns)], refs[len(columns) :]
    if parts:
        out_ref, sums = refs
        peaks = None
    else:
        peaks, sums = refs
    span = q_ref.shape[0] // heads
    near = near_ref[0]
    keys = [(ref, 0, column) for ref, column in zip(kv_refs, columns)]
    for tile in range(heads):
        rows = slice(tile * span, (tile + 1) * span)
        new, sums[rows, :] = attend_rows(
            near, tile, span, q_ref, free_ref, bias_ref, keys, peak_in[rows, :], sum_in[rows, :]
        )
        if peaks is not None:
            peaks[rows, :] = new
    if parts:
        finish(heads, parts, near, span, sums, out_ref)


def whole_kernel(heads, picks, parts, near_ref, far_ref, listed_ref, kv_ref, *refs):
    messages, refs = refs[:heads], refs[heads:]
    out_ref, peaks, sums, q_ref, free_ref, bias_ref, block_ref, pick_ref = refs
    span = q_ref.shape[0] // heads
    near, far = near_ref[0], far_ref[0]
    step = pl.program_id(0)

    @pl.when(step == 0)
    def _():
        peaks[...] = jnp.full_like(peaks, NEVER)
        sums[...] = jnp.zeros_like(sums)
        prepare(heads, picks, near, far, span, messages, listed_ref, q_ref, free_ref, block_ref, pick_ref)

    fill_bias(heads, [step], near, listed_ref, block_ref, pick_ref, bias_ref)
    keys = [(kv_ref, d * span, d * span) for d in range(heads)]
    for tile in range(heads):
        rows = slice(tile * span, (tile + 1) * span)
        peaks[rows, :], sums[rows, :] = attend_rows(
            near, tile, span, q_ref, free_ref, bias_ref, keys, peaks[rows, :], sums[rows, :]
        )

    @pl.when(step == pl.num_programs(0) - 1)
    def _():
        finish(heads, parts, near, span, sums, out_ref)


def attend_cost(rows, keys):
    return pl.CostEstimate(
        flops=4 * rows * keys * LANES, bytes_accessed=4 * (rows + keys) * LANES, transcendentals=rows * keys
    )


def open_attend(near, far, picks, listed, messages, span):
    heads = len(messages)
    rows = heads * span
    blocks = rows // BLOCK
    state = jax.ShapeDtypeStruct((rows, LANES), jnp.float32)
    return pl.pallas_call(
        functools.partial(open_kernel, heads, picks),
        in_specs=[SMEM, SMEM] + [VMEM] * (1 + heads),
        out_specs=[VMEM] * 5,
        out_shape=[
            state,
            state,
            jax.ShapeDtypeStruct((rows, LANES), jnp.bfloat16),
            state,
            jax.ShapeDtypeStruct((blocks, 2 * rows), jnp.float32),
        ],
        scratch_shapes=[
            pltpu.VMEM((blocks, LANES), jnp.int32),
            pltpu.VMEM((picks, blocks, LANES), jnp.int32),
        ],
        compiler_params=pltpu.CompilerParams(vmem_limit_bytes=24 * MIB),
        cost_estimate=attend_cost(rows, rows),
    )(near, far, listed, *messages)


def piece_shape(heads, parts, span):
    return jax.ShapeDtypeStruct((heads * parts, span // parts // 2, LANES), jnp.bfloat16)


def more_attend(near, heads, queries, old, kvs, columns, parts):
    rows = queries[0].shape[0]
    span = rows // heads
    state = jax.ShapeDtypeStruct((rows, LANES), jnp.float32)
    if parts:
        out_shape, out_specs = piece_shape(heads, parts, span), VMEM
        scratch = [pltpu.VMEM(state.shape, state.dtype)]
    else:
        out_shape, out_specs, scratch = [state] * 2, [VMEM] * 2, []
    return pl.pallas_call(
        functools.partial(more_kernel, heads, columns, parts),
        in_specs=[SMEM] + [VMEM] * (5 + len(kvs)),
        out_specs=out_specs,
        out_shape=out_shape,
        scratch_shapes=scratch,
        compiler_params=pltpu.CompilerParams(vmem_limit_bytes=24 * MIB),
        cost_estimate=attend_cost(rows, span * len(kvs)),
    )(near, *queries, *old, *kvs)


def whole_attend(near, far, picks, listed, messages, kvs, span, parts):
    heads = len(messages)
    rows = heads * span
    blocks, steps = rows // BLOCK, kvs.shape[0] // rows
    return pl.pallas_call(
        functools.partial(whole_kernel, heads, picks, parts),
        grid=(steps,),
        in_specs=[SMEM, SMEM, VMEM, pl.BlockSpec((rows, LANES), lambda s: (s, 0))] + [VMEM] * heads,
        out_specs=VMEM,
        out_shape=piece_shape(heads, parts, span),
        scratch_shapes=[
            pltpu.VMEM((rows, LANES), jnp.float32),
            pltpu.VMEM((rows, LANES), jnp.float32),
            pltpu.VMEM((rows, LANES), jnp.bfloat16),
            pltpu.VMEM((rows, LANES), jnp.float32),
            pltpu.VMEM((blocks, rows), jnp.float32),
            pltpu.VMEM((blocks, LANES), jnp.int32),
            pltpu.VMEM((picks, blocks, LANES), jnp.int32),
        ],
        compiler_params=pltpu.CompilerParams(vmem_limit_bytes=24 * MIB),
        cost_estimate=attend_cost(rows, kvs.shape[0]),
    )(near, far, listed, kvs, *messages)


def mix_kernel(near_count, order, here_ref, got_ref, *refs):
    parts = len(order)
    low = low_half()
    depth = refs[0].shape[0]
    blocks = []
    for ref in refs[:-1]:
        blocks += [ref.at[first : first + depth, :] for first in range(0, ref.shape[0], depth)]
    total = None
    for i, d in enumerate(order):
        source = here_ref[0] ^ d
        columns = []
        for near in range(0, near_count, 2):
            even, odd = (got_ref[at * parts + source].astype(jnp.float32) for at in (near, near + 1))
            top = jnp.where(low, even, odd)
            bottom = half_turn(jnp.where(low, odd, even))
            columns.append(jnp.concatenate([top, bottom], axis=0).astype(jnp.bfloat16))
        rows = jnp.concatenate(columns, axis=1)
        term = jnp.dot(rows, blocks[i][...], preferred_element_type=jnp.float32)
        total = term if total is None else total + term
    refs[-1][...] = total.astype(refs[-1].dtype)


def mix(here, got, o_blocks, order):
    parts = len(order)
    return pl.pallas_call(
        functools.partial(mix_kernel, got.shape[0] // parts, order),
        out_shape=jax.ShapeDtypeStruct((2 * got.shape[1], o_blocks[0].shape[1]), jnp.bfloat16),
        in_specs=[SMEM] + [VMEM] * (1 + len(o_blocks)),
        out_specs=VMEM,
        compiler_params=pltpu.CompilerParams(vmem_limit_bytes=24 * MIB),
    )(here, got, *o_blocks)


def swapped(block, axis, distance):
    return lax.ppermute(block, axis, [(i, i ^ distance) for i in range(lax.axis_size(axis))])


def shards(tokens, q_weight, k_weight, v_weight, o_weight, rand_blocks, global_pos):
    tok_rows = tokens.shape[0]
    far_count, heads, parts = (lax.axis_size(axis) for axis in ("far", "near", "head"))
    near, far, here = (
        lax.axis_index(axis).astype(jnp.int32).reshape(1) for axis in ("near", "far", "head")
    )
    picks = rand_blocks.shape[1]

    blocks = far_count * heads * tok_rows // BLOCK
    *ready, listed = project(
        near, blocks, global_pos, rand_blocks, tokens, q_weight, k_weight, v_weight
    )
    leaving, sent = ready[:heads], ready[heads:]
    messages = [sent[0]] + [swapped(sent[d], "near", d) for d in range(1, heads)]

    if far_count == 2:
        apart = [swapped(leaving[d], ("far", "near"), heads + d) for d in range(heads)]
        peaks, sums, *queries = open_attend(near, far, picks, listed, messages, tok_rows)
        columns = [(heads + d) * tok_rows for d in range(heads)]
        more = functools.partial(more_attend, near, heads, queries)
        old = more([peaks, sums], apart[:1], columns[:1], 0)
        old = more(old, apart[1:-1], columns[1:-1], 0)
        pieces = more(old, apart[-1:], columns[-1:], parts)
    else:
        kvs = lax.all_gather(pack(tok_rows, messages), "far", tiled=True)
        pieces = whole_attend(near, far, picks, listed, messages, kvs, tok_rows, parts)

    distance = parts // 2
    o_blocks = [o_weight, swapped(o_weight, "head", distance)]
    order = [0, distance]
    while distance > 1:
        distance //= 2
        o_blocks.append(swapped(gather(o_blocks, [pieces]), "head", distance))
        order = order + [d ^ distance for d in order]
    got = lax.all_to_all(pieces, ("near", "head"), 0, 0, tiled=True)
    return mix(here, got, o_blocks, order)


def solution(mesh):
    count, columns = mesh.devices.shape
    tm = ("far", "near")
    placed = (
        P(tm, None),
        P(None, "head"),
        P(None, "head"),
        P(None, "head"),
        P("head", None),
        P(tm, None),
        P(),
    )

    def run(tokens, q_weight, *rest):
        heads = q_weight.shape[1] // HEAD_DIM // columns
        split = Mesh(mesh.devices.reshape(count // heads, heads, columns), (*tm, "head"))
        body = jax.shard_map(
            shards, mesh=split, in_specs=placed, out_specs=P((*tm, "head"), None), check_vma=False
        )
        return body(tokens, q_weight, *rest)

    return run
```
